32 devices in a mesh: groups: 2 (over x), ctx: 16 (over z, y, core).
Axes of the slice: x: 2, y: 2, z: 4, core: 2. Of those that a mesh axis runs over, the one named last changes fastest.
Arguments:
- queries: bfloat16 [4096, 2048], P(('groups', 'ctx')), parts along dimension 0, may hold values from -6 to 6
- keys: bfloat16 [4096, 256], P(('groups', 'ctx')), parts along dimension 0, may hold values from -6 to 6
- hidden: bfloat16 [4096, 2560], P(('groups', 'ctx')), parts along dimension 0, may hold values from -6 to 6
- value_weight: bfloat16 [2560, 256], replicated, may hold values from -0.125 to 0.125
- out_grad: bfloat16 [4096, 2048], P(('groups', 'ctx')), parts along dimension 0, may hold values from -6 to 6
- new_logp: float32 [4096], P(('groups', 'ctx')), parts along dimension 0, may hold values from -2 to -0.2
- old_logp: float32 [4096], P(('groups', 'ctx')), parts along dimension 0, may hold values from -2 to -0.2
- rewards: float32 [10], P('groups'), parts along dimension 0, may hold values from -4 to 4
- group_ids: int32 [10], P('groups'), parts along dimension 0, may hold values from 0 to 2
- seq_lengths: int32 [10], P('groups'), parts along dimension 0, may hold values from 1 to 1024, 2048 in all
Outputs:
- attn_out: bfloat16 [4096, 2048], P(('groups', 'ctx')), parts along dimension 0
- q_grad: bfloat16 [4096, 2048], P(('groups', 'ctx')), parts along dimension 0
- k_grad: bfloat16 [4096, 256], P(('groups', 'ctx')), parts along dimension 0
- x_grad: bfloat16 [4096, 2560], P(('groups', 'ctx')), parts along dimension 0
- wv_grad: float32 [5120, 256], P(('groups', 'ctx')), parts along dimension 0
The draws below stay inside these ranges and needn't reach their ends.
There are 2 independent parts, one for each index of `groups`. The reference program is written for one: setup_inputs(seed, part) draws one part's arguments, and reference() takes and returns one part's arrays. A program takes and returns all parts, laid end to end along the dimension named above; an argument that names none is the same for every part. Nothing has to cross between parts.
Inputs may be any that keep to these rules, and one draw needn't show every extreme that they name: `seq_lengths`: the 5 responses fill all 2048 positions of a replica in order; the longest has exactly 1024 tokens.
All inputs are finite; a program needn't handle non-finite values.
Results may differ from the reference program's by a relative error of at most 0.0087.
Values may be sent and summed in bfloat16 or wider, within the bound.
No kernel may reach another device: no remote copies, remote signals or barrier semaphores. Data moves between devices by JAX's collectives and lax.ppermute only.
A program may use at most 192 MiB of HBM per device.

```python
import math
import jax
import jax.numpy as jnp
import numpy as np
from jax import lax

D = 2560
HD = 64
KVH = 4
GQ = 8
QH = 32
TOK_DEV = 128
HOPS = 8
PROMPTS = 3
MAXLEN = 1024
TOKENS = 2048
NSEQ = 5
N_CTX = 16


def draw_queries(key, part):
    key = jax.random.fold_in(key, 11)
    base = jnp.clip(jax.random.normal(key, (TOKENS, KVH, GQ, HD), jnp.float32), -6.0, 6.0)
    return base.reshape(TOKENS, KVH * GQ * HD).astype(jnp.bfloat16)


def draw_keys(key, part):
    key = jax.random.fold_in(key, 23)
    base = jnp.clip(jax.random.normal(key, (TOKENS, KVH, HD), jnp.float32), -6.0, 6.0)
    return base.reshape(TOKENS, KVH * HD).astype(jnp.bfloat16)


def set_ends(entries, stream_key, least, largest):
    longest = entries.shape.index(max(entries.shape))
    spots = []
    for shift in (0, 1):
        where = [jax.random.randint(jax.random.fold_in(stream_key, axis), (), 0, length) for axis, length in enumerate(entries.shape)]
        where[longest] = (where[longest] + shift) % entries.shape[longest]
        spots.append(tuple(where))
    return entries.at[spots[0]].set(least).at[spots[1]].set(largest)


def strengthened(result, own_key, source, target, parts, factor):
    def block_of(position):
        return (jnp.arange(result.shape[position]) // (result.shape[position] // parts)).reshape((-1,) + (1,) * (result.ndim - 1 - position))

    first = jax.random.permutation(own_key, parts)[block_of(target)]
    second = (block_of(target) + parts // 2) % parts
    return jnp.where((block_of(source) == first) | (block_of(source) == second), factor * result, result)


def level_of(own_key, extent, cuts, low, high):
    def one(axis_at, blocks):
        heights = jax.random.uniform(jax.random.fold_in(jax.random.fold_in(own_key, 6), axis_at), (blocks,), jnp.float32, low / len(cuts), high / len(cuts))
        return jnp.repeat(jnp.exp(heights), extent[axis_at] // blocks).reshape((-1,) + (1,) * (len(extent) - axis_at - 1))

    gain = one(*cuts[0])
    for cut in cuts[1:]:
        gain = gain * one(*cut)
    return gain


def length_profile(number_of, total, reach, slope):
    loads = [(1 << 20) // math.isqrt(rank ** slope) + 1 for rank in range(2, number_of + 1)]
    rest, counts = total - reach - (number_of - 1), [1] * (number_of - 1)
    while rest > 0:
        free = [i for i in range(number_of - 1) if counts[i] < reach]
        pool, remaining = sum([loads[i] for i in free]), rest
        for i in free:
            extra = min(reach - counts[i], max(1, remaining * loads[i] // pool), rest)
            counts[i] = counts[i] + extra
            rest = rest - extra
    return np.array([reach] + counts)


def uneven_parts(key, number_of, total, reach, slope):
    if number_of == 2:
        one = jax.random.randint(key, (), max(1, total - reach), min(reach, total - 1) + 1)
        return jnp.stack([one, total - one])
    sizes = jnp.asarray(length_profile(number_of, total, reach, slope), jnp.int32)
    twos = (number_of - 1) // 2
    donor, receiver = sizes[1:1 + 2 * twos:2], sizes[2:2 + 2 * twos:2]
    room = jnp.minimum(donor - 1, reach - receiver)
    passed = jax.random.randint(jax.random.fold_in(key, 1), (twos,), 0, 1 << 20) % (room + 1)
    sizes = sizes.at[1:1 + 2 * twos:2].set(donor - passed).at[2:2 + 2 * twos:2].set(receiver + passed)
    return sizes[jax.random.permutation(jax.random.fold_in(key, 2), number_of)]


def gaussian(key, shape, spread, most, cuts=(), kind=jnp.bfloat16):
    level = level_of(key, shape, cuts, -0.22, 0.18) if cuts else 1.0
    values = jax.random.normal(key, shape, jnp.float32) * spread * level
    return jnp.minimum(jnp.maximum(values, -most), most).astype(kind)


def heavy_noise(own_key, shape, scale, limit, cuts, heavy, held_as=jnp.bfloat16):
    values = scale * jax.random.normal(own_key, shape, jnp.float32)
    if cuts:
        values = values * level_of(own_key, shape, cuts, -0.22, 0.18)
    return jnp.clip(strengthened(values, jax.random.fold_in(own_key, 3), *heavy), -limit, limit).astype(held_as)


def setup_inputs(seed: int = 0, part: int = 0) -> dict:
    key_of = jax.random.split(jax.random.key(seed), 11)
    own_keys = jax.random.split(jax.random.fold_in(key_of[10], part), 11)
    queries = draw_queries(jax.random.fold_in(jax.random.fold_in(key_of[10], part), 71), part)
    keys = draw_keys(jax.random.fold_in(jax.random.fold_in(key_of[10], part), 71), part)
    hidden = heavy_noise(own_keys[2], (TOKENS, D), 1.0, 6.0, ((0, 16),), (0, 1, 16, 2.0))
    value_weight = gaussian(key_of[3], (D, KVH * HD), D ** -0.5, 0.125)
    out_grad = gaussian(own_keys[4], (TOKENS, QH * HD), 1.0, 6.0, ((0, 16),))
    new_logp = jnp.clip(-2.0 + 1.8 * jax.random.uniform(own_keys[5], (TOKENS,), jnp.float32) ** level_of(own_keys[5], (TOKENS,), ((0, 16),), -0.2, 0.2), -2.0, -0.2)
    old_logp = jnp.clip(-2.0 + 1.8 * jax.random.uniform(own_keys[6], (TOKENS,), jnp.float32) ** level_of(own_keys[6], (TOKENS,), ((0, 16),), -0.2, 0.2), -2.0, -0.2)
    rewards = gaussian(own_keys[7], (NSEQ,), 1.0, 4.0, (), jnp.float32)
    group_ids = set_ends(jax.random.randint(own_keys[8], (NSEQ,), 0, PROMPTS), jax.random.fold_in(own_keys[8], 1), 0, PROMPTS - 1).astype(jnp.int32)
    seq_lengths = uneven_parts(own_keys[9], NSEQ, TOKENS, MAXLEN, 1).astype(jnp.int32)
    return {"queries": queries, "keys": keys, "hidden": hidden, "value_weight": value_weight, "out_grad": out_grad, "new_logp": new_logp, "old_logp": old_logp, "rewards": rewards, "group_ids": group_ids, "seq_lengths": seq_lengths}


big_negative = -1e+30

def rounded(values_in):
    return lax.optimization_barrier(values_in.astype(jnp.bfloat16)).astype(jnp.float32)

def token_layout(seq_lengths, rewards, group_ids, positions):
    seq_ends = jnp.cumsum(seq_lengths, dtype=jnp.int32)
    seq_starts = seq_ends - seq_lengths
    seq_of = lax.optimization_barrier(jnp.sum((positions[:, None] >= seq_ends[None, :]).astype(jnp.int32), axis=1, dtype=jnp.int32))
    membership = seq_of[:, None] == jnp.arange(seq_lengths.shape[0], dtype=jnp.int32)[None, :]
    tok_start = lax.optimization_barrier(jnp.sum(jnp.where(membership, seq_starts[None, :], 0), axis=1, dtype=jnp.int32))
    same_group = (group_ids[:, None] == group_ids[None, :]).astype(jnp.float32)
    group_mean = lax.optimization_barrier(jnp.sum(same_group * rewards[None, :], axis=1)) / lax.optimization_barrier(jnp.sum(same_group, axis=1))
    advantage = rewards - group_mean
    tok_adv = lax.optimization_barrier(jnp.sum(jnp.where(membership, advantage[None, :], jnp.zeros_like(advantage)[None, :]), axis=1))
    return (tok_start, tok_adv)

def reference(queries, keys, hidden, value_weight, out_grad, new_logp, old_logp, rewards, group_ids, seq_lengths):
    positions = jnp.arange(TOKENS, dtype=jnp.int32)
    tok_start, tok_adv = token_layout(seq_lengths, rewards, group_ids, positions)
    values = jnp.dot(hidden, value_weight, preferred_element_type=jnp.float32).astype(jnp.bfloat16)
    token_weight = -tok_adv * jnp.exp(new_logp - old_logp)
    kv_width = KVH * HD
    window_len = (HOPS + 1) * TOK_DEV
    front_pad = HOPS * TOK_DEV
    key_pad = jnp.concatenate([jnp.zeros((front_pad, kv_width), jnp.bfloat16), keys], axis=0)
    value_pad = jnp.concatenate([jnp.zeros((front_pad, kv_width), jnp.bfloat16), values], axis=0)
    score_scale = 1.0 / math.sqrt(HD)

    def one_block(carry, block):
        key_cots, value_cots = carry
        row_start = (block * TOK_DEV).astype(jnp.int32)
        query_rows = lax.dynamic_slice_in_dim(queries, row_start, TOK_DEV, 0).astype(jnp.float32).reshape(TOK_DEV, KVH, GQ, HD)
        key_rows = lax.dynamic_slice_in_dim(key_pad, row_start, window_len, 0).astype(jnp.float32).reshape(window_len, KVH, HD)
        value_rows = lax.dynamic_slice_in_dim(value_pad, row_start, window_len, 0).astype(jnp.float32).reshape(window_len, KVH, HD)
        query_pos = row_start + jnp.arange(TOK_DEV, dtype=jnp.int32)
        query_start = lax.dynamic_slice_in_dim(tok_start, row_start, TOK_DEV, 0)
        key_pos = row_start - front_pad + jnp.arange(window_len, dtype=jnp.int32)
        allowed = (key_pos[None, :] <= query_pos[:, None]) & (key_pos[None, :] >= query_start[:, None])
        scores = jnp.einsum('tgjd,sgd->gjts', query_rows, key_rows) * score_scale
        scores = jnp.where(allowed[None, None], scores, big_negative)
        row_max = lax.optimization_barrier(jnp.max(scores, axis=-1, keepdims=True))
        row_total = lax.optimization_barrier(jnp.sum(jnp.exp(scores - row_max), axis=-1, keepdims=True))
        probs = jnp.exp(scores - row_max - jnp.log(row_total))
        probs_b = rounded(probs)
        attn_rows = jnp.einsum('gjts,sgd->tgjd', probs_b, value_rows).astype(jnp.bfloat16).reshape(TOK_DEV, KVH * GQ * HD)
        weight_rows = lax.dynamic_slice_in_dim(token_weight, row_start, TOK_DEV, 0)
        grad_rows = lax.dynamic_slice_in_dim(out_grad, row_start, TOK_DEV, 0).astype(jnp.float32)
        out_cot = rounded(weight_rows[:, None] * grad_rows).reshape(TOK_DEV, KVH, GQ, HD)
        value_cot = jnp.einsum('gjts,tgjd->sgd', probs_b, out_cot).reshape(window_len, kv_width)
        prob_cot = jnp.einsum('tgjd,sgd->gjts', out_cot, value_rows)
        inner_sum = lax.optimization_barrier(jnp.sum(probs * prob_cot, axis=-1, keepdims=True))
        score_cot = rounded(probs * (prob_cot - inner_sum) * score_scale)
        query_cot = jnp.einsum('gjts,sgd->tgjd', score_cot, key_rows).astype(jnp.bfloat16).reshape(TOK_DEV, KVH * GQ * HD)
        key_cot = jnp.einsum('gjts,tgjd->sgd', score_cot, query_rows).reshape(window_len, kv_width)
        key_cots = lax.dynamic_update_slice_in_dim(key_cots, lax.dynamic_slice_in_dim(key_cots, row_start, window_len, 0) + key_cot, row_start, 0)
        value_cots = lax.dynamic_update_slice_in_dim(value_cots, lax.dynamic_slice_in_dim(value_cots, row_start, window_len, 0) + value_cot, row_start, 0)
        return ((key_cots, value_cots), (attn_rows, query_cot))
    start_cots = jnp.zeros((front_pad + TOKENS, kv_width), jnp.float32)
    carried, stacked = lax.scan(one_block, (start_cots, start_cots), jnp.arange(N_CTX, dtype=jnp.int32))
    key_cots, value_cots = carried
    attn_blocks, query_blocks = stacked
    attn_out = attn_blocks.reshape(TOKENS, KVH * GQ * HD)
    q_grad = query_blocks.reshape(TOKENS, KVH * GQ * HD)
    k_grad = key_cots[front_pad:].astype(jnp.bfloat16)
    value_cot_b = value_cots[front_pad:].astype(jnp.bfloat16)
    x_grad = jnp.dot(value_cot_b, value_weight.T, preferred_element_type=jnp.float32).astype(jnp.bfloat16)
    wv_grad = jnp.dot(hidden.T, value_cot_b, preferred_element_type=jnp.float32)
    return (attn_out, q_grad, k_grad, x_grad, wv_grad)
```

```python
import functools
import math

import jax
import jax.numpy as jnp
from jax import lax
from jax.experimental import pallas as pl
from jax.experimental.pallas import tpu as pltpu
from jax.sharding import PartitionSpec as P

HD = 64
PLANE = 4
BIG_NEGATIVE = -1e30
VMEM = pltpu.VMEM
SMEM = pltpu.SMEM


def dot(a, b, dims):
    return lax.dot_general(a, b, (dims, ((), ())), preferred_element_type=jnp.float32)


NN = ((1,), (0,))
NT = ((1,), (1,))
TN = ((0,), (0,))


def token_rows(pos, seq_ref, rew_ref, gid_ref):
    nseq = seq_ref.shape[0]
    start = jnp.zeros_like(pos)
    reward = jnp.zeros(pos.shape, jnp.float32)
    total = jnp.zeros(pos.shape, jnp.float32)
    count = jnp.ones(pos.shape, jnp.float32)
    begin = jnp.int32(0)
    for i in range(nseq):
        gsum = jnp.float32(0)
        gcount = jnp.float32(0)
        for j in range(nseq):
            same = gid_ref[j] == gid_ref[i]
            gsum = gsum + jnp.where(same, rew_ref[j], 0.0)
            gcount = gcount + jnp.where(same, 1.0, 0.0)
        here = pos >= begin
        start = jnp.where(here, begin, start)
        reward = jnp.where(here, rew_ref[i], reward)
        total = jnp.where(here, gsum, total)
        count = jnp.where(here, gcount, count)
        begin = begin + seq_ref[i]
    return start, reward - total / count


def attention_kernel(
    idx_ref, seq_ref, gid_ref, rew_ref,
    new_ref, old_ref, q_ref, og_ref, k_ref, v_ref,
    attn_ref, qg_ref, dk_ref, dv_ref,
    qpad, opad, dot_t, probs, fac, acc_k, acc_v, o_t, q_t, stat,
    *, kv_heads, group_size, back,
):
    tok = q_ref.shape[0]
    cols = group_size * tok
    idx = idx_ref[0]
    key_rows = 2 * tok
    lane = lax.broadcasted_iota(jnp.int32, (1, tok), 1)
    pos = idx * tok + lane
    start, advantage = token_rows(pos, seq_ref, rew_ref, gid_ref)
    weight = -advantage * jnp.exp(new_ref[...] - old_ref[...])
    weight_t = jnp.transpose(jnp.broadcast_to(weight, (tok, tok)))

    seq_first = jnp.int32(0)
    begin = jnp.int32(0)
    for i in range(seq_ref.shape[0]):
        seq_first = jnp.where(idx * tok >= begin, begin, seq_first)
        begin = begin + seq_ref[i]
    pair_hi = idx // 2
    pair_lo = seq_first // key_rows

    half = lax.broadcasted_iota(jnp.int32, (tok, 2 * HD), 1) // HD
    for g in range(kv_heads):
        for a in range(group_size // 2):
            at = (g * group_size + 2 * a) * HD
            q2 = q_ref[:, at:at + 2 * HD].astype(jnp.float32) * (1.0 / math.sqrt(HD))
            o2 = (og_ref[:, at:at + 2 * HD].astype(jnp.float32) * weight_t).astype(jnp.bfloat16).astype(jnp.float32)
            dot_t[g, :, a * tok:(a + 1) * tok] = jnp.transpose(o2)
            for side in range(2):
                qs, os_ = q2, o2
                if side != g % 2:
                    qs, os_ = pltpu.roll(q2, HD, 1), pltpu.roll(o2, HD, 1)
                keep = half == (g % 2)
                rows = slice((2 * a + side) * tok, (2 * a + side + 1) * tok)
                qpad[g, rows, :] = jnp.where(keep, qs, 0.0).astype(jnp.bfloat16)
                opad[g, rows, :] = jnp.where(keep, os_, 0.0).astype(jnp.bfloat16)

    acc_k[...] = jnp.zeros_like(acc_k)
    acc_v[...] = jnp.zeros_like(acc_v)

    qpos = jnp.concatenate([pos] * group_size, axis=1)
    qstart = jnp.concatenate([start] * group_size, axis=1)
    span = qpos - qstart

    def head(g, carry):
        lanes = pl.ds(pl.multiple_of((g // 2) * 2 * HD, 2 * HD), 2 * HD)
        side = g % 2
        stat[0:1, :] = jnp.full((1, cols), BIG_NEGATIVE, jnp.float32)
        stat[1:2, :] = jnp.zeros((1, cols), jnp.float32)
        o_t[...] = jnp.zeros_like(o_t)
        q_t[...] = jnp.zeros_like(q_t)

        def forward(step, carry):
            pair = pair_hi - step
            rows = pl.ds(pl.multiple_of(pair * key_rows, key_rows), key_rows)
            kk = k_ref[rows, lanes]
            vv = v_ref[rows, lanes]
            kpos = pair * key_rows + lax.broadcasted_iota(jnp.int32, (key_rows, 2 * tok), 0)
            for c in range(cols // (2 * tok)):
                at = slice(c * 2 * tok, (c + 1) * 2 * tok)
                s = dot(kk, qpad[g, at, :], NT)
                off = kpos - qstart[:, at]
                s = jnp.where((off >= 0) & (off <= span[:, at]), s, BIG_NEGATIVE)
                m_old = stat[0:1, at]
                m_new = jnp.maximum(m_old, jnp.max(s, axis=0, keepdims=True))
                e = jnp.exp(s - m_new)
                alpha = jnp.exp(m_old - m_new)
                stat[0:1, at] = m_new
                stat[1:2, at] = stat[1:2, at] * alpha + jnp.sum(e, axis=0, keepdims=True)
                fac[step, 0:1, at] = m_new
                eb = e.astype(jnp.bfloat16)
                probs[step, :, at] = eb
                o_t[:, at] = o_t[:, at] * alpha + dot(vv, eb, TN)
            return carry

        lax.fori_loop(0, pair_hi - pair_lo + 1, forward, 0)

        inv = 1.0 / stat[1:2, :]
        m_end = stat[0:1, :]
        own = pl.ds(pl.multiple_of(side * HD, HD), HD)
        out = o_t[own, :] * inv
        inner = []
        for j in range(group_size):
            d_t = dot_t[g, (j % 2) * HD:(j % 2 + 1) * HD, (j // 2) * tok:(j // 2 + 1) * tok]
            inner.append(jnp.sum(d_t * out[:, j * tok:(j + 1) * tok], axis=0, keepdims=True))
        inner = jnp.concatenate(inner, axis=1)
        for a in range(group_size // 2):
            both = jnp.concatenate(
                [out[:, 2 * a * tok:(2 * a + 1) * tok], out[:, (2 * a + 1) * tok:(2 * a + 2) * tok]], axis=0
            )
            to = pl.ds(pl.multiple_of(g * group_size * HD + a * 2 * HD, 2 * HD), 2 * HD)
            attn_ref[:, to] = jnp.transpose(both).astype(jnp.bfloat16)

        def backward(step, carry):
            pair = pair_hi - step
            rows = pl.ds(pl.multiple_of(pair * key_rows, key_rows), key_rows)
            kk = k_ref[rows, lanes]
            vv = v_ref[rows, lanes]
            dk = acc_k[rows, lanes]
            dv = acc_v[rows, lanes]
            for c in range(cols // (2 * tok)):
                at = slice(c * 2 * tok, (c + 1) * 2 * tok)
                scale = jnp.exp(fac[step, 0:1, at] - m_end[:, at]) * inv[:, at]
                p = probs[step, :, at].astype(jnp.float32) * scale
                dp = dot(vv, opad[g, at, :], NT)
                ds = (p * (dp - inner[:, at])).astype(jnp.bfloat16)
                dv = dv + dot(p.astype(jnp.bfloat16), opad[g, at, :], NN)
                dk = dk + dot(ds, qpad[g, at, :], NN)
                q_t[:, at] = q_t[:, at] + dot(kk, ds, TN)
            acc_k[rows, lanes] = dk
            acc_v[rows, lanes] = dv
            return carry

        lax.fori_loop(0, pair_hi - pair_lo + 1, backward, 0)

        qg = q_t[own, :] * (1.0 / math.sqrt(HD))
        for a in range(group_size // 2):
            both = jnp.concatenate(
                [qg[:, 2 * a * tok:(2 * a + 1) * tok], qg[:, (2 * a + 1) * tok:(2 * a + 2) * tok]], axis=0
            )
            to = pl.ds(pl.multiple_of(g * group_size * HD + a * 2 * HD, 2 * HD), 2 * HD)
            qg_ref[:, to] = jnp.transpose(both).astype(jnp.bfloat16)
        return carry

    lax.fori_loop(0, kv_heads, head, 0)

    plane = idx // PLANE
    place = idx % PLANE
    for r in range(PLANE):
        for w in range(back + 1):
            block = (plane - w) * PLANE + (place ^ r)
            held = block >= 0
            rows = pl.ds(pl.multiple_of(jnp.maximum(block, 0) * tok, tok), tok)
            dk_ref[r, w] = jnp.where(held, acc_k[rows, :], 0.0).astype(jnp.bfloat16)
            dv_ref[r, w] = jnp.where(held, acc_v[rows, :], 0.0).astype(jnp.bfloat16)


def attention(idx, seq, gid, rew, new_logp, old_logp, q, og, k_all, v_all, back):
    tok, width = q.shape
    rows, kv_width = k_all.shape
    kv_heads = kv_width // HD
    group_size = width // kv_width
    cols = group_size * tok
    pairs = back * PLANE // 2 + 1
    whole = lambda space: pl.BlockSpec(memory_space=space)
    flops = 12 * (pairs * 2 * tok) * width * tok
    return pl.pallas_call(
        functools.partial(attention_kernel, kv_heads=kv_heads, group_size=group_size, back=back),
        out_shape=(
            jax.ShapeDtypeStruct((tok, width), jnp.bfloat16),
            jax.ShapeDtypeStruct((tok, width), jnp.bfloat16),
            jax.ShapeDtypeStruct((PLANE, back + 1, tok, kv_width), jnp.bfloat16),
            jax.ShapeDtypeStruct((PLANE, back + 1, tok, kv_width), jnp.bfloat16),
        ),
        in_specs=[whole(SMEM)] * 4 + [whole(VMEM)] * 6,
        out_specs=[whole(VMEM)] * 4,
        scratch_shapes=[
            VMEM((kv_heads, cols, 2 * HD), jnp.bfloat16),
            VMEM((kv_heads, cols, 2 * HD), jnp.bfloat16),
            VMEM((kv_heads, 2 * HD, cols // 2), jnp.float32),
            VMEM((pairs, 2 * tok, cols), jnp.bfloat16),
            VMEM((pairs, 8, cols), jnp.float32),
            VMEM((rows, kv_width), jnp.float32),
            VMEM((rows, kv_width), jnp.float32),
            VMEM((2 * HD, cols), jnp.float32),
            VMEM((2 * HD, cols), jnp.float32),
            VMEM((8, cols), jnp.float32),
        ],
        compiler_params=pltpu.CompilerParams(vmem_limit_bytes=56 * 2**20),
        cost_estimate=pl.CostEstimate(flops=4 * flops, bytes_accessed=8 * 2**20, transcendentals=0),
        name="attention",
    )(idx, seq, gid, rew, new_logp, old_logp, q, og, k_all, v_all)


def shifted(x, by):
    n = lax.axis_size("ctx")
    return lax.ppermute(x, "ctx", [(i, i + by) for i in range(n) if 0 <= i + by < n])


def crossed(x, by):
    n = lax.axis_size("ctx")
    return lax.ppermute(x, "ctx", [(i, i ^ by) for i in range(n)])


def reduced(part, back):
    f32 = jnp.float32
    total = part[0].astype(f32)
    for r in range(1, PLANE):
        total = total + crossed(part[r], r).astype(f32)
    mine = total[0]
    for w in range(1, back + 1):
        mine = mine + shifted(total[w].astype(jnp.bfloat16), -w * PLANE).astype(f32)
    return mine.astype(jnp.bfloat16)


def shards(
    queries, keys, hidden, value_weight, out_grad, new_logp, old_logp, rewards, group_ids, seq_lengths
):
    n_ctx = lax.axis_size("ctx")
    back = n_ctx // 2 // PLANE
    idx = lax.axis_index("ctx").astype(jnp.int32).reshape(1)
    k_all = lax.all_gather(keys, "ctx", axis=0, tiled=True)
    values = jnp.dot(hidden, value_weight, preferred_element_type=jnp.float32).astype(jnp.bfloat16)
    v_all = lax.all_gather(values, "ctx", axis=0, tiled=True)
    hidden_cols = lax.all_to_all(hidden, "ctx", split_axis=1, concat_axis=0, tiled=True)
    attn_out, q_grad, dk, dv = attention(
        idx, seq_lengths, group_ids, rewards, new_logp[None, :], old_logp[None, :],
        queries, out_grad, k_all, v_all, back,
    )
    value_cot_b = reduced(dv, back)
    cot_all = lax.all_gather(value_cot_b, "ctx", axis=0, tiled=True)
    k_grad = reduced(dk, back)
    x_grad = jnp.einsum(
        "tf,df->td", value_cot_b, value_weight, preferred_element_type=jnp.float32
    ).astype(jnp.bfloat16)
    wv_grad = jnp.einsum("tc,tf->cf", hidden_cols, cot_all, preferred_element_type=jnp.float32)
    return (attn_out, q_grad, k_grad, x_grad, wv_grad)


def solution(mesh):
    rows = P(("groups", "ctx"), None)
    flat = P(("groups", "ctx"))
    placed = (rows, rows, rows, P(), rows, flat, flat, P("groups"), P("groups"), P("groups"))
    return jax.shard_map(
        shards, mesh=mesh, in_specs=placed, out_specs=(rows,) * 5, check_vma=False
    )
```

```python
import functools
import math

import jax
import jax.numpy as jnp
from jax import lax
from jax.experimental import pallas as pl
from jax.experimental.pallas import tpu as pltpu
from jax.sharding import PartitionSpec as P

HD = 64
PLANE = 4
SCALE = 1.0 / math.sqrt(HD)
BIG_NEGATIVE = -1e30
VMEM = pltpu.VMEM
SMEM = pltpu.SMEM
BF16 = jnp.bfloat16
F32 = jnp.float32


def dot(a, b):
    return lax.dot_general(a, b, (((1,), (0,)), ((), ())), preferred_element_type=F32)


def whole(space):
    return pl.BlockSpec(memory_space=space)


def token_weights(idx, tok, seq_ref, rew_ref, gid_ref, new_ref, old_ref):
    nseq = seq_ref.shape[0]
    pos = idx * tok + lax.broadcasted_iota(jnp.int32, (1, tok), 1)
    reward = jnp.zeros(pos.shape, F32)
    total = jnp.zeros(pos.shape, F32)
    count = jnp.ones(pos.shape, F32)
    begin = jnp.int32(0)
    for i in range(nseq):
        gsum = F32(0)
        gcount = F32(0)
        for j in range(nseq):
            same = gid_ref[j] == gid_ref[i]
            gsum = gsum + jnp.where(same, rew_ref[j], 0.0)
            gcount = gcount + jnp.where(same, 1.0, 0.0)
        here = pos >= begin
        reward = jnp.where(here, rew_ref[i], reward)
        total = jnp.where(here, gsum, total)
        count = jnp.where(here, gcount, count)
        begin = begin + seq_ref[i]
    return (total / count - reward) * jnp.exp(new_ref[...] - old_ref[...])


def values_kernel(hidden_ref, weight_ref, keys_ref, kv_ref):
    values = dot(hidden_ref[...], weight_ref[...]).astype(BF16)
    for g in range(PLANE):
        at = slice(g * HD, (g + 1) * HD)
        kv_ref[g] = jnp.concatenate([keys_ref[:, at], values[:, at]], axis=1)


def queries_kernel(
    idx_ref, seq_ref, gid_ref, rew_ref, new_ref, old_ref, q_ref, og_ref, qs_ref, oc_ref
):
    tok, width = q_ref.shape
    lanes = width // PLANE
    for g in range(PLANE):
        qs_ref[g] = (q_ref[:, g * lanes:(g + 1) * lanes].astype(F32) * SCALE).astype(BF16)
    weight = token_weights(idx_ref[0], tok, seq_ref, rew_ref, gid_ref, new_ref, old_ref)
    weight = jnp.transpose(jnp.broadcast_to(weight, (tok, tok)))[:, 0:1]
    for g in range(PLANE):
        oc_ref[g] = (og_ref[:, g * lanes:(g + 1) * lanes].astype(F32) * weight).astype(BF16)


def attention_kernel(idx_ref, seq_ref, q_ref, oc_ref, *rest, back, heads, per_pass):
    kv_refs = rest[:back + 1]
    attn_ref, qg_ref, own_ref, back_ref = rest[back + 1:back + 5]
    kv, kvt, qm, om, qt, ot, bias, score, probs, dscore, o_t, q_t, top, low, acc_k, acc_v = rest[back + 5:]
    rows_all = q_ref.shape[0]
    blk = rows_all // 2
    cols = per_pass * blk
    plane = idx_ref[0] // PLANE
    base = (plane - back) * 2

    for w in range(back + 1):
        for c in range(2):
            at = slice((back - w) * rows_all + c * blk, (back - w) * rows_all + (c + 1) * blk)
            part = kv_refs[w][c * blk:(c + 1) * blk, :]
            kv[at, :] = part
            kvt[:, at] = jnp.transpose(part.astype(F32)).astype(BF16)
    acc_k[...] = jnp.zeros_like(acc_k)
    acc_v[...] = jnp.zeros_like(acc_v)
    ot[...] = jnp.zeros_like(ot)
    half = lax.broadcasted_iota(jnp.int32, (blk, 2 * HD), 1) // HD

    def block(b, carry):
        pair_hi = plane * 2 + b
        first = pair_hi * blk
        pos = first + lax.broadcasted_iota(jnp.int32, (1, blk), 1)
        start = jnp.zeros_like(pos)
        start_lo = jnp.int32(0)
        start_hi = jnp.int32(0)
        begin = jnp.int32(0)
        for i in range(seq_ref.shape[0]):
            start = jnp.where(pos >= begin, begin, start)
            start_lo = jnp.where(first >= begin, begin, start_lo)
            start_hi = jnp.where(first + blk - 1 >= begin, begin, start_hi)
            begin = begin + seq_ref[i]
        pair_lo = start_lo // blk
        steps = pair_hi - pair_lo + 1
        q_rows = pl.ds(pl.multiple_of(b * blk, blk), blk)

        for h0 in range(0, heads, per_pass):
            for a in range(per_pass // 2):
                lanes = slice((h0 + 2 * a) * HD, (h0 + 2 * a + 2) * HD)
                q2 = q_ref[q_rows, lanes]
                q2t = jnp.transpose(q2.astype(F32)).astype(BF16)
                o2t = jnp.transpose(oc_ref[q_rows, lanes].astype(F32)).astype(BF16)
                for side in range(2):
                    at = slice((2 * a + side) * blk, (2 * a + side + 1) * blk)
                    qm[at, :] = jnp.where(half == side, q2, jnp.zeros_like(q2))
                    qt[:, at] = q2t[side * HD:(side + 1) * HD, :]
                    ot[HD:2 * HD, at] = o2t[side * HD:(side + 1) * HD, :]

            top[...] = jnp.full(top.shape, BIG_NEGATIVE, F32)
            low[...] = jnp.zeros_like(low)
            o_t[...] = jnp.zeros_like(o_t)
            q_t[...] = jnp.zeros_like(q_t)

            def scores(step, carry):
                pair = pair_hi - step
                rows = pl.ds(pl.multiple_of((pair - base) * blk, blk), blk)
                k_one = kv[rows, 0:HD]
                inside = (step > 0) & (pair * blk >= start_hi)

                def keep(j, s):
                    at = slice(j * blk, (j + 1) * blk)
                    score[step, :, at] = s
                    top[:, at] = jnp.maximum(top[:, at], jnp.max(s.reshape(blk // 8, 8, blk), axis=0))

                @pl.when(inside)
                def _():
                    for j in range(per_pass):
                        keep(j, dot(k_one, qt[:, j * blk:(j + 1) * blk]))

                @pl.when(jnp.logical_not(inside))
                def _():
                    key_pos = pair * blk + lax.broadcasted_iota(jnp.int32, (blk, blk), 0)
                    bias[...] = jnp.where((key_pos >= start) & (key_pos <= pos), 0.0, BIG_NEGATIVE)
                    for j in range(per_pass):
                        keep(j, dot(k_one, qt[:, j * blk:(j + 1) * blk]) + bias[...])

                return carry

            lax.fori_loop(0, steps, scores, 0)
            m = jnp.max(top[...], axis=0, keepdims=True)

            def outputs(step, carry):
                pair = pair_hi - step
                cols_k = pl.ds(pl.multiple_of((pair - base) * blk, blk), blk)
                v_t = kvt[HD:2 * HD, cols_k]
                for j in range(per_pass):
                    at = slice(j * blk, (j + 1) * blk)
                    e = jnp.exp(score[step, :, at] - m[:, at])
                    eb = e.astype(BF16)
                    probs[step, :, at] = eb
                    low[:, at] = low[:, at] + jnp.sum(e.reshape(blk // 8, 8, blk), axis=0)
                    o_t[:, at] = o_t[:, at] + dot(v_t, eb)
                return carry

            lax.fori_loop(0, steps, outputs, 0)
            inv = 1.0 / jnp.sum(low[...], axis=0, keepdims=True)
            out = o_t[...] * inv
            inner = inv * jnp.sum(ot[HD:2 * HD, :].astype(F32) * out, axis=0, keepdims=True)
            ot[HD:2 * HD, :] = (ot[HD:2 * HD, :].astype(F32) * inv).astype(BF16)
            for a in range(per_pass // 2):
                lanes = slice((h0 + 2 * a) * HD, (h0 + 2 * a + 2) * HD)
                o2 = oc_ref[q_rows, lanes].astype(F32)
                both = []
                for side in range(2):
                    at = slice((2 * a + side) * blk, (2 * a + side + 1) * blk)
                    both.append(out[:, at])
                    inv_t = jnp.transpose(jnp.broadcast_to(inv[:, at], (2 * HD, blk)))
                    om[at, :] = jnp.where(half == side, o2 * inv_t, 0.0).astype(BF16)
                attn_ref[q_rows, lanes] = jnp.transpose(jnp.concatenate(both, axis=0)).astype(BF16)

            def gradients(step, carry):
                pair = pair_hi - step
                rows = pl.ds(pl.multiple_of((pair - base) * blk, blk), blk)
                kv_one = kv[rows, :]
                k_t = kvt[0:HD, rows]
                for j in range(per_pass):
                    at = slice(j * blk, (j + 1) * blk)
                    dp = dot(kv_one, ot[:, at])
                    ds = (probs[step, :, at].astype(F32) * (dp - inner[:, at])).astype(BF16)
                    dscore[:, at] = ds
                    q_t[:, at] = q_t[:, at] + dot(k_t, ds)
                acc_v[rows, :] = acc_v[rows, :] + dot(probs[step], om[...])
                acc_k[rows, :] = acc_k[rows, :] + dot(dscore[...], qm[...])
                return carry

            lax.fori_loop(0, steps, gradients, 0)
            qg = q_t[...] * SCALE
            for a in range(per_pass // 2):
                lanes = slice((h0 + 2 * a) * HD, (h0 + 2 * a + 2) * HD)
                both = jnp.concatenate(
                    [qg[:, 2 * a * blk:(2 * a + 1) * blk], qg[:, (2 * a + 1) * blk:(2 * a + 2) * blk]], axis=0
                )
                qg_ref[q_rows, lanes] = jnp.transpose(both).astype(BF16)
        return carry

    lax.fori_loop(0, 2, block, 0)

    lower = lax.broadcasted_iota(jnp.int32, (rows_all, 2 * HD), 1) < HD
    for w in range(back + 1):
        at = slice((back - w) * rows_all, (back - w + 1) * rows_all)
        dk, dv = acc_k[at, :], acc_v[at, :]
        both = jnp.where(lower, dk + pltpu.roll(dk, HD, 1), dv + pltpu.roll(dv, HD, 1))
        if w == 0:
            own_ref[...] = both
        else:
            back_ref[w - 1] = both.astype(BF16)


def attention(idx, seq, q, oc, kvs):
    rows, width = q.shape
    back = len(kvs) - 1
    heads = width // HD
    keys = rows * (back + 1)
    blk = rows // 2
    pairs = 2 * back + 1
    per_pass = heads
    while per_pass > 2 and pairs * blk * per_pass * blk * 6 > 20 * 2**20:
        per_pass //= 2
    cols = per_pass * blk
    return pl.pallas_call(
        functools.partial(attention_kernel, back=back, heads=heads, per_pass=per_pass),
        out_shape=(
            jax.ShapeDtypeStruct((rows, width), BF16),
            jax.ShapeDtypeStruct((rows, width), BF16),
            jax.ShapeDtypeStruct((rows, 2 * HD), F32),
            jax.ShapeDtypeStruct((back, rows, 2 * HD), BF16),
        ),
        in_specs=[whole(SMEM)] * 2 + [whole(VMEM)] * (2 + len(kvs)),
        out_specs=[whole(VMEM)] * 4,
        scratch_shapes=[
            VMEM((keys, 2 * HD), BF16),
            VMEM((2 * HD, keys), BF16),
            VMEM((cols, 2 * HD), BF16),
            VMEM((cols, 2 * HD), BF16),
            VMEM((HD, cols), BF16),
            VMEM((2 * HD, cols), BF16),
            VMEM((blk, blk), F32),
            VMEM((pairs, blk, cols), F32),
            VMEM((pairs, blk, cols), BF16),
            VMEM((blk, cols), BF16),
            VMEM((HD, cols), F32),
            VMEM((HD, cols), F32),
            VMEM((8, cols), F32),
            VMEM((8, cols), F32),
            VMEM((keys, 2 * HD), F32),
            VMEM((keys, 2 * HD), F32),
        ],
        compiler_params=pltpu.CompilerParams(vmem_limit_bytes=56 * 2**20),
        cost_estimate=pl.CostEstimate(
            flops=40 * keys * rows * width, bytes_accessed=4 * 2**20, transcendentals=0
        ),
        name="attention",
    )(idx, seq, q, oc, *kvs)


def finish_kernel(parts_ref, weight_ref, kg_ref, xg_ref):
    vc = []
    kg = []
    for g in range(PLANE):
        kg.append(parts_ref[g, :, 0:HD])
        vc.append(parts_ref[g, :, HD:2 * HD])
    kg_ref[...] = jnp.concatenate(kg, axis=1)
    value_cot = jnp.concatenate(vc, axis=1)
    xg_ref[...] = lax.dot_general(
        value_cot, weight_ref[...], (((1,), (1,)), ((), ())), preferred_element_type=F32
    ).astype(BF16)


def shifted(x, by):
    n = lax.axis_size("ctx")
    return lax.ppermute(x, "ctx", [(i, i + by) for i in range(n) if 0 <= i + by < n])


def crossed(x, by):
    n = lax.axis_size("ctx")
    return lax.ppermute(x, "ctx", [(i, i ^ by) for i in range(n)])


def in_plane(x):
    n = lax.axis_size("ctx")
    planes = [list(range(i, i + PLANE)) for i in range(0, n, PLANE)]
    return lax.all_to_all(x, "ctx", 0, 0, axis_index_groups=planes, tiled=True)


def shards(
    queries, keys, hidden, value_weight, out_grad, new_logp, old_logp, rewards, group_ids, seq_lengths
):
    n_ctx = lax.axis_size("ctx")
    tok, width = queries.shape
    kv_width = keys.shape[1]
    features = hidden.shape[1]
    back = n_ctx // 2 // PLANE
    ctx = lax.axis_index("ctx").astype(jnp.int32)
    idx = ctx.reshape(1)
    lanes = width // PLANE
    plane_rows = PLANE * tok

    kv = pl.pallas_call(
        values_kernel,
        out_shape=jax.ShapeDtypeStruct((PLANE, tok, 2 * HD), BF16),
        in_specs=[whole(VMEM)] * 3,
        out_specs=whole(VMEM),
        name="values",
    )(hidden, value_weight, keys)
    qs, oc = pl.pallas_call(
        queries_kernel,
        out_shape=(jax.ShapeDtypeStruct((PLANE, tok, lanes), BF16),) * 2,
        in_specs=[whole(SMEM)] * 4 + [whole(VMEM)] * 4,
        out_specs=(whole(VMEM),) * 2,
        name="queries",
    )(idx, seq_lengths, group_ids, rewards, new_logp[None, :], old_logp[None, :], queries, out_grad)

    kv = in_plane(kv.reshape(plane_rows, 2 * HD))
    kvs = [kv] + [shifted(kv, w * PLANE) for w in range(1, back + 1)]
    q_plane = in_plane(qs.reshape(plane_rows, lanes))
    oc_plane = in_plane(oc.reshape(plane_rows, lanes))
    hidden_y = crossed(hidden, 2)
    hidden_c = crossed(hidden, 1)
    hidden_cy = crossed(hidden_y, 1)

    attn, qg, own, backs = attention(idx, seq_lengths, q_plane, oc_plane, kvs)

    total = own
    for w in range(1, back + 1):
        total = total + shifted(backs[w - 1], -w * PLANE).astype(F32)
    total = total.astype(BF16)
    attn = in_plane(attn).reshape(PLANE, tok, lanes).transpose(1, 0, 2).reshape(tok, width)
    qg = in_plane(qg).reshape(PLANE, tok, lanes).transpose(1, 0, 2).reshape(tok, width)
    parts = in_plane(total).reshape(PLANE, tok, 2 * HD)
    k_grad, x_grad = pl.pallas_call(
        finish_kernel,
        out_shape=(
            jax.ShapeDtypeStruct((tok, kv_width), BF16),
            jax.ShapeDtypeStruct((tok, features), BF16),
        ),
        in_specs=[whole(VMEM)] * 2,
        out_specs=(whole(VMEM),) * 2,
        name="finish",
    )(parts, value_weight)

    place = ctx % PLANE
    cot = total[:, HD:].reshape(PLANE, tok, HD)
    wv = jnp.zeros((features, HD), F32)
    for r, block in enumerate((hidden, hidden_c, hidden_y, hidden_cy)):
        one = lax.dynamic_index_in_dim(cot, place ^ r, 0, keepdims=False)
        wv = wv + jnp.einsum("tc,tf->cf", block, one, preferred_element_type=F32)
    rows = features // n_ctx
    wv = wv.astype(BF16).reshape(n_ctx, 2, rows // 2, HD).transpose(0, 2, 1, 3).reshape(n_ctx, rows // 2, 2 * HD)
    wv = lax.all_to_all(wv, "ctx", 0, 0, tiled=True)
    wv = wv.reshape(n_ctx // PLANE, PLANE, rows // 2, 2, HD).astype(F32).sum(axis=0)
    wv_grad = wv.transpose(2, 1, 0, 3).reshape(rows, kv_width)
    return (attn, qg, k_grad, x_grad, wv_grad)


def solution(mesh):
    rows = P(("groups", "ctx"), None)
    flat = P(("groups", "ctx"))
    placed = (rows, rows, rows, P(), rows, flat, flat, P("groups"), P("groups"), P("groups"))
    return jax.shard_map(
        shards, mesh=mesh, in_specs=placed, out_specs=(rows,) * 5, check_vma=False
    )
```

```python
import functools
import math

import jax
import jax.numpy as jnp
from jax import lax
from jax.experimental import pallas as pl
from jax.experimental.pallas import tpu as pltpu
from jax.sharding import PartitionSpec as P

HD = 64
PLANE = 4
SCALE = 1.0 / math.sqrt(HD)
BIG_NEGATIVE = -1e30
VMEM = pltpu.VMEM
SMEM = pltpu.SMEM
BF16 = jnp.bfloat16
F32 = jnp.float32


def dot(a, b):
    return lax.dot_general(a, b, (((1,), (0,)), ((), ())), preferred_element_type=F32)


def whole(space):
    return pl.BlockSpec(memory_space=space)


def token_weights(idx, tok, seq_ref, rew_ref, gid_ref, new_ref, old_ref):
    nseq = seq_ref.shape[0]
    pos = idx * tok + lax.broadcasted_iota(jnp.int32, (1, tok), 1)
    reward = jnp.zeros(pos.shape, F32)
    total = jnp.zeros(pos.shape, F32)
    count = jnp.ones(pos.shape, F32)
    begin = jnp.int32(0)
    for i in range(nseq):
        gsum = F32(0)
        gcount = F32(0)
        for j in range(nseq):
            same = gid_ref[j] == gid_ref[i]
            gsum = gsum + jnp.where(same, rew_ref[j], 0.0)
            gcount = gcount + jnp.where(same, 1.0, 0.0)
        here = pos >= begin
        reward = jnp.where(here, rew_ref[i], reward)
        total = jnp.where(here, gsum, total)
        count = jnp.where(here, gcount, count)
        begin = begin + seq_ref[i]
    return (total / count - reward) * jnp.exp(new_ref[...] - old_ref[...])


def values_kernel(idx_ref, hidden_ref, weight_ref, keys_ref, *rest):
    out_refs, parts = rest[:PLANE], rest[PLANE]
    place = idx_ref[0] % PLANE
    values = dot(hidden_ref[...], weight_ref[...]).astype(BF16)
    for g in range(PLANE):
        at = slice(g * HD, (g + 1) * HD)
        parts[g] = jnp.concatenate([keys_ref[:, at], values[:, at]], axis=1)
    for r in range(PLANE):
        out_refs[r][...] = parts[place ^ r]


def join_kernel(*refs):
    tok = refs[0].shape[0]
    for r in range(PLANE):
        refs[PLANE][r * tok:(r + 1) * tok, :] = refs[r][...]


def queries_kernel(
    idx_ref, seq_ref, gid_ref, rew_ref, new_ref, old_ref, q_ref, og_ref, *out_refs
):
    tok, width = q_ref.shape
    lanes = width // PLANE
    place = idx_ref[0] % PLANE
    weight = token_weights(idx_ref[0], tok, seq_ref, rew_ref, gid_ref, new_ref, old_ref)
    weight = jnp.transpose(jnp.broadcast_to(weight, (tok, tok)))[:, 0:1]
    for r in range(PLANE):
        at = pl.ds(pl.multiple_of((place ^ r) * lanes, lanes), lanes)
        out_refs[r][:, 0:lanes] = (q_ref[:, at].astype(F32) * SCALE).astype(BF16)
        out_refs[r][:, lanes:2 * lanes] = (og_ref[:, at].astype(F32) * weight).astype(BF16)


def attention_kernel(idx_ref, seq_ref, *rest, back, heads, per_pass):
    in_refs = rest[:PLANE]
    kv_refs = rest[PLANE:PLANE + back + 1]
    rest = rest[PLANE + back + 1:]
    out_refs = rest[:PLANE]
    own_ref = rest[PLANE]
    back_refs = rest[PLANE + 1:PLANE + 1 + back]
    (q_in, res, kv, kvt, qm, om, qt, ot, bias, score, probs, dscore, o_t, q_t, top, low, acc_k, acc_v) = rest[
        PLANE + 1 + back:]
    tok = in_refs[0].shape[0]
    rows_all = PLANE * tok
    blk = rows_all // 2
    width = heads * HD
    plane = idx_ref[0] // PLANE
    place = idx_ref[0] % PLANE
    base = (plane - back) * 2

    for r in range(PLANE):
        q_in[pl.ds(pl.multiple_of((place ^ r) * tok, tok), tok), :] = in_refs[r][...]

    for w in range(back + 1):
        for r in range(PLANE):
            at = pl.ds(pl.multiple_of((back - w) * rows_all + (place ^ r) * tok, tok), tok)
            part = kv_refs[w][r * tok:(r + 1) * tok, :]
            kv[at, :] = part
            kvt[:, at] = jnp.transpose(part.astype(F32)).astype(BF16)
    acc_k[...] = jnp.zeros_like(acc_k)
    acc_v[...] = jnp.zeros_like(acc_v)
    ot[...] = jnp.zeros_like(ot)
    half = lax.broadcasted_iota(jnp.int32, (blk, 2 * HD), 1) // HD

    def block(b, carry):
        pair_hi = plane * 2 + b
        first = pair_hi * blk
        pos = first + lax.broadcasted_iota(jnp.int32, (1, blk), 1)
        start = jnp.zeros_like(pos)
        start_lo = jnp.int32(0)
        start_hi = jnp.int32(0)
        begin = jnp.int32(0)
        for i in range(seq_ref.shape[0]):
            start = jnp.where(pos >= begin, begin, start)
            start_lo = jnp.where(first >= begin, begin, start_lo)
            start_hi = jnp.where(first + blk - 1 >= begin, begin, start_hi)
            begin = begin + seq_ref[i]
        pair_lo = start_lo // blk
        steps = pair_hi - pair_lo + 1
        q_rows = pl.ds(pl.multiple_of(b * blk, blk), blk)

        for h0 in range(0, heads, per_pass):
            for a in range(per_pass // 2):
                lanes = slice((h0 + 2 * a) * HD, (h0 + 2 * a + 2) * HD)
                q2 = q_in[q_rows, lanes]
                o2 = q_in[q_rows, slice(width + lanes.start, width + lanes.stop)]
                q2t = jnp.transpose(q2.astype(F32)).astype(BF16)
                o2t = jnp.transpose(o2.astype(F32)).astype(BF16)
                for side in range(2):
                    at = slice((2 * a + side) * blk, (2 * a + side + 1) * blk)
                    qm[at, :] = jnp.where(half == side, q2, jnp.zeros_like(q2))
                    qt[:, at] = q2t[side * HD:(side + 1) * HD, :]
                    ot[HD:2 * HD, at] = o2t[side * HD:(side + 1) * HD, :]

            top[...] = jnp.full(top.shape, BIG_NEGATIVE, F32)
            low[...] = jnp.zeros_like(low)
            o_t[...] = jnp.zeros_like(o_t)
            q_t[...] = jnp.zeros_like(q_t)

            def scores(step, carry):
                pair = pair_hi - step
                rows = pl.ds(pl.multiple_of((pair - base) * blk, blk), blk)
                k_one = kv[rows, 0:HD]
                inside = (step > 0) & (pair * blk >= start_hi)

                def keep(j, s):
                    at = slice(j * blk, (j + 1) * blk)
                    score[step, :, at] = s
                    top[:, at] = jnp.maximum(top[:, at], jnp.max(s.reshape(blk // 8, 8, blk), axis=0))

                @pl.when(inside)
                def _():
                    for j in range(per_pass):
                        keep(j, dot(k_one, qt[:, j * blk:(j + 1) * blk]))

                @pl.when(jnp.logical_not(inside))
                def _():
                    key_pos = pair * blk + lax.broadcasted_iota(jnp.int32, (blk, blk), 0)
                    bias[...] = jnp.where((key_pos >= start) & (key_pos <= pos), 0.0, BIG_NEGATIVE)
                    for j in range(per_pass):
                        keep(j, dot(k_one, qt[:, j * blk:(j + 1) * blk]) + bias[...])

                return carry

            lax.fori_loop(0, steps, scores, 0)
            m = jnp.max(top[...], axis=0, keepdims=True)

            def outputs(step, carry):
                pair = pair_hi - step
                cols_k = pl.ds(pl.multiple_of((pair - base) * blk, blk), blk)
                v_t = kvt[HD:2 * HD, cols_k]
                for j in range(per_pass):
                    at = slice(j * blk, (j + 1) * blk)
                    e = jnp.exp(score[step, :, at] - m[:, at])
                    eb = e.astype(BF16)
                    probs[step, :, at] = eb
                    low[:, at] = low[:, at] + jnp.sum(e.reshape(blk // 8, 8, blk), axis=0)
                    o_t[:, at] = o_t[:, at] + dot(v_t, eb)
                return carry

            lax.fori_loop(0, steps, outputs, 0)
            inv = 1.0 / jnp.sum(low[...], axis=0, keepdims=True)
            out = o_t[...] * inv
            inner = inv * jnp.sum(ot[HD:2 * HD, :].astype(F32) * out, axis=0, keepdims=True)
            ot[HD:2 * HD, :] = (ot[HD:2 * HD, :].astype(F32) * inv).astype(BF16)
            for a in range(per_pass // 2):
                lanes = slice((h0 + 2 * a) * HD, (h0 + 2 * a + 2) * HD)
                pair_at = [slice((2 * a + side) * blk, (2 * a + side + 1) * blk) for side in range(2)]
                o2 = jnp.transpose(jnp.concatenate([ot[HD:2 * HD, at].astype(F32) for at in pair_at], axis=0))
                for side in range(2):
                    om[pair_at[side], :] = jnp.where(half == side, o2, 0.0).astype(BF16)
                both = jnp.concatenate([out[:, at] for at in pair_at], axis=0)
                res[q_rows, lanes] = jnp.transpose(both).astype(BF16)

            def gradients(step, carry):
                pair = pair_hi - step
                rows = pl.ds(pl.multiple_of((pair - base) * blk, blk), blk)
                kv_one = kv[rows, :]
                k_t = kvt[0:HD, rows]
                for j in range(per_pass):
                    at = slice(j * blk, (j + 1) * blk)
                    dp = dot(kv_one, ot[:, at])
                    ds = (probs[step, :, at].astype(F32) * (dp - inner[:, at])).astype(BF16)
                    dscore[:, at] = ds
                    q_t[:, at] = q_t[:, at] + dot(k_t, ds)
                acc_v[rows, :] = acc_v[rows, :] + dot(probs[step], om[...])
                acc_k[rows, :] = acc_k[rows, :] + dot(dscore[...], qm[...])
                return carry

            lax.fori_loop(0, steps, gradients, 0)
            qg = q_t[...] * SCALE
            for a in range(per_pass // 2):
                lanes = slice((h0 + 2 * a) * HD, (h0 + 2 * a + 2) * HD)
                both = jnp.concatenate(
                    [qg[:, 2 * a * blk:(2 * a + 1) * blk], qg[:, (2 * a + 1) * blk:(2 * a + 2) * blk]], axis=0
                )
                res[q_rows, slice(width + lanes.start, width + lanes.stop)] = jnp.transpose(both).astype(BF16)
        return carry

    lax.fori_loop(0, 2, block, 0)

    lower = lax.broadcasted_iota(jnp.int32, (rows_all, 2 * HD), 1) < HD
    for w in range(back + 1):
        at = slice((back - w) * rows_all, (back - w + 1) * rows_all)
        dk, dv = acc_k[at, :], acc_v[at, :]
        both = jnp.where(lower, dk + pltpu.roll(dk, HD, 1), dv + pltpu.roll(dv, HD, 1))
        if w == 0:
            own_ref[...] = both
        else:
            back_refs[w - 1][...] = both.astype(BF16)
    for r in range(PLANE):
        out_refs[r][...] = res[pl.ds(pl.multiple_of((place ^ r) * tok, tok), tok), :]


def attention(idx, seq, q_oc, kvs):
    tok, width2 = q_oc[0].shape
    rows = PLANE * tok
    width = width2 // 2
    back = len(kvs) - 1
    heads = width // HD
    keys = rows * (back + 1)
    blk = rows // 2
    pairs = 2 * back + 1
    per_pass = heads
    while per_pass > 2 and pairs * blk * per_pass * blk * 6 > 20 * 2**20:
        per_pass //= 2
    cols = per_pass * blk
    held = pairs * blk * cols * 6 + 10 * rows * width2 + 16 * keys * 2 * HD + 64 * cols * 2 * HD
    return pl.pallas_call(
        functools.partial(attention_kernel, back=back, heads=heads, per_pass=per_pass),
        out_shape=(
            [jax.ShapeDtypeStruct((tok, width2), BF16)] * PLANE
            + [jax.ShapeDtypeStruct((rows, 2 * HD), F32)]
            + [jax.ShapeDtypeStruct((rows, 2 * HD), BF16)] * back
        ),
        in_specs=[whole(SMEM)] * 2 + [whole(VMEM)] * (PLANE + len(kvs)),
        out_specs=[whole(VMEM)] * (PLANE + 1 + back),
        scratch_shapes=[
            VMEM((rows, width2), BF16),
            VMEM((rows, width2), BF16),
            VMEM((keys, 2 * HD), BF16),
            VMEM((2 * HD, keys), BF16),
            VMEM((cols, 2 * HD), BF16),
            VMEM((cols, 2 * HD), BF16),
            VMEM((HD, cols), BF16),
            VMEM((2 * HD, cols), BF16),
            VMEM((blk, blk), F32),
            VMEM((pairs, blk, cols), F32),
            VMEM((pairs, blk, cols), BF16),
            VMEM((blk, cols), BF16),
            VMEM((HD, cols), F32),
            VMEM((HD, cols), F32),
            VMEM((8, cols), F32),
            VMEM((8, cols), F32),
            VMEM((keys, 2 * HD), F32),
            VMEM((keys, 2 * HD), F32),
        ],
        compiler_params=pltpu.CompilerParams(vmem_limit_bytes=min(56 * 2**20, held + 8 * 2**20)),
        cost_estimate=pl.CostEstimate(
            flops=40 * keys * rows * width, bytes_accessed=4 * 2**20, transcendentals=0
        ),
        name="attention",
    )(idx, seq, *q_oc, *kvs)


def collect_kernel(idx_ref, own_ref, *rest, back, n_ctx):
    got_refs = rest[:back]
    hidden_refs = rest[back:back + PLANE]
    part_refs = rest[back + PLANE:back + 2 * PLANE]
    wv_ref, total = rest[back + 2 * PLANE:]
    tok, features = hidden_refs[0].shape
    place = idx_ref[0] % PLANE
    summed = own_ref[...]
    for got in got_refs:
        summed = summed + got[...].astype(F32)
    total[...] = summed
    wv = jnp.zeros((HD, features), F32)
    for r in range(PLANE):
        part = total[pl.ds(pl.multiple_of((place ^ r) * tok, tok), tok), :]
        part_refs[r][...] = part.astype(BF16)
        cot_t = jnp.transpose(part)[HD:2 * HD, :].astype(BF16)
        wv = wv + dot(cot_t, hidden_refs[r][...])
    wv = jnp.transpose(wv)
    rows = features // n_ctx
    if wv_ref.shape[2] == 2 * HD:
        for d in range(n_ctx):
            one = wv[d * rows:(d + 1) * rows]
            wv_ref[d] = jnp.concatenate([one[:rows // 2], one[rows // 2:]], axis=1).astype(BF16)
    else:
        for d in range(n_ctx):
            wv_ref[d] = wv[d * rows:(d + 1) * rows].astype(BF16)


def finish_kernel(idx_ref, weight_ref, *rest):
    part_refs, out_refs = rest[:PLANE], rest[PLANE:2 * PLANE]
    kg_ref, xg_ref, attn_ref, qg_ref, parts = rest[2 * PLANE:]
    place = idx_ref[0] % PLANE
    lanes = out_refs[0].shape[1] // 2
    for r in range(PLANE):
        parts[place ^ r] = part_refs[r][...]
        at = pl.ds(pl.multiple_of((place ^ r) * lanes, lanes), lanes)
        attn_ref[:, at] = out_refs[r][:, 0:lanes]
        qg_ref[:, at] = out_refs[r][:, lanes:2 * lanes]
    kg_ref[...] = jnp.concatenate([parts[g, :, 0:HD] for g in range(PLANE)], axis=1)
    value_cot = jnp.concatenate([parts[g, :, HD:2 * HD] for g in range(PLANE)], axis=1)
    xg_ref[...] = lax.dot_general(
        value_cot, weight_ref[...], (((1,), (1,)), ((), ())), preferred_element_type=F32
    ).astype(BF16)


def wv_sum_kernel(wv_ref, out_ref):
    n_ctx, depth, lanes = wv_ref.shape
    sums = []
    for g in range(PLANE):
        total = wv_ref[g].astype(F32)
        for d in range(g + PLANE, n_ctx, PLANE):
            total = total + wv_ref[d].astype(F32)
        sums.append(total)
    for side in range(lanes // HD):
        out_ref[side * depth:(side + 1) * depth, :] = jnp.concatenate(
            [total[:, side * HD:(side + 1) * HD] for total in sums], axis=1
        )


def shifted(x, by):
    n = lax.axis_size("ctx")
    return lax.ppermute(x, "ctx", [(i, i + by) for i in range(n) if 0 <= i + by < n])


def crossed(x, by):
    n = lax.axis_size("ctx")
    return lax.ppermute(x, "ctx", [(i, i ^ by) for i in range(n)])


def in_plane(x):
    n = lax.axis_size("ctx")
    planes = [list(range(i, i + PLANE)) for i in range(0, n, PLANE)]
    return lax.all_to_all(x, "ctx", 0, 0, axis_index_groups=planes, tiled=True)


def shards(
    queries, keys, hidden, value_weight, out_grad, new_logp, old_logp, rewards, group_ids, seq_lengths
):
    n_ctx = lax.axis_size("ctx")
    tok, width = queries.shape
    kv_width = keys.shape[1]
    features = hidden.shape[1]
    back = n_ctx // 2 // PLANE
    ctx = lax.axis_index("ctx").astype(jnp.int32)
    idx = ctx.reshape(1)
    lanes = width // PLANE
    plane_rows = PLANE * tok

    kv = pl.pallas_call(
        values_kernel,
        out_shape=[jax.ShapeDtypeStruct((tok, 2 * HD), BF16)] * PLANE,
        in_specs=[whole(SMEM)] + [whole(VMEM)] * 3,
        out_specs=[whole(VMEM)] * PLANE,
        scratch_shapes=[VMEM((PLANE, tok, 2 * HD), BF16)],
        name="values",
    )(idx, hidden, value_weight, keys)
    kv = list(kv)
    queries, kv[0] = lax.optimization_barrier((queries, kv[0]))
    q_oc = pl.pallas_call(
        queries_kernel,
        out_shape=[jax.ShapeDtypeStruct((tok, 2 * lanes), BF16)] * PLANE,
        in_specs=[whole(SMEM)] * 4 + [whole(VMEM)] * 4,
        out_specs=[whole(VMEM)] * PLANE,
        name="queries",
    )(idx, seq_lengths, group_ids, rewards, new_logp[None, :], old_logp[None, :], queries, out_grad)

    kv = [kv[0]] + [crossed(kv[r], r) for r in range(1, PLANE)]
    kv = pl.pallas_call(
        join_kernel,
        out_shape=jax.ShapeDtypeStruct((plane_rows, 2 * HD), BF16),
        in_specs=[whole(VMEM)] * PLANE,
        out_specs=whole(VMEM),
        name="join",
    )(*kv)
    kv, q_oc = lax.optimization_barrier((kv, list(q_oc)))
    kvs = [kv] + [shifted(kv, w * PLANE) for w in range(1, back + 1)]
    q_oc = [q_oc[0]] + [crossed(q_oc[r], r) for r in range(1, PLANE)]
    hidden_c = crossed(hidden, 1)
    late_hidden, q_oc, kvs = lax.optimization_barrier((hidden, q_oc, kvs))
    hidden_y = crossed(late_hidden, 2)

    outs = attention(idx, seq_lengths, q_oc, kvs)
    hidden_y, outs = lax.optimization_barrier((hidden_y, list(outs)))
    hidden_cy = crossed(hidden_y, 1)
    res, own, backs = outs[:PLANE], outs[PLANE], outs[PLANE + 1:]

    got = [shifted(backs[w - 1], -w * PLANE) for w in range(1, back + 1)]
    res = [res[0]] + [crossed(res[r], r) for r in range(1, PLANE)]
    rows = features // n_ctx
    packed = (rows // 2) % 8 == 0
    piece = (rows // 2, 2 * HD) if packed else (rows, HD)
    outs = pl.pallas_call(
        functools.partial(collect_kernel, back=back, n_ctx=n_ctx),
        out_shape=[jax.ShapeDtypeStruct((tok, 2 * HD), BF16)] * PLANE
        + [jax.ShapeDtypeStruct((n_ctx,) + piece, BF16)],
        in_specs=[whole(SMEM)] + [whole(VMEM)] * (1 + back + PLANE),
        out_specs=[whole(VMEM)] * (PLANE + 1),
        scratch_shapes=[VMEM((plane_rows, 2 * HD), F32)],
        name="collect",
    )(idx, own, *got, hidden, hidden_c, hidden_y, hidden_cy)
    parts, wv = outs[:PLANE], outs[PLANE]
    parts = [parts[0]] + [crossed(parts[r], r) for r in range(1, PLANE)]
    wv = lax.all_to_all(wv, "ctx", 0, 0, tiled=True)
    k_grad, x_grad, attn, q_grad = pl.pallas_call(
        finish_kernel,
        out_shape=[
            jax.ShapeDtypeStruct((tok, kv_width), BF16),
            jax.ShapeDtypeStruct((tok, features), BF16),
            jax.ShapeDtypeStruct((tok, width), BF16),
            jax.ShapeDtypeStruct((tok, width), BF16),
        ],
        in_specs=[whole(SMEM)] + [whole(VMEM)] * (1 + 2 * PLANE),
        out_specs=[whole(VMEM)] * 4,
        scratch_shapes=[VMEM((PLANE, tok, 2 * HD), BF16)],
        name="finish",
    )(idx, value_weight, *parts, *res)

    wv_grad = pl.pallas_call(
        wv_sum_kernel,
        out_shape=jax.ShapeDtypeStruct((rows, kv_width), F32),
        in_specs=[whole(VMEM)],
        out_specs=whole(VMEM),
        name="wv_sum",
    )(wv)
    return (attn, q_grad, k_grad, x_grad, wv_grad)


def solution(mesh):
    rows = P(("groups", "ctx"), None)
    flat = P(("groups", "ctx"))
    placed = (rows, rows, rows, P(), rows, flat, flat, P("groups"), P("groups"), P("groups"))
    return jax.shard_map(
        shards, mesh=mesh, in_specs=placed, out_specs=(rows,) * 5, check_vma=False
    )
```

```python
import functools
import math

import jax
import jax.numpy as jnp
from jax import lax
from jax.experimental import pallas as pl
from jax.experimental.pallas import tpu as pltpu
from jax.sharding import PartitionSpec as P

HD = 64
PLANE = 4
SCALE = 1.0 / math.sqrt(HD)
BIG_NEGATIVE = -1e30
VMEM = pltpu.VMEM
SMEM = pltpu.SMEM
BF16 = jnp.bfloat16
F32 = jnp.float32


def dot(a, b):
    return lax.dot_general(a, b, (((1,), (0,)), ((), ())), preferred_element_type=F32)


def whole(space):
    return pl.BlockSpec(memory_space=space)


def token_weights(idx, tok, seq_ref, rew_ref, gid_ref, new_ref, old_ref):
    nseq = seq_ref.shape[0]
    pos = idx * tok + lax.broadcasted_iota(jnp.int32, (1, tok), 1)
    reward = jnp.zeros(pos.shape, F32)
    total = jnp.zeros(pos.shape, F32)
    count = jnp.ones(pos.shape, F32)
    begin = jnp.int32(0)
    for i in range(nseq):
        gsum = F32(0)
        gcount = F32(0)
        for j in range(nseq):
            same = gid_ref[j] == gid_ref[i]
            gsum = gsum + jnp.where(same, rew_ref[j], 0.0)
            gcount = gcount + jnp.where(same, 1.0, 0.0)
        here = pos >= begin
        reward = jnp.where(here, rew_ref[i], reward)
        total = jnp.where(here, gsum, total)
        count = jnp.where(here, gcount, count)
        begin = begin + seq_ref[i]
    return (total / count - reward) * jnp.exp(new_ref[...] - old_ref[...])


def values_kernel(idx_ref, hidden_ref, weight_ref, keys_ref, *rest):
    out_refs, parts = rest[:PLANE], rest[PLANE]
    place = idx_ref[0] % PLANE
    values = dot(hidden_ref[...], weight_ref[...]).astype(BF16)
    for g in range(PLANE):
        at = slice(g * HD, (g + 1) * HD)
        parts[g] = jnp.concatenate([keys_ref[:, at], values[:, at]], axis=1)
    for r in range(PLANE):
        out_refs[r][...] = parts[place ^ r]


def join_kernel(*refs):
    tok = refs[0].shape[0]
    for r in range(PLANE):
        refs[PLANE][r * tok:(r + 1) * tok, :] = refs[r][...]


def queries_kernel(
    idx_ref, seq_ref, gid_ref, rew_ref, new_ref, old_ref, q_ref, og_ref, *out_refs
):
    tok, width = q_ref.shape
    lanes = width // PLANE
    place = idx_ref[0] % PLANE
    weight = token_weights(idx_ref[0], tok, seq_ref, rew_ref, gid_ref, new_ref, old_ref)
    weight = jnp.transpose(jnp.broadcast_to(weight, (tok, tok)))[:, 0:1]
    for r in range(PLANE):
        at = pl.ds(pl.multiple_of((place ^ r) * lanes, lanes), lanes)
        out_refs[r][:, 0:lanes] = (q_ref[:, at].astype(F32) * SCALE).astype(BF16)
        out_refs[r][:, lanes:2 * lanes] = (og_ref[:, at].astype(F32) * weight).astype(BF16)


def attention_kernel(idx_ref, seq_ref, *rest, back, heads, per_pass):
    in_refs = rest[:PLANE]
    kv_refs = rest[PLANE:PLANE + back + 1]
    rest = rest[PLANE + back + 1:]
    out_refs = rest[:PLANE]
    own_ref = rest[PLANE]
    back_refs = rest[PLANE + 1:PLANE + 1 + back]
    (q_in, res, k2, v2, k2t, v2t, qm, om, qt, ot, start, bias, score, probs, dscore, o_acc, q_acc, top, low, inner,
     acc_k, acc_v) = rest[PLANE + 1 + back:]
    tok = in_refs[0].shape[0]
    rows_all = PLANE * tok
    blk = rows_all // 2
    width = heads * HD
    plane = idx_ref[0] // PLANE
    place = idx_ref[0] % PLANE
    base = (plane - back) * 2

    for r in range(PLANE):
        q_in[pl.ds(pl.multiple_of((place ^ r) * tok, tok), tok), :] = in_refs[r][...]
    lower = lax.broadcasted_iota(jnp.int32, (tok, 2 * HD), 1) < HD
    for w in range(back + 1):
        for r in range(PLANE):
            at = pl.ds(pl.multiple_of((back - w) * rows_all + (place ^ r) * tok, tok), tok)
            part = kv_refs[w][r * tok:(r + 1) * tok, :].astype(F32)
            swapped = pltpu.roll(part, HD, 1)
            k2[at, :] = jnp.where(lower, part, swapped).astype(BF16)
            v2[at, :] = jnp.where(lower, swapped, part).astype(BF16)
            part_t = jnp.transpose(part).astype(BF16)
            k2t[:, at] = jnp.concatenate([part_t[:HD], part_t[:HD]], axis=0)
            v2t[:, at] = jnp.concatenate([part_t[HD:], part_t[HD:]], axis=0)
    acc_k[...] = jnp.zeros_like(acc_k)
    acc_v[...] = jnp.zeros_like(acc_v)
    left = lax.broadcasted_iota(jnp.int32, (blk, 2 * HD), 1) < HD
    pairs_at = [
        (slice(2 * a * blk, (2 * a + 1) * blk), slice((2 * a + 1) * blk, (2 * a + 2) * blk))
        for a in range(per_pass // 2)
    ]

    def twice(x):
        return jnp.concatenate([x, x], axis=1)

    def block(b, carry):
        pair_hi = plane * 2 + b
        first = pair_hi * blk
        pos = first + lax.broadcasted_iota(jnp.int32, (blk, 2 * HD), 0)
        starts = jnp.zeros_like(pos)
        start_lo = jnp.int32(0)
        start_hi = jnp.int32(0)
        begin = jnp.int32(0)
        for i in range(seq_ref.shape[0]):
            starts = jnp.where(pos >= begin, begin, starts)
            start_lo = jnp.where(first >= begin, begin, start_lo)
            start_hi = jnp.where(first + blk - 1 >= begin, begin, start_hi)
            begin = begin + seq_ref[i]
        start[...] = starts
        steps = pair_hi - start_lo // blk + 1
        q_rows = pl.ds(pl.multiple_of(b * blk, blk), blk)

        for h0 in range(0, heads, per_pass):
            def lanes_of(a, side=0):
                return slice(side * width + (h0 + 2 * a) * HD, side * width + (h0 + 2 * a + 2) * HD)

            for a, (even, odd) in enumerate(pairs_at):
                q2 = q_in[q_rows, lanes_of(a)]
                qm[even, :] = jnp.where(left, q2, jnp.zeros_like(q2))
                qm[odd, :] = jnp.where(left, jnp.zeros_like(q2), q2)
                q2t = jnp.transpose(q2.astype(F32)).astype(BF16)
                qt[:, even] = q2t[:HD]
                qt[:, odd] = q2t[HD:]

            top[...] = jnp.full(top.shape, BIG_NEGATIVE, F32)
            low[...] = jnp.zeros_like(low)
            o_acc[...] = jnp.zeros_like(o_acc)
            q_acc[...] = jnp.zeros_like(q_acc)

            def scores(step, carry):
                pair = pair_hi - step
                cols_k = pl.ds(pl.multiple_of((pair - base) * blk, blk), blk)
                inside = (step > 0) & (pair * blk >= start_hi)

                def keep(at, s):
                    score[step, at, :] = s
                    top[at, :] = jnp.maximum(top[at, :], jnp.maximum(s[:, :2 * HD], s[:, 2 * HD:]))

                @pl.when(inside)
                def _():
                    k_t = k2t[:, cols_k]
                    for even, odd in pairs_at:
                        at = slice(even.start, odd.stop)
                        keep(at, dot(qm[at, :], k_t))

                @pl.when(jnp.logical_not(inside))
                def _():
                    k_t = k2t[:, cols_k]
                    key_pos = pair * blk + lax.broadcasted_iota(jnp.int32, (blk, blk), 1)
                    tok_pos = first + lax.broadcasted_iota(jnp.int32, (blk, blk), 0)
                    seen = (key_pos >= twice(start[...])) & (key_pos <= tok_pos)
                    bias[...] = jnp.where(seen, 0.0, BIG_NEGATIVE)
                    for even, odd in pairs_at:
                        s = dot(qm[even.start:odd.stop, :], k_t)
                        keep(even, s[:blk] + bias[...])
                        keep(odd, s[blk:] + bias[...])

                return carry

            lax.fori_loop(0, steps, scores, 0)
            top[...] = jnp.broadcast_to(jnp.max(top[...], axis=1, keepdims=True), top.shape)

            def outputs(step, carry):
                pair = pair_hi - step
                rows = pl.ds(pl.multiple_of((pair - base) * blk, blk), blk)
                vv = v2[rows, :]
                for even, odd in pairs_at:
                    at = slice(even.start, odd.stop)
                    e = jnp.exp(score[step, at, :] - twice(top[at, :]))
                    eb = e.astype(BF16)
                    probs[step, at, :] = eb
                    low[at, :] = low[at, :] + (e[:, :2 * HD] + e[:, 2 * HD:])
                    o_acc[at, :] = o_acc[at, :] + dot(eb, vv)
                return carry

            lax.fori_loop(0, steps, outputs, 0)
            for a, pair_at in enumerate(pairs_at):
                o2 = q_in[q_rows, lanes_of(a, 1)].astype(F32)
                out = []
                scaled = []
                for side, at in enumerate(pair_at):
                    inv = 1.0 / jnp.sum(low[at, :], axis=1, keepdims=True)
                    out.append(o_acc[at, :] * inv)
                    mine = jnp.where(left if side == 0 else jnp.logical_not(left), o2, 0.0)
                    inner[at, :] = jnp.broadcast_to(
                        jnp.sum(mine * out[side], axis=1, keepdims=True) * inv, (blk, 2 * HD)
                    )
                    scaled.append(mine * inv)
                    om[at, :] = scaled[side].astype(BF16)
                res[q_rows, lanes_of(a)] = jnp.where(left, out[0], out[1]).astype(BF16)
                o2t = jnp.transpose(scaled[0] + scaled[1]).astype(BF16)
                ot[:, pair_at[0]] = o2t[:HD]
                ot[:, pair_at[1]] = o2t[HD:]

            def gradients(step, carry):
                pair = pair_hi - step
                rows = pl.ds(pl.multiple_of((pair - base) * blk, blk), blk)
                kk = k2[rows, :]
                v_t = v2t[:, rows]
                for even, odd in pairs_at:
                    at = slice(even.start, odd.stop)
                    dp = dot(om[at, :], v_t)
                    ds = (probs[step, at, :].astype(F32) * (dp - twice(inner[at, :]))).astype(BF16)
                    dscore[at, :] = ds
                    q_acc[at, :] = q_acc[at, :] + dot(ds, kk)
                acc_v[:, rows] = acc_v[:, rows] + dot(ot[...], probs[step])
                acc_k[:, rows] = acc_k[:, rows] + dot(qt[...], dscore[...])
                return carry

            lax.fori_loop(0, steps, gradients, 0)
            for a, (even, odd) in enumerate(pairs_at):
                qg = jnp.where(left, q_acc[even, :], q_acc[odd, :]) * SCALE
                res[q_rows, lanes_of(a, 1)] = qg.astype(BF16)
        return carry

    lax.fori_loop(0, 2, block, 0)

    for w in range(back + 1):
        at = slice((back - w) * rows_all, (back - w + 1) * rows_all)
        both = jnp.transpose(jnp.concatenate([acc_k[:, at], acc_v[:, at]], axis=0))
        if w == 0:
            own_ref[...] = both
        else:
            back_refs[w - 1][...] = both.astype(BF16)
    for r in range(PLANE):
        out_refs[r][...] = res[pl.ds(pl.multiple_of((place ^ r) * tok, tok), tok), :]


def attention(idx, seq, q_oc, kvs):
    tok, width2 = q_oc[0].shape
    rows = PLANE * tok
    width = width2 // 2
    back = len(kvs) - 1
    heads = width // HD
    keys = rows * (back + 1)
    blk = rows // 2
    pairs = 2 * back + 1
    per_pass = heads
    while per_pass > 2 and pairs * blk * per_pass * blk * 6 > 20 * 2**20:
        per_pass //= 2
    cols = per_pass * blk
    held = pairs * blk * cols * 6 + 10 * rows * width2 + 16 * keys * 2 * HD + 64 * cols * 2 * HD
    return pl.pallas_call(
        functools.partial(attention_kernel, back=back, heads=heads, per_pass=per_pass),
        out_shape=(
            [jax.ShapeDtypeStruct((tok, width2), BF16)] * PLANE
            + [jax.ShapeDtypeStruct((rows, 2 * HD), F32)]
            + [jax.ShapeDtypeStruct((rows, 2 * HD), BF16)] * back
        ),
        in_specs=[whole(SMEM)] * 2 + [whole(VMEM)] * (PLANE + len(kvs)),
        out_specs=[whole(VMEM)] * (PLANE + 1 + back),
        scratch_shapes=[
            VMEM((rows, width2), BF16),
            VMEM((rows, width2), BF16),
            VMEM((keys, 2 * HD), BF16),
            VMEM((keys, 2 * HD), BF16),
            VMEM((2 * HD, keys), BF16),
            VMEM((2 * HD, keys), BF16),
            VMEM((cols, 2 * HD), BF16),
            VMEM((cols, 2 * HD), BF16),
            VMEM((HD, cols), BF16),
            VMEM((HD, cols), BF16),
            VMEM((blk, 2 * HD), jnp.int32),
            VMEM((blk, blk), F32),
            VMEM((pairs, cols, blk), F32),
            VMEM((pairs, cols, blk), BF16),
            VMEM((cols, blk), BF16),
            VMEM((cols, 2 * HD), F32),
            VMEM((cols, 2 * HD), F32),
            VMEM((cols, 2 * HD), F32),
            VMEM((cols, 2 * HD), F32),
            VMEM((cols, 2 * HD), F32),
            VMEM((HD, keys), F32),
            VMEM((HD, keys), F32),
        ],
        compiler_params=pltpu.CompilerParams(vmem_limit_bytes=min(56 * 2**20, held + 8 * 2**20)),
        cost_estimate=pl.CostEstimate(
            flops=40 * keys * rows * width, bytes_accessed=4 * 2**20, transcendentals=0
        ),
        name="attention",
    )(idx, seq, *q_oc, *kvs)


def collect_kernel(idx_ref, own_ref, *rest, back, n_ctx):
    got_refs = rest[:back]
    hidden_refs = rest[back:back + PLANE]
    part_refs = rest[back + PLANE:back + 2 * PLANE]
    wv_ref, total = rest[back + 2 * PLANE:]
    tok, features = hidden_refs[0].shape
    place = idx_ref[0] % PLANE
    summed = own_ref[...]
    for got in got_refs:
        summed = summed + got[...].astype(F32)
    total[...] = summed
    wv = jnp.zeros((HD, features), F32)
    for r in range(PLANE):
        part = total[pl.ds(pl.multiple_of((place ^ r) * tok, tok), tok), :]
        part_refs[r][...] = part.astype(BF16)
        cot_t = jnp.transpose(part)[HD:2 * HD, :].astype(BF16)
        wv = wv + dot(cot_t, hidden_refs[r][...])
    wv = jnp.transpose(wv)
    rows = features // n_ctx
    if wv_ref.shape[2] == 2 * HD:
        for d in range(n_ctx):
            one = wv[d * rows:(d + 1) * rows]
            wv_ref[d] = jnp.concatenate([one[:rows // 2], one[rows // 2:]], axis=1).astype(BF16)
    else:
        for d in range(n_ctx):
            wv_ref[d] = wv[d * rows:(d + 1) * rows].astype(BF16)


def finish_kernel(idx_ref, weight_ref, *rest):
    part_refs, out_refs = rest[:PLANE], rest[PLANE:2 * PLANE]
    kg_ref, xg_ref, attn_ref, qg_ref, parts = rest[2 * PLANE:]
    place = idx_ref[0] % PLANE
    lanes = out_refs[0].shape[1] // 2
    for r in range(PLANE):
        parts[place ^ r] = part_refs[r][...]
        at = pl.ds(pl.multiple_of((place ^ r) * lanes, lanes), lanes)
        attn_ref[:, at] = out_refs[r][:, 0:lanes]
        qg_ref[:, at] = out_refs[r][:, lanes:2 * lanes]
    kg_ref[...] = jnp.concatenate([parts[g, :, 0:HD] for g in range(PLANE)], axis=1)
    value_cot = jnp.concatenate([parts[g, :, HD:2 * HD] for g in range(PLANE)], axis=1)
    xg_ref[...] = lax.dot_general(
        value_cot, weight_ref[...], (((1,), (1,)), ((), ())), preferred_element_type=F32
    ).astype(BF16)


def wv_sum_kernel(wv_ref, out_ref):
    n_ctx, depth, lanes = wv_ref.shape
    sums = []
    for g in range(PLANE):
        total = wv_ref[g].astype(F32)
        for d in range(g + PLANE, n_ctx, PLANE):
            total = total + wv_ref[d].astype(F32)
        sums.append(total)
    for side in range(lanes // HD):
        out_ref[side * depth:(side + 1) * depth, :] = jnp.concatenate(
            [total[:, side * HD:(side + 1) * HD] for total in sums], axis=1
        )


def shifted(x, by):
    n = lax.axis_size("ctx")
    return lax.ppermute(x, "ctx", [(i, i + by) for i in range(n) if 0 <= i + by < n])


def crossed(x, by):
    n = lax.axis_size("ctx")
    return lax.ppermute(x, "ctx", [(i, i ^ by) for i in range(n)])


def in_plane(x):
    n = lax.axis_size("ctx")
    planes = [list(range(i, i + PLANE)) for i in range(0, n, PLANE)]
    return lax.all_to_all(x, "ctx", 0, 0, axis_index_groups=planes, tiled=True)


def shards(
    queries, keys, hidden, value_weight, out_grad, new_logp, old_logp, rewards, group_ids, seq_lengths
):
    n_ctx = lax.axis_size("ctx")
    tok, width = queries.shape
    kv_width = keys.shape[1]
    features = hidden.shape[1]
    back = n_ctx // 2 // PLANE
    ctx = lax.axis_index("ctx").astype(jnp.int32)
    idx = ctx.reshape(1)
    lanes = width // PLANE
    plane_rows = PLANE * tok

    kv = pl.pallas_call(
        values_kernel,
        out_shape=[jax.ShapeDtypeStruct((tok, 2 * HD), BF16)] * PLANE,
        in_specs=[whole(SMEM)] + [whole(VMEM)] * 3,
        out_specs=[whole(VMEM)] * PLANE,
        scratch_shapes=[VMEM((PLANE, tok, 2 * HD), BF16)],
        name="values",
    )(idx, hidden, value_weight, keys)
    kv = list(kv)
    queries, kv[0] = lax.optimization_barrier((queries, kv[0]))
    q_oc = pl.pallas_call(
        queries_kernel,
        out_shape=[jax.ShapeDtypeStruct((tok, 2 * lanes), BF16)] * PLANE,
        in_specs=[whole(SMEM)] * 4 + [whole(VMEM)] * 4,
        out_specs=[whole(VMEM)] * PLANE,
        name="queries",
    )(idx, seq_lengths, group_ids, rewards, new_logp[None, :], old_logp[None, :], queries, out_grad)

    kv = [kv[0]] + [crossed(kv[r], r) for r in range(1, PLANE)]
    kv = pl.pallas_call(
        join_kernel,
        out_shape=jax.ShapeDtypeStruct((plane_rows, 2 * HD), BF16),
        in_specs=[whole(VMEM)] * PLANE,
        out_specs=whole(VMEM),
        name="join",
    )(*kv)
    kv, q_oc = lax.optimization_barrier((kv, list(q_oc)))
    kvs = [kv] + [shifted(kv, w * PLANE) for w in range(1, back + 1)]
    q_oc = [q_oc[0]] + [crossed(q_oc[r], r) for r in range(1, PLANE)]
    hidden_c = crossed(hidden, 1)
    late_hidden, q_oc, kvs = lax.optimization_barrier((hidden, q_oc, kvs))
    hidden_y = crossed(late_hidden, 2)

    outs = attention(idx, seq_lengths, q_oc, kvs)
    hidden_y, outs = lax.optimization_barrier((hidden_y, list(outs)))
    hidden_cy = crossed(hidden_y, 1)
    res, own, backs = outs[:PLANE], outs[PLANE], outs[PLANE + 1:]

    got = [shifted(backs[w - 1], -w * PLANE) for w in range(1, back + 1)]
    res = [res[0]] + [crossed(res[r], r) for r in range(1, PLANE)]
    rows = features // n_ctx
    packed = (rows // 2) % 8 == 0
    piece = (rows // 2, 2 * HD) if packed else (rows, HD)
    outs = pl.pallas_call(
        functools.partial(collect_kernel, back=back, n_ctx=n_ctx),
        out_shape=[jax.ShapeDtypeStruct((tok, 2 * HD), BF16)] * PLANE
        + [jax.ShapeDtypeStruct((n_ctx,) + piece, BF16)],
        in_specs=[whole(SMEM)] + [whole(VMEM)] * (1 + back + PLANE),
        out_specs=[whole(VMEM)] * (PLANE + 1),
        scratch_shapes=[VMEM((plane_rows, 2 * HD), F32)],
        name="collect",
    )(idx, own, *got, hidden, hidden_c, hidden_y, hidden_cy)
    parts, wv = outs[:PLANE], outs[PLANE]
    parts, wv, res = lax.optimization_barrier((list(parts), wv, res))
    parts = [parts[0]] + [crossed(parts[r], r) for r in range(1, PLANE)]
    wv = lax.all_to_all(wv, "ctx", 0, 0, tiled=True)
    k_grad, x_grad, attn, q_grad = pl.pallas_call(
        finish_kernel,
        out_shape=[
            jax.ShapeDtypeStruct((tok, kv_width), BF16),
            jax.ShapeDtypeStruct((tok, features), BF16),
            jax.ShapeDtypeStruct((tok, width), BF16),
            jax.ShapeDtypeStruct((tok, width), BF16),
        ],
        in_specs=[whole(SMEM)] + [whole(VMEM)] * (1 + 2 * PLANE),
        out_specs=[whole(VMEM)] * 4,
        scratch_shapes=[VMEM((PLANE, tok, 2 * HD), BF16)],
        name="finish",
    )(idx, value_weight, *parts, *res)

    wv_grad = pl.pallas_call(
        wv_sum_kernel,
        out_shape=jax.ShapeDtypeStruct((rows, kv_width), F32),
        in_specs=[whole(VMEM)],
        out_specs=whole(VMEM),
        name="wv_sum",
    )(wv)
    return (attn, q_grad, k_grad, x_grad, wv_grad)


def solution(mesh):
    rows = P(("groups", "ctx"), None)
    flat = P(("groups", "ctx"))
    placed = (rows, rows, rows, P(), rows, flat, flat, P("groups"), P("groups"), P("groups"))
    return jax.shard_map(
        shards, mesh=mesh, in_specs=placed, out_specs=(rows,) * 5, check_vma=False
    )
```

```python
import functools
import math

import jax
import jax.numpy as jnp
from jax import lax
from jax.experimental import pallas as pl
from jax.experimental.pallas import tpu as pltpu
from jax.sharding import PartitionSpec as P

HD = 64
PLANE = 4
SCALE = 1.0 / math.sqrt(HD)
BIG_NEGATIVE = -1e30
VMEM = pltpu.VMEM
SMEM = pltpu.SMEM
BF16 = jnp.bfloat16
F32 = jnp.float32


def dot(a, b):
    return lax.dot_general(a, b, (((1,), (0,)), ((), ())), preferred_element_type=F32)


def whole(space):
    return pl.BlockSpec(memory_space=space)


def small(name, mib=12):
    return dict(name=name, compiler_params=pltpu.CompilerParams(vmem_limit_bytes=mib * 2**20))


def token_weights(idx, tok, seq_ref, rew_ref, gid_ref, new_ref, old_ref):
    nseq = seq_ref.shape[0]
    pos = idx * tok + lax.broadcasted_iota(jnp.int32, (1, tok), 1)
    reward = jnp.zeros(pos.shape, F32)
    total = jnp.zeros(pos.shape, F32)
    count = jnp.ones(pos.shape, F32)
    begin = jnp.int32(0)
    for i in range(nseq):
        gsum = F32(0)
        gcount = F32(0)
        for j in range(nseq):
            same = gid_ref[j] == gid_ref[i]
            gsum = gsum + jnp.where(same, rew_ref[j], 0.0)
            gcount = gcount + jnp.where(same, 1.0, 0.0)
        here = pos >= begin
        reward = jnp.where(here, rew_ref[i], reward)
        total = jnp.where(here, gsum, total)
        count = jnp.where(here, gcount, count)
        begin = begin + seq_ref[i]
    return (total / count - reward) * jnp.exp(new_ref[...] - old_ref[...])


def values_kernel(idx_ref, hidden_ref, weight_ref, keys_ref, *rest):
    out_refs, parts = rest[:PLANE], rest[PLANE]
    place = idx_ref[0] % PLANE
    values = dot(hidden_ref[...], weight_ref[...]).astype(BF16)
    for g in range(PLANE):
        at = slice(g * HD, (g + 1) * HD)
        parts[g] = jnp.concatenate([keys_ref[:, at], values[:, at]], axis=1)
    for r in range(PLANE):
        out_refs[r][...] = parts[place ^ r]


def join_kernel(*refs):
    tok = refs[0].shape[0]
    for r in range(PLANE):
        refs[PLANE][r * tok:(r + 1) * tok, :] = refs[r][...]


def queries_kernel(
    idx_ref, seq_ref, gid_ref, rew_ref, new_ref, old_ref, q_ref, og_ref, *out_refs
):
    tok, width = q_ref.shape
    lanes = width // PLANE
    place = idx_ref[0] % PLANE
    weight = token_weights(idx_ref[0], tok, seq_ref, rew_ref, gid_ref, new_ref, old_ref)
    weight = jnp.transpose(jnp.broadcast_to(weight, (tok, tok)))[:, 0:1]
    for r in range(PLANE):
        at = pl.ds(pl.multiple_of((place ^ r) * lanes, lanes), lanes)
        out_refs[r][:, 0:lanes] = (q_ref[:, at].astype(F32) * SCALE).astype(BF16)
        out_refs[r][:, lanes:2 * lanes] = (og_ref[:, at].astype(F32) * weight).astype(BF16)


def attention_kernel(idx_ref, seq_ref, *rest, back, heads, per_pass):
    in_refs = rest[:PLANE]
    kv_refs = rest[PLANE:PLANE + back + 1]
    rest = rest[PLANE + back + 1:]
    out_refs = rest[:PLANE]
    own_ref = rest[PLANE]
    back_refs = rest[PLANE + 1:PLANE + 1 + back]
    (q_in, res, k2, v2, k2t, v2t, qm, om, qt, ot, start, bias, score, probs, dscore, o_acc, q_acc, top, low, inner,
     acc_k, acc_v) = rest[PLANE + 1 + back:]
    tok = in_refs[0].shape[0]
    rows_all = PLANE * tok
    blk = rows_all // 2
    width = heads * HD
    plane = idx_ref[0] // PLANE
    place = idx_ref[0] % PLANE
    base = (plane - back) * 2

    for r in range(PLANE):
        q_in[pl.ds(pl.multiple_of((place ^ r) * tok, tok), tok), :] = in_refs[r][...]
    lower = lax.broadcasted_iota(jnp.int32, (tok, 2 * HD), 1) < HD
    for w in range(back + 1):
        for r in range(PLANE):
            at = pl.ds(pl.multiple_of((back - w) * rows_all + (place ^ r) * tok, tok), tok)
            part = kv_refs[w][r * tok:(r + 1) * tok, :].astype(F32)
            swapped = pltpu.roll(part, HD, 1)
            k2[at, :] = jnp.where(lower, part, swapped).astype(BF16)
            v2[at, :] = jnp.where(lower, swapped, part).astype(BF16)
            part_t = jnp.transpose(part).astype(BF16)
            k2t[:, at] = jnp.concatenate([part_t[:HD], part_t[:HD]], axis=0)
            v2t[:, at] = jnp.concatenate([part_t[HD:], part_t[HD:]], axis=0)
    acc_k[...] = jnp.zeros_like(acc_k)
    acc_v[...] = jnp.zeros_like(acc_v)
    left = lax.broadcasted_iota(jnp.int32, (blk, 2 * HD), 1) < HD
    pairs_at = [
        (slice(2 * a * blk, (2 * a + 1) * blk), slice((2 * a + 1) * blk, (2 * a + 2) * blk))
        for a in range(per_pass // 2)
    ]

    def twice(x):
        return jnp.concatenate([x, x], axis=1)

    def block(b, carry):
        pair_hi = plane * 2 + b
        first = pair_hi * blk
        pos = first + lax.broadcasted_iota(jnp.int32, (blk, 2 * HD), 0)
        starts = jnp.zeros_like(pos)
        start_lo = jnp.int32(0)
        start_hi = jnp.int32(0)
        begin = jnp.int32(0)
        for i in range(seq_ref.shape[0]):
            starts = jnp.where(pos >= begin, begin, starts)
            start_lo = jnp.where(first >= begin, begin, start_lo)
            start_hi = jnp.where(first + blk - 1 >= begin, begin, start_hi)
            begin = begin + seq_ref[i]
        start[...] = starts
        steps = pair_hi - start_lo // blk + 1
        q_rows = pl.ds(pl.multiple_of(b * blk, blk), blk)

        for h0 in range(0, heads, per_pass):
            def lanes_of(a, side=0):
                return slice(side * width + (h0 + 2 * a) * HD, side * width + (h0 + 2 * a + 2) * HD)

            for a, (even, odd) in enumerate(pairs_at):
                q2 = q_in[q_rows, lanes_of(a)]
                qm[even, :] = jnp.where(left, q2, jnp.zeros_like(q2))
                qm[odd, :] = jnp.where(left, jnp.zeros_like(q2), q2)
                q2t = jnp.transpose(q2.astype(F32)).astype(BF16)
                qt[:, even] = q2t[:HD]
                qt[:, odd] = q2t[HD:]

            top[...] = jnp.full(top.shape, BIG_NEGATIVE, F32)
            low[...] = jnp.zeros_like(low)
            o_acc[...] = jnp.zeros_like(o_acc)
            q_acc[...] = jnp.zeros_like(q_acc)

            def scores(step, carry):
                pair = pair_hi - step
                cols_k = pl.ds(pl.multiple_of((pair - base) * blk, blk), blk)
                inside = (step > 0) & (pair * blk >= start_hi)

                def keep(at, s):
                    score[step, at, :] = s
                    top[at, :] = jnp.maximum(top[at, :], jnp.maximum(s[:, :2 * HD], s[:, 2 * HD:]))

                @pl.when(inside)
                def _():
                    k_t = k2t[:, cols_k]
                    for even, odd in pairs_at:
                        at = slice(even.start, odd.stop)
                        keep(at, dot(qm[at, :], k_t))

                @pl.when(jnp.logical_not(inside))
                def _():
                    k_t = k2t[:, cols_k]
                    key_pos = pair * blk + lax.broadcasted_iota(jnp.int32, (blk, blk), 1)
                    tok_pos = first + lax.broadcasted_iota(jnp.int32, (blk, blk), 0)
                    seen = (key_pos >= twice(start[...])) & (key_pos <= tok_pos)
                    bias[...] = jnp.where(seen, 0.0, BIG_NEGATIVE)
                    for even, odd in pairs_at:
                        s = dot(qm[even.start:odd.stop, :], k_t)
                        keep(even, s[:blk] + bias[...])
                        keep(odd, s[blk:] + bias[...])

                return carry

            lax.fori_loop(0, steps, scores, 0)
            top[...] = jnp.broadcast_to(jnp.max(top[...], axis=1, keepdims=True), top.shape)

            def outputs(step, carry):
                pair = pair_hi - step
                rows = pl.ds(pl.multiple_of((pair - base) * blk, blk), blk)
                vv = v2[rows, :]
                for even, odd in pairs_at:
                    at = slice(even.start, odd.stop)
                    e = jnp.exp(score[step, at, :] - twice(top[at, :]))
                    eb = e.astype(BF16)
                    probs[step, at, :] = eb
                    low[at, :] = low[at, :] + (e[:, :2 * HD] + e[:, 2 * HD:])
                    o_acc[at, :] = o_acc[at, :] + dot(eb, vv)
                return carry

            lax.fori_loop(0, steps, outputs, 0)
            for a, pair_at in enumerate(pairs_at):
                o2 = q_in[q_rows, lanes_of(a, 1)].astype(F32)
                out = []
                scaled = []
                for side, at in enumerate(pair_at):
                    inv = 1.0 / jnp.sum(low[at, :], axis=1, keepdims=True)
                    out.append(o_acc[at, :] * inv)
                    mine = jnp.where(left if side == 0 else jnp.logical_not(left), o2, 0.0)
                    inner[at, :] = jnp.broadcast_to(
                        jnp.sum(mine * out[side], axis=1, keepdims=True) * inv, (blk, 2 * HD)
                    )
                    scaled.append(mine * inv)
                    om[at, :] = scaled[side].astype(BF16)
                res[q_rows, lanes_of(a)] = jnp.where(left, out[0], out[1]).astype(BF16)
                o2t = jnp.transpose(scaled[0] + scaled[1]).astype(BF16)
                ot[:, pair_at[0]] = o2t[:HD]
                ot[:, pair_at[1]] = o2t[HD:]

            def gradients(step, carry):
                pair = pair_hi - step
                rows = pl.ds(pl.multiple_of((pair - base) * blk, blk), blk)
                kk = k2[rows, :]
                v_t = v2t[:, rows]
                for even, odd in pairs_at:
                    at = slice(even.start, odd.stop)
                    dp = dot(om[at, :], v_t)
                    ds = (probs[step, at, :].astype(F32) * (dp - twice(inner[at, :]))).astype(BF16)
                    dscore[at, :] = ds
                    q_acc[at, :] = q_acc[at, :] + dot(ds, kk)
                acc_v[:, rows] = acc_v[:, rows] + dot(ot[...], probs[step])
                acc_k[:, rows] = acc_k[:, rows] + dot(qt[...], dscore[...])
                return carry

            lax.fori_loop(0, steps, gradients, 0)
            for a, (even, odd) in enumerate(pairs_at):
                qg = jnp.where(left, q_acc[even, :], q_acc[odd, :]) * SCALE
                res[q_rows, lanes_of(a, 1)] = qg.astype(BF16)
        return carry

    lax.fori_loop(0, 2, block, 0)

    for w in range(back + 1):
        at = slice((back - w) * rows_all, (back - w + 1) * rows_all)
        both = jnp.transpose(jnp.concatenate([acc_k[:, at], acc_v[:, at]], axis=0))
        if w == 0:
            own_ref[...] = both
        else:
            back_refs[w - 1][...] = both.astype(BF16)
    for r in range(PLANE):
        out_refs[r][...] = res[pl.ds(pl.multiple_of((place ^ r) * tok, tok), tok), :]


def attention(idx, seq, q_oc, kvs):
    tok, width2 = q_oc[0].shape
    rows = PLANE * tok
    width = width2 // 2
    back = len(kvs) - 1
    heads = width // HD
    keys = rows * (back + 1)
    blk = rows // 2
    pairs = 2 * back + 1
    per_pass = heads
    while per_pass > 2 and pairs * blk * per_pass * blk * 6 > 20 * 2**20:
        per_pass //= 2
    cols = per_pass * blk
    held = pairs * blk * cols * 6 + 10 * rows * width2 + 16 * keys * 2 * HD + 64 * cols * 2 * HD
    return pl.pallas_call(
        functools.partial(attention_kernel, back=back, heads=heads, per_pass=per_pass),
        out_shape=(
            [jax.ShapeDtypeStruct((tok, width2), BF16)] * PLANE
            + [jax.ShapeDtypeStruct((rows, 2 * HD), F32)]
            + [jax.ShapeDtypeStruct((rows, 2 * HD), BF16)] * back
        ),
        in_specs=[whole(SMEM)] * 2 + [whole(VMEM)] * (PLANE + len(kvs)),
        out_specs=[whole(VMEM)] * (PLANE + 1 + back),
        scratch_shapes=[
            VMEM((rows, width2), BF16),
            VMEM((rows, width2), BF16),
            VMEM((keys, 2 * HD), BF16),
            VMEM((keys, 2 * HD), BF16),
            VMEM((2 * HD, keys), BF16),
            VMEM((2 * HD, keys), BF16),
            VMEM((cols, 2 * HD), BF16),
            VMEM((cols, 2 * HD), BF16),
            VMEM((HD, cols), BF16),
            VMEM((HD, cols), BF16),
            VMEM((blk, 2 * HD), jnp.int32),
            VMEM((blk, blk), F32),
            VMEM((pairs, cols, blk), F32),
            VMEM((pairs, cols, blk), BF16),
            VMEM((cols, blk), BF16),
            VMEM((cols, 2 * HD), F32),
            VMEM((cols, 2 * HD), F32),
            VMEM((cols, 2 * HD), F32),
            VMEM((cols, 2 * HD), F32),
            VMEM((cols, 2 * HD), F32),
            VMEM((HD, keys), F32),
            VMEM((HD, keys), F32),
        ],
        compiler_params=pltpu.CompilerParams(vmem_limit_bytes=min(56 * 2**20, held + 8 * 2**20)),
        cost_estimate=pl.CostEstimate(
            flops=40 * keys * rows * width, bytes_accessed=4 * 2**20, transcendentals=0
        ),
        name="attention",
    )(idx, seq, *q_oc, *kvs)


def sum_kernel(idx_ref, own_ref, *rest, back):
    got_refs = rest[:back]
    part_refs = rest[back:back + PLANE]
    total = rest[back + PLANE]
    tok = part_refs[0].shape[0]
    place = idx_ref[0] % PLANE
    summed = own_ref[...]
    for got in got_refs:
        summed = summed + got[...].astype(F32)
    total[...] = summed
    for r in range(PLANE):
        part_refs[r][...] = total[pl.ds(pl.multiple_of((place ^ r) * tok, tok), tok), :].astype(BF16)


def wv_kernel(*refs, n_ctx):
    part_refs, hidden_refs, wv_ref = refs[:PLANE], refs[PLANE:2 * PLANE], refs[2 * PLANE]
    features = hidden_refs[0].shape[1]
    wv = jnp.zeros((HD, features), F32)
    for r in range(PLANE):
        cot_t = jnp.transpose(part_refs[r][...].astype(F32))[HD:2 * HD, :].astype(BF16)
        wv = wv + dot(cot_t, hidden_refs[r][...])
    wv = jnp.transpose(wv)
    rows = features // n_ctx
    if wv_ref.shape[2] == 2 * HD:
        for d in range(n_ctx):
            one = wv[d * rows:(d + 1) * rows]
            wv_ref[d] = jnp.concatenate([one[:rows // 2], one[rows // 2:]], axis=1).astype(BF16)
    else:
        for d in range(n_ctx):
            wv_ref[d] = wv[d * rows:(d + 1) * rows].astype(BF16)


def results_kernel(idx_ref, *refs):
    out_refs = refs[:PLANE]
    attn_ref, qg_ref = refs[PLANE:]
    place = idx_ref[0] % PLANE
    lanes = out_refs[0].shape[1] // 2
    for r in range(PLANE):
        at = pl.ds(pl.multiple_of((place ^ r) * lanes, lanes), lanes)
        attn_ref[:, at] = out_refs[r][:, 0:lanes]
        qg_ref[:, at] = out_refs[r][:, lanes:2 * lanes]


def finish_kernel(idx_ref, weight_ref, *rest):
    part_refs = rest[:PLANE]
    kg_ref, xg_ref, parts = rest[PLANE:]
    place = idx_ref[0] % PLANE
    for r in range(PLANE):
        parts[place ^ r] = part_refs[r][...]
    kg_ref[...] = jnp.concatenate([parts[g, :, 0:HD] for g in range(PLANE)], axis=1)
    value_cot = jnp.concatenate([parts[g, :, HD:2 * HD] for g in range(PLANE)], axis=1)
    xg_ref[...] = lax.dot_general(
        value_cot, weight_ref[...], (((1,), (1,)), ((), ())), preferred_element_type=F32
    ).astype(BF16)


def wv_sum_kernel(wv_ref, out_ref):
    n_ctx, depth, lanes = wv_ref.shape
    sums = []
    for g in range(PLANE):
        total = wv_ref[g].astype(F32)
        for d in range(g + PLANE, n_ctx, PLANE):
            total = total + wv_ref[d].astype(F32)
        sums.append(total)
    for side in range(lanes // HD):
        out_ref[side * depth:(side + 1) * depth, :] = jnp.concatenate(
            [total[:, side * HD:(side + 1) * HD] for total in sums], axis=1
        )


def shifted(x, by):
    n = lax.axis_size("ctx")
    return lax.ppermute(x, "ctx", [(i, i + by) for i in range(n) if 0 <= i + by < n])


def crossed(x, by):
    n = lax.axis_size("ctx")
    return lax.ppermute(x, "ctx", [(i, i ^ by) for i in range(n)])


def in_plane(x):
    n = lax.axis_size("ctx")
    planes = [list(range(i, i + PLANE)) for i in range(0, n, PLANE)]
    return lax.all_to_all(x, "ctx", 0, 0, axis_index_groups=planes, tiled=True)


def shards(
    queries, keys, hidden, value_weight, out_grad, new_logp, old_logp, rewards, group_ids, seq_lengths
):
    n_ctx = lax.axis_size("ctx")
    tok, width = queries.shape
    kv_width = keys.shape[1]
    features = hidden.shape[1]
    back = n_ctx // 2 // PLANE
    ctx = lax.axis_index("ctx").astype(jnp.int32)
    idx = ctx.reshape(1)
    lanes = width // PLANE
    plane_rows = PLANE * tok

    kv = pl.pallas_call(
        values_kernel,
        out_shape=[jax.ShapeDtypeStruct((tok, 2 * HD), BF16)] * PLANE,
        in_specs=[whole(SMEM)] + [whole(VMEM)] * 3,
        out_specs=[whole(VMEM)] * PLANE,
        scratch_shapes=[VMEM((PLANE, tok, 2 * HD), BF16)],
        **small("values"),
    )(idx, hidden, value_weight, keys)
    kv = list(kv)
    queries, kv[0] = lax.optimization_barrier((queries, kv[0]))
    q_oc = pl.pallas_call(
        queries_kernel,
        out_shape=[jax.ShapeDtypeStruct((tok, 2 * lanes), BF16)] * PLANE,
        in_specs=[whole(SMEM)] * 4 + [whole(VMEM)] * 4,
        out_specs=[whole(VMEM)] * PLANE,
        **small("queries"),
    )(idx, seq_lengths, group_ids, rewards, new_logp[None, :], old_logp[None, :], queries, out_grad)

    kv = [kv[0]] + [crossed(kv[r], r) for r in range(1, PLANE)]
    kv, q_oc = lax.optimization_barrier((kv, list(q_oc)))
    kv = pl.pallas_call(
        join_kernel,
        out_shape=jax.ShapeDtypeStruct((plane_rows, 2 * HD), BF16),
        in_specs=[whole(VMEM)] * PLANE,
        out_specs=whole(VMEM),
        **small("join"),
    )(*kv)
    kvs = [kv] + [shifted(kv, w * PLANE) for w in range(1, back + 1)]
    q_oc = [q_oc[0]] + [crossed(q_oc[r], r) for r in range(1, PLANE)]
    late_hidden, q_oc, hidden_c = lax.optimization_barrier((hidden, q_oc, crossed(hidden, 1)))
    hidden_y = crossed(late_hidden, 2)

    outs = attention(idx, seq_lengths, q_oc, kvs)
    hidden_y, outs = lax.optimization_barrier((hidden_y, list(outs)))
    hidden_cy = crossed(hidden_y, 1)
    res, own, backs = list(outs[:PLANE]), outs[PLANE], outs[PLANE + 1:]

    got = [shifted(backs[w - 1], -w * PLANE) for w in range(1, back + 1)]
    got, res[1] = lax.optimization_barrier((got, res[1]))
    res = [res[0]] + [crossed(res[r], r) for r in range(1, PLANE)]
    parts = pl.pallas_call(
        functools.partial(sum_kernel, back=back),
        out_shape=[jax.ShapeDtypeStruct((tok, 2 * HD), BF16)] * PLANE,
        in_specs=[whole(SMEM)] + [whole(VMEM)] * (1 + back),
        out_specs=[whole(VMEM)] * PLANE,
        scratch_shapes=[VMEM((plane_rows, 2 * HD), F32)],
        **small("sum"),
    )(idx, own, *got)
    own_parts = list(parts)
    parts = [parts[0]] + [crossed(parts[r], r) for r in range(1, PLANE)]
    rows = features // n_ctx
    packed = (rows // 2) % 8 == 0
    piece = (rows // 2, 2 * HD) if packed else (rows, HD)
    wv = pl.pallas_call(
        functools.partial(wv_kernel, n_ctx=n_ctx),
        out_shape=jax.ShapeDtypeStruct((n_ctx,) + piece, BF16),
        in_specs=[whole(VMEM)] * (2 * PLANE),
        out_specs=whole(VMEM),
        **small("wv"),
    )(*own_parts, hidden, hidden_c, hidden_y, hidden_cy)
    wv, parts[1] = lax.optimization_barrier((wv, parts[1]))
    wv = lax.all_to_all(wv, "ctx", 0, 0, tiled=True)
    attn, q_grad = pl.pallas_call(
        results_kernel,
        out_shape=[jax.ShapeDtypeStruct((tok, width), BF16)] * 2,
        in_specs=[whole(SMEM)] + [whole(VMEM)] * PLANE,
        out_specs=[whole(VMEM)] * 2,
        **small("results"),
    )(idx, *res)
    k_grad, x_grad = pl.pallas_call(
        finish_kernel,
        out_shape=[
            jax.ShapeDtypeStruct((tok, kv_width), BF16),
            jax.ShapeDtypeStruct((tok, features), BF16),
        ],
        in_specs=[whole(SMEM)] + [whole(VMEM)] * (1 + PLANE),
        out_specs=[whole(VMEM)] * 2,
        scratch_shapes=[VMEM((PLANE, tok, 2 * HD), BF16)],
        **small("finish"),
    )(idx, value_weight, *parts)

    wv_grad = pl.pallas_call(
        wv_sum_kernel,
        out_shape=jax.ShapeDtypeStruct((rows, kv_width), F32),
        in_specs=[whole(VMEM)],
        out_specs=whole(VMEM),
        **small("wv_sum"),
    )(wv)
    return (attn, q_grad, k_grad, x_grad, wv_grad)


def solution(mesh):
    rows = P(("groups", "ctx"), None)
    flat = P(("groups", "ctx"))
    placed = (rows, rows, rows, P(), rows, flat, flat, P("groups"), P("groups"), P("groups"))
    return jax.shard_map(
        shards, mesh=mesh, in_specs=placed, out_specs=(rows,) * 5, check_vma=False
    )
```

```python
import functools
import math

import jax
import jax.numpy as jnp
from jax import lax
from jax.experimental import pallas as pl
from jax.experimental.pallas import tpu as pltpu
from jax.sharding import PartitionSpec as P

HD = 64
PLANE = 4
SCALE = 1.0 / math.sqrt(HD)
BIG_NEGATIVE = -1e30
VMEM = pltpu.VMEM
SMEM = pltpu.SMEM
BF16 = jnp.bfloat16
F32 = jnp.float32


def dot(a, b):
    return lax.dot_general(a, b, (((1,), (0,)), ((), ())), preferred_element_type=F32)


def whole(space):
    return pl.BlockSpec(memory_space=space)


def small(name, mib=12):
    return dict(name=name, compiler_params=pltpu.CompilerParams(vmem_limit_bytes=mib * 2**20))


def token_weights(idx, tok, seq_ref, rew_ref, gid_ref, new_ref, old_ref):
    nseq = seq_ref.shape[0]
    pos = idx * tok + lax.broadcasted_iota(jnp.int32, (1, tok), 1)
    reward = jnp.zeros(pos.shape, F32)
    total = jnp.zeros(pos.shape, F32)
    count = jnp.ones(pos.shape, F32)
    begin = jnp.int32(0)
    for i in range(nseq):
        gsum = F32(0)
        gcount = F32(0)
        for j in range(nseq):
            same = gid_ref[j] == gid_ref[i]
            gsum = gsum + jnp.where(same, rew_ref[j], 0.0)
            gcount = gcount + jnp.where(same, 1.0, 0.0)
        here = pos >= begin
        reward = jnp.where(here, rew_ref[i], reward)
        total = jnp.where(here, gsum, total)
        count = jnp.where(here, gcount, count)
        begin = begin + seq_ref[i]
    return (total / count - reward) * jnp.exp(new_ref[...] - old_ref[...])


def values_kernel(idx_ref, hidden_ref, weight_ref, keys_ref, *rest):
    out_refs, parts = rest[:PLANE], rest[PLANE]
    place = idx_ref[0] % PLANE
    values = dot(hidden_ref[...], weight_ref[...]).astype(BF16)
    for g in range(PLANE):
        at = slice(g * HD, (g + 1) * HD)
        parts[g] = jnp.concatenate([keys_ref[:, at], values[:, at]], axis=1)
    for r in range(PLANE):
        out_refs[r][...] = parts[place ^ r]


def join_kernel(*refs):
    tok = refs[0].shape[0]
    for r in range(PLANE):
        refs[PLANE][r * tok:(r + 1) * tok, :] = refs[r][...]


def queries_kernel(
    idx_ref, seq_ref, gid_ref, rew_ref, new_ref, old_ref, q_ref, og_ref, *out_refs
):
    tok, width = q_ref.shape
    lanes = width // PLANE
    place = idx_ref[0] % PLANE
    weight = token_weights(idx_ref[0], tok, seq_ref, rew_ref, gid_ref, new_ref, old_ref)
    weight = jnp.transpose(jnp.broadcast_to(weight, (tok, tok)))[:, 0:1]
    for r in range(PLANE):
        at = pl.ds(pl.multiple_of((place ^ r) * lanes, lanes), lanes)
        out_refs[r][:, 0:lanes] = (q_ref[:, at].astype(F32) * SCALE).astype(BF16)
        out_refs[r][:, lanes:2 * lanes] = (og_ref[:, at].astype(F32) * weight).astype(BF16)


def attention_kernel(idx_ref, seq_ref, *rest, back, heads, per_pass):
    in_refs = rest[:PLANE]
    kv_refs = rest[PLANE:PLANE + back + 1]
    rest = rest[PLANE + back + 1:]
    out_refs = rest[:PLANE]
    own_ref = rest[PLANE]
    back_refs = rest[PLANE + 1:PLANE + 1 + back]
    (q_in, res, k2, v2, k2t, v2t, qm, om, qt, ot, start, bias, score, probs, dscore, o_acc, q_acc, top, low, inner,
     acc_k, acc_v) = rest[PLANE + 1 + back:]
    tok = in_refs[0].shape[0]
    rows_all = PLANE * tok
    blk = rows_all // 2
    width = heads * HD
    plane = idx_ref[0] // PLANE
    place = idx_ref[0] % PLANE
    base = (plane - back) * 2

    for r in range(PLANE):
        q_in[pl.ds(pl.multiple_of((place ^ r) * tok, tok), tok), :] = in_refs[r][...]
    lower = lax.broadcasted_iota(jnp.int32, (tok, 2 * HD), 1) < HD
    for w in range(back + 1):
        for r in range(PLANE):
            at = pl.ds(pl.multiple_of((back - w) * rows_all + (place ^ r) * tok, tok), tok)
            part = kv_refs[w][r * tok:(r + 1) * tok, :].astype(F32)
            swapped = pltpu.roll(part, HD, 1)
            k2[at, :] = jnp.where(lower, part, swapped).astype(BF16)
            v2[at, :] = jnp.where(lower, swapped, part).astype(BF16)
            part_t = jnp.transpose(part).astype(BF16)
            k2t[:, at] = jnp.concatenate([part_t[:HD], part_t[:HD]], axis=0)
            v2t[:, at] = jnp.concatenate([part_t[HD:], part_t[HD:]], axis=0)
    acc_k[...] = jnp.zeros_like(acc_k)
    acc_v[...] = jnp.zeros_like(acc_v)
    left = lax.broadcasted_iota(jnp.int32, (blk, 2 * HD), 1) < HD
    pairs_at = [
        (slice(2 * a * blk, (2 * a + 1) * blk), slice((2 * a + 1) * blk, (2 * a + 2) * blk))
        for a in range(per_pass // 2)
    ]

    def twice(x):
        return jnp.concatenate([x, x], axis=1)

    def block(b, carry):
        pair_hi = plane * 2 + b
        first = pair_hi * blk
        pos = first + lax.broadcasted_iota(jnp.int32, (blk, 2 * HD), 0)
        starts = jnp.zeros_like(pos)
        start_lo = jnp.int32(0)
        start_hi = jnp.int32(0)
        begin = jnp.int32(0)
        for i in range(seq_ref.shape[0]):
            starts = jnp.where(pos >= begin, begin, starts)
            start_lo = jnp.where(first >= begin, begin, start_lo)
            start_hi = jnp.where(first + blk - 1 >= begin, begin, start_hi)
            begin = begin + seq_ref[i]
        start[...] = starts
        steps = pair_hi - start_lo // blk + 1
        q_rows = pl.ds(pl.multiple_of(b * blk, blk), blk)

        for h0 in range(0, heads, per_pass):
            def lanes_of(a, side=0):
                return slice(side * width + (h0 + 2 * a) * HD, side * width + (h0 + 2 * a + 2) * HD)

            for a, (even, odd) in enumerate(pairs_at):
                q2 = q_in[q_rows, lanes_of(a)]
                qm[even, :] = jnp.where(left, q2, jnp.zeros_like(q2))
                qm[odd, :] = jnp.where(left, jnp.zeros_like(q2), q2)
                q2t = jnp.transpose(q2.astype(F32)).astype(BF16)
                qt[:, even] = q2t[:HD]
                qt[:, odd] = q2t[HD:]

            top[...] = jnp.full(top.shape, BIG_NEGATIVE, F32)
            low[...] = jnp.zeros_like(low)
            o_acc[...] = jnp.zeros_like(o_acc)
            q_acc[...] = jnp.zeros_like(q_acc)

            def scores(step, carry):
                pair = pair_hi - step
                cols_k = pl.ds(pl.multiple_of((pair - base) * blk, blk), blk)
                inside = (step > 0) & (pair * blk >= start_hi)

                def keep(at, s):
                    score[step, at, :] = s
                    top[at, :] = jnp.maximum(top[at, :], jnp.maximum(s[:, :2 * HD], s[:, 2 * HD:]))

                @pl.when(inside)
                def _():
                    k_t = k2t[:, cols_k]
                    for even, odd in pairs_at:
                        at = slice(even.start, odd.stop)
                        keep(at, dot(qm[at, :], k_t))

                @pl.when(jnp.logical_not(inside))
                def _():
                    k_t = k2t[:, cols_k]
                    key_pos = pair * blk + lax.broadcasted_iota(jnp.int32, (blk, blk), 1)
                    tok_pos = first + lax.broadcasted_iota(jnp.int32, (blk, blk), 0)
                    seen = (key_pos >= twice(start[...])) & (key_pos <= tok_pos)
                    bias[...] = jnp.where(seen, 0.0, BIG_NEGATIVE)
                    for even, odd in pairs_at:
                        s = dot(qm[even.start:odd.stop, :], k_t)
                        keep(even, s[:blk] + bias[...])
                        keep(odd, s[blk:] + bias[...])

                return carry

            lax.fori_loop(0, steps, scores, 0)
            top[...] = jnp.broadcast_to(jnp.max(top[...], axis=1, keepdims=True), top.shape)

            def outputs(step, carry):
                pair = pair_hi - step
                rows = pl.ds(pl.multiple_of((pair - base) * blk, blk), blk)
                vv = v2[rows, :]
                for even, odd in pairs_at:
                    at = slice(even.start, odd.stop)
                    e = jnp.exp(score[step, at, :] - twice(top[at, :]))
                    eb = e.astype(BF16)
                    probs[step, at, :] = eb
                    low[at, :] = low[at, :] + (e[:, :2 * HD] + e[:, 2 * HD:])
                    o_acc[at, :] = o_acc[at, :] + dot(eb, vv)
                return carry

            lax.fori_loop(0, steps, outputs, 0)
            for a, pair_at in enumerate(pairs_at):
                o2 = q_in[q_rows, lanes_of(a, 1)].astype(F32)
                out = []
                scaled = []
                for side, at in enumerate(pair_at):
                    inv = 1.0 / jnp.sum(low[at, :], axis=1, keepdims=True)
                    out.append(o_acc[at, :] * inv)
                    mine = jnp.where(left if side == 0 else jnp.logical_not(left), o2, 0.0)
                    inner[at, :] = jnp.broadcast_to(
                        jnp.sum(mine * out[side], axis=1, keepdims=True) * inv, (blk, 2 * HD)
                    )
                    scaled.append(mine * inv)
                    om[at, :] = scaled[side].astype(BF16)
                res[q_rows, lanes_of(a)] = jnp.where(left, out[0], out[1]).astype(BF16)
                o2t = jnp.transpose(scaled[0] + scaled[1]).astype(BF16)
                ot[:, pair_at[0]] = o2t[:HD]
                ot[:, pair_at[1]] = o2t[HD:]

            def gradients(step, carry):
                pair = pair_hi - step
                rows = pl.ds(pl.multiple_of((pair - base) * blk, blk), blk)
                kk = k2[rows, :]
                v_t = v2t[:, rows]
                for even, odd in pairs_at:
                    at = slice(even.start, odd.stop)
                    dp = dot(om[at, :], v_t)
                    ds = (probs[step, at, :].astype(F32) * (dp - twice(inner[at, :]))).astype(BF16)
                    dscore[at, :] = ds
                    q_acc[at, :] = q_acc[at, :] + dot(ds, kk)
                acc_v[:, rows] = acc_v[:, rows] + dot(ot[...], probs[step])
                acc_k[:, rows] = acc_k[:, rows] + dot(qt[...], dscore[...])
                return carry

            lax.fori_loop(0, steps, gradients, 0)
            for a, (even, odd) in enumerate(pairs_at):
                qg = jnp.where(left, q_acc[even, :], q_acc[odd, :]) * SCALE
                res[q_rows, lanes_of(a, 1)] = qg.astype(BF16)
        return carry

    lax.fori_loop(0, 2, block, 0)

    for w in range(back + 1):
        at = slice((back - w) * rows_all, (back - w + 1) * rows_all)
        both = jnp.transpose(jnp.concatenate([acc_k[:, at], acc_v[:, at]], axis=0))
        if w == 0:
            own_ref[...] = both
        else:
            back_refs[w - 1][...] = both.astype(BF16)
    for r in range(PLANE):
        out_refs[r][...] = res[pl.ds(pl.multiple_of((place ^ r) * tok, tok), tok), :]


def attention(idx, seq, q_oc, kvs):
    tok, width2 = q_oc[0].shape
    rows = PLANE * tok
    width = width2 // 2
    back = len(kvs) - 1
    heads = width // HD
    keys = rows * (back + 1)
    blk = rows // 2
    pairs = 2 * back + 1
    per_pass = heads
    while per_pass > 2 and pairs * blk * per_pass * blk * 6 > 20 * 2**20:
        per_pass //= 2
    cols = per_pass * blk
    held = pairs * blk * cols * 6 + 10 * rows * width2 + 16 * keys * 2 * HD + 64 * cols * 2 * HD
    return pl.pallas_call(
        functools.partial(attention_kernel, back=back, heads=heads, per_pass=per_pass),
        out_shape=(
            [jax.ShapeDtypeStruct((tok, width2), BF16)] * PLANE
            + [jax.ShapeDtypeStruct((rows, 2 * HD), F32)]
            + [jax.ShapeDtypeStruct((rows, 2 * HD), BF16)] * back
        ),
        in_specs=[whole(SMEM)] * 2 + [whole(VMEM)] * (PLANE + len(kvs)),
        out_specs=[whole(VMEM)] * (PLANE + 1 + back),
        scratch_shapes=[
            VMEM((rows, width2), BF16),
            VMEM((rows, width2), BF16),
            VMEM((keys, 2 * HD), BF16),
            VMEM((keys, 2 * HD), BF16),
            VMEM((2 * HD, keys), BF16),
            VMEM((2 * HD, keys), BF16),
            VMEM((cols, 2 * HD), BF16),
            VMEM((cols, 2 * HD), BF16),
            VMEM((HD, cols), BF16),
            VMEM((HD, cols), BF16),
            VMEM((blk, 2 * HD), jnp.int32),
            VMEM((blk, blk), F32),
            VMEM((pairs, cols, blk), F32),
            VMEM((pairs, cols, blk), BF16),
            VMEM((cols, blk), BF16),
            VMEM((cols, 2 * HD), F32),
            VMEM((cols, 2 * HD), F32),
            VMEM((cols, 2 * HD), F32),
            VMEM((cols, 2 * HD), F32),
            VMEM((cols, 2 * HD), F32),
            VMEM((HD, keys), F32),
            VMEM((HD, keys), F32),
        ],
        compiler_params=pltpu.CompilerParams(vmem_limit_bytes=min(56 * 2**20, held + 8 * 2**20)),
        cost_estimate=pl.CostEstimate(
            flops=40 * keys * rows * width, bytes_accessed=4 * 2**20, transcendentals=0
        ),
        name="attention",
    )(idx, seq, *q_oc, *kvs)


def sum_kernel(idx_ref, own_ref, *rest, back):
    got_refs = rest[:back]
    part_refs = rest[back:back + PLANE]
    total = rest[back + PLANE]
    tok = part_refs[0].shape[0]
    place = idx_ref[0] % PLANE
    summed = own_ref[...]
    for got in got_refs:
        summed = summed + got[...].astype(F32)
    total[...] = summed
    for r in range(PLANE):
        part_refs[r][...] = total[pl.ds(pl.multiple_of((place ^ r) * tok, tok), tok), :].astype(BF16)


def wv_kernel(*refs, n_ctx):
    part_refs, hidden_refs, wv_ref = refs[:PLANE], refs[PLANE:2 * PLANE], refs[2 * PLANE]
    features = hidden_refs[0].shape[1]
    wv = jnp.zeros((HD, features), F32)
    for r in range(PLANE):
        cot_t = jnp.transpose(part_refs[r][...].astype(F32))[HD:2 * HD, :].astype(BF16)
        wv = wv + dot(cot_t, hidden_refs[r][...])
    wv = jnp.transpose(wv)
    rows = features // n_ctx
    if wv_ref.shape[2] == 2 * HD:
        for d in range(n_ctx):
            one = wv[d * rows:(d + 1) * rows]
            wv_ref[d] = jnp.concatenate([one[:rows // 2], one[rows // 2:]], axis=1).astype(BF16)
    else:
        for d in range(n_ctx):
            wv_ref[d] = wv[d * rows:(d + 1) * rows].astype(BF16)


def results_kernel(idx_ref, *refs):
    out_refs = refs[:PLANE]
    attn_ref, qg_ref = refs[PLANE:]
    place = idx_ref[0] % PLANE
    lanes = out_refs[0].shape[1] // 2
    for r in range(PLANE):
        at = pl.ds(pl.multiple_of((place ^ r) * lanes, lanes), lanes)
        attn_ref[:, at] = out_refs[r][:, 0:lanes]
        qg_ref[:, at] = out_refs[r][:, lanes:2 * lanes]


def finish_kernel(idx_ref, weight_ref, *rest):
    part_refs = rest[:PLANE]
    kg_ref, xg_ref, parts = rest[PLANE:]
    place = idx_ref[0] % PLANE
    for r in range(PLANE):
        parts[place ^ r] = part_refs[r][...]
    kg_ref[...] = jnp.concatenate([parts[g, :, 0:HD] for g in range(PLANE)], axis=1)
    value_cot = jnp.concatenate([parts[g, :, HD:2 * HD] for g in range(PLANE)], axis=1)
    xg_ref[...] = lax.dot_general(
        value_cot, weight_ref[...], (((1,), (1,)), ((), ())), preferred_element_type=F32
    ).astype(BF16)


def wv_sum_kernel(wv_ref, out_ref):
    n_ctx, depth, lanes = wv_ref.shape
    sums = []
    for g in range(PLANE):
        total = wv_ref[g].astype(F32)
        for d in range(g + PLANE, n_ctx, PLANE):
            total = total + wv_ref[d].astype(F32)
        sums.append(total)
    for side in range(lanes // HD):
        out_ref[side * depth:(side + 1) * depth, :] = jnp.concatenate(
            [total[:, side * HD:(side + 1) * HD] for total in sums], axis=1
        )


def shifted(x, by):
    n = lax.axis_size("ctx")
    return lax.ppermute(x, "ctx", [(i, i + by) for i in range(n) if 0 <= i + by < n])


def crossed(x, by):
    n = lax.axis_size("ctx")
    return lax.ppermute(x, "ctx", [(i, i ^ by) for i in range(n)])


def in_plane(x):
    n = lax.axis_size("ctx")
    planes = [list(range(i, i + PLANE)) for i in range(0, n, PLANE)]
    return lax.all_to_all(x, "ctx", 0, 0, axis_index_groups=planes, tiled=True)


def shards(
    queries, keys, hidden, value_weight, out_grad, new_logp, old_logp, rewards, group_ids, seq_lengths
):
    n_ctx = lax.axis_size("ctx")
    tok, width = queries.shape
    kv_width = keys.shape[1]
    features = hidden.shape[1]
    back = n_ctx // 2 // PLANE
    ctx = lax.axis_index("ctx").astype(jnp.int32)
    idx = ctx.reshape(1)
    lanes = width // PLANE
    plane_rows = PLANE * tok

    kv = pl.pallas_call(
        values_kernel,
        out_shape=[jax.ShapeDtypeStruct((tok, 2 * HD), BF16)] * PLANE,
        in_specs=[whole(SMEM)] + [whole(VMEM)] * 3,
        out_specs=[whole(VMEM)] * PLANE,
        scratch_shapes=[VMEM((PLANE, tok, 2 * HD), BF16)],
        **small("values"),
    )(idx, hidden, value_weight, keys)
    kv = list(kv)
    queries, kv[0] = lax.optimization_barrier((queries, kv[0]))
    q_oc = pl.pallas_call(
        queries_kernel,
        out_shape=[jax.ShapeDtypeStruct((tok, 2 * lanes), BF16)] * PLANE,
        in_specs=[whole(SMEM)] * 4 + [whole(VMEM)] * 4,
        out_specs=[whole(VMEM)] * PLANE,
        **small("queries"),
    )(idx, seq_lengths, group_ids, rewards, new_logp[None, :], old_logp[None, :], queries, out_grad)

    kv = [kv[0]] + [crossed(kv[r], r) for r in range(1, PLANE)]
    kv, q_oc = lax.optimization_barrier((kv, list(q_oc)))
    kv = pl.pallas_call(
        join_kernel,
        out_shape=jax.ShapeDtypeStruct((plane_rows, 2 * HD), BF16),
        in_specs=[whole(VMEM)] * PLANE,
        out_specs=whole(VMEM),
        **small("join"),
    )(*kv)
    kvs = [kv] + [shifted(kv, w * PLANE) for w in range(1, back + 1)]
    q_oc = [q_oc[0]] + [crossed(q_oc[r], r) for r in range(1, PLANE)]
    late_hidden, q_oc, hidden_c = lax.optimization_barrier((hidden, q_oc, crossed(hidden, 1)))
    hidden_y = crossed(late_hidden, 2)

    outs = attention(idx, seq_lengths, q_oc, kvs)
    hidden_y, outs = lax.optimization_barrier((hidden_y, list(outs)))
    hidden_cy = crossed(hidden_y, 1)
    res, own, backs = list(outs[:PLANE]), outs[PLANE], outs[PLANE + 1:]

    got = [shifted(backs[w - 1], -w * PLANE) for w in range(1, back + 1)]
    got, res[1] = lax.optimization_barrier((got, res[1]))
    res = [res[0]] + [crossed(res[r], r) for r in range(1, PLANE)]
    parts = pl.pallas_call(
        functools.partial(sum_kernel, back=back),
        out_shape=[jax.ShapeDtypeStruct((tok, 2 * HD), BF16)] * PLANE,
        in_specs=[whole(SMEM)] + [whole(VMEM)] * (1 + back),
        out_specs=[whole(VMEM)] * PLANE,
        scratch_shapes=[VMEM((plane_rows, 2 * HD), F32)],
        **small("sum"),
    )(idx, own, *got)
    own_parts = list(parts)
    parts = [parts[0]] + [crossed(parts[r], r) for r in range(1, PLANE)]
    rows = features // n_ctx
    packed = (rows // 2) % 8 == 0
    piece = (rows // 2, 2 * HD) if packed else (rows, HD)
    wv = pl.pallas_call(
        functools.partial(wv_kernel, n_ctx=n_ctx),
        out_shape=jax.ShapeDtypeStruct((n_ctx,) + piece, BF16),
        in_specs=[whole(VMEM)] * (2 * PLANE),
        out_specs=whole(VMEM),
        **small("wv"),
    )(*own_parts, hidden, hidden_c, hidden_y, hidden_cy)
    wv, parts[1], res = lax.optimization_barrier((wv, parts[1], res))
    wv = lax.all_to_all(wv, "ctx", 0, 0, tiled=True)
    attn, q_grad = pl.pallas_call(
        results_kernel,
        out_shape=[jax.ShapeDtypeStruct((tok, width), BF16)] * 2,
        in_specs=[whole(SMEM)] + [whole(VMEM)] * PLANE,
        out_specs=[whole(VMEM)] * 2,
        **small("results"),
    )(idx, *res)
    k_grad, x_grad = pl.pallas_call(
        finish_kernel,
        out_shape=[
            jax.ShapeDtypeStruct((tok, kv_width), BF16),
            jax.ShapeDtypeStruct((tok, features), BF16),
        ],
        in_specs=[whole(SMEM)] + [whole(VMEM)] * (1 + PLANE),
        out_specs=[whole(VMEM)] * 2,
        scratch_shapes=[VMEM((PLANE, tok, 2 * HD), BF16)],
        **small("finish"),
    )(idx, value_weight, *parts)

    wv_grad = pl.pallas_call(
        wv_sum_kernel,
        out_shape=jax.ShapeDtypeStruct((rows, kv_width), F32),
        in_specs=[whole(VMEM)],
        out_specs=whole(VMEM),
        **small("wv_sum"),
    )(wv)
    return (attn, q_grad, k_grad, x_grad, wv_grad)


def solution(mesh):
    rows = P(("groups", "ctx"), None)
    flat = P(("groups", "ctx"))
    placed = (rows, rows, rows, P(), rows, flat, flat, P("groups"), P("groups"), P("groups"))
    return jax.shard_map(
        shards, mesh=mesh, in_specs=placed, out_specs=(rows,) * 5, check_vma=False
    )
```

```python
import functools
import math

import jax
import jax.numpy as jnp
from jax import lax
from jax.experimental import pallas as pl
from jax.experimental.pallas import tpu as pltpu
from jax.sharding import PartitionSpec as P

HD = 64
PLANE = 4
SCALE = 1.0 / math.sqrt(HD)
BIG_NEGATIVE = -1e30
VMEM = pltpu.VMEM
SMEM = pltpu.SMEM
BF16 = jnp.bfloat16
F32 = jnp.float32


def dot(a, b):
    return lax.dot_general(a, b, (((1,), (0,)), ((), ())), preferred_element_type=F32)


def whole(space):
    return pl.BlockSpec(memory_space=space)


def small(name, mib=12):
    return dict(name=name, compiler_params=pltpu.CompilerParams(vmem_limit_bytes=mib * 2**20))


def token_weights(idx, tok, seq_ref, rew_ref, gid_ref, new_ref, old_ref):
    nseq = seq_ref.shape[0]
    pos = idx * tok + lax.broadcasted_iota(jnp.int32, (1, tok), 1)
    reward = jnp.zeros(pos.shape, F32)
    total = jnp.zeros(pos.shape, F32)
    count = jnp.ones(pos.shape, F32)
    begin = jnp.int32(0)
    for i in range(nseq):
        gsum = F32(0)
        gcount = F32(0)
        for j in range(nseq):
            same = gid_ref[j] == gid_ref[i]
            gsum = gsum + jnp.where(same, rew_ref[j], 0.0)
            gcount = gcount + jnp.where(same, 1.0, 0.0)
        here = pos >= begin
        reward = jnp.where(here, rew_ref[i], reward)
        total = jnp.where(here, gsum, total)
        count = jnp.where(here, gcount, count)
        begin = begin + seq_ref[i]
    return (total / count - reward) * jnp.exp(new_ref[...] - old_ref[...])


def values_kernel(idx_ref, hidden_ref, weight_ref, keys_ref, *rest):
    out_refs, parts = rest[:PLANE], rest[PLANE]
    place = idx_ref[0] % PLANE
    values = dot(hidden_ref[...], weight_ref[...]).astype(BF16)
    for g in range(PLANE):
        at = slice(g * HD, (g + 1) * HD)
        parts[g] = jnp.concatenate([keys_ref[:, at], values[:, at]], axis=1)
    for r in range(PLANE):
        out_refs[r][...] = parts[place ^ r]


def join_kernel(*refs):
    tok = refs[0].shape[0]
    for r in range(PLANE):
        refs[PLANE][r * tok:(r + 1) * tok, :] = refs[r][...]


def queries_kernel(
    idx_ref, seq_ref, gid_ref, rew_ref, new_ref, old_ref, q_ref, og_ref, *out_refs
):
    tok, width = q_ref.shape
    lanes = width // PLANE
    place = idx_ref[0] % PLANE
    weight = token_weights(idx_ref[0], tok, seq_ref, rew_ref, gid_ref, new_ref, old_ref)
    weight = jnp.transpose(jnp.broadcast_to(weight, (tok, tok)))[:, 0:1]
    for r in range(PLANE):
        at = pl.ds(pl.multiple_of((place ^ r) * lanes, lanes), lanes)
        out_refs[r][:, 0:lanes] = (q_ref[:, at].astype(F32) * SCALE).astype(BF16)
        out_refs[r][:, lanes:2 * lanes] = (og_ref[:, at].astype(F32) * weight).astype(BF16)


def twice(x):
    return jnp.concatenate([x, x], axis=1)


def first_of(position, seq_ref):
    start = position * 0
    begin = jnp.int32(0)
    for i in range(seq_ref.shape[0]):
        start = jnp.where(position >= begin, begin, start)
        begin = begin + seq_ref[i]
    return start


def head_pairs(per_pass, blk):
    return [
        (slice(2 * a * blk, (2 * a + 1) * blk), slice((2 * a + 1) * blk, (2 * a + 2) * blk))
        for a in range(per_pass // 2)
    ]


def lanes_of(h0, a, offset=0):
    return slice(offset + (h0 + 2 * a) * HD, offset + (h0 + 2 * a + 2) * HD)


def gather_queries(in_refs, place, q_in):
    tok = in_refs[0].shape[0]
    for r in range(PLANE):
        q_in[pl.ds(pl.multiple_of((place ^ r) * tok, tok), tok), :] = in_refs[r][...]


def key_blocks(kv_refs, place, tok, back):
    for w in range(back + 1):
        for r in range(PLANE):
            at = pl.ds(pl.multiple_of(((back - w) * PLANE + (place ^ r)) * tok, tok), tok)
            yield at, kv_refs[w][r * tok:(r + 1) * tok, :].astype(F32)


def send_back(acc, own_ref, back_refs, rows_all):
    back = len(back_refs)
    own_ref[...] = acc[:, back * rows_all:]
    for w in range(1, back + 1):
        back_refs[w - 1][...] = acc[:, (back - w) * rows_all:(back - w + 1) * rows_all].astype(BF16)


def forward_kernel(idx_ref, seq_ref, *rest, back, heads, per_pass):
    in_refs = rest[:PLANE]
    kv_refs = rest[PLANE:PLANE + back + 1]
    rest = rest[PLANE + back + 1:]
    out_refs = rest[:PLANE]
    own_ref = rest[PLANE]
    back_refs = rest[PLANE + 1:PLANE + 1 + back]
    probs, om, inner, q_in, res, k2t, v2, qm, ot, start, bias, score, o_acc, top, acc_v = rest[PLANE + 1 + back:]
    tok = in_refs[0].shape[0]
    rows_all = PLANE * tok
    blk = rows_all // 2
    width = heads * HD
    passes = heads // per_pass
    pairs = 2 * back + 1
    plane = idx_ref[0] // PLANE
    place = idx_ref[0] % PLANE
    base = (plane - back) * 2

    gather_queries(in_refs, place, q_in)
    lower = lax.broadcasted_iota(jnp.int32, (tok, 2 * HD), 1) < HD
    for at, part in key_blocks(kv_refs, place, tok, back):
        v2[at, 0:2 * HD] = jnp.where(lower, pltpu.roll(part, HD, 1), part).astype(BF16)
        key_t = jnp.transpose(part).astype(BF16)[:HD]
        k2t[:, at] = jnp.concatenate([key_t, key_t], axis=0)
    v2[:, 2 * HD:] = jnp.ones((v2.shape[0], 2 * HD), BF16)
    acc_v[...] = jnp.zeros_like(acc_v)
    left = lax.broadcasted_iota(jnp.int32, (blk, 2 * HD), 1) < HD
    pairs_at = head_pairs(per_pass, blk)

    def block(b, carry):
        pair_hi = plane * 2 + b
        first = pair_hi * blk
        start[...] = first_of(first + lax.broadcasted_iota(jnp.int32, (blk, 2 * HD), 0), seq_ref)
        start_hi = first_of(first + blk - 1, seq_ref)
        steps = pair_hi - first_of(first, seq_ref) // blk + 1
        q_rows = pl.ds(pl.multiple_of(b * blk, blk), blk)

        for h0 in range(0, heads, per_pass):
            kept = b * passes + h0 // per_pass
            for a, (even, odd) in enumerate(pairs_at):
                q2 = q_in[q_rows, lanes_of(h0, a)]
                qm[even, :] = jnp.where(left, q2, jnp.zeros_like(q2))
                qm[odd, :] = jnp.where(left, jnp.zeros_like(q2), q2)
            top[...] = jnp.full(top.shape, BIG_NEGATIVE, F32)
            o_acc[...] = jnp.zeros_like(o_acc)

            def scores(step, carry):
                pair = pair_hi - step
                cols_k = pl.ds(pl.multiple_of((pair - base) * blk, blk), blk)
                inside = (step > 0) & (pair * blk >= start_hi)

                def keep(at, s):
                    score[step, at, :] = s
                    top[at, :] = jnp.maximum(top[at, :], jnp.maximum(s[:, :2 * HD], s[:, 2 * HD:]))

                @pl.when(inside)
                def _():
                    k_t = k2t[:, cols_k]
                    for even, odd in pairs_at:
                        at = slice(even.start, odd.stop)
                        keep(at, dot(qm[at, :], k_t))

                @pl.when(jnp.logical_not(inside))
                def _():
                    k_t = k2t[:, cols_k]
                    key_pos = pair * blk + lax.broadcasted_iota(jnp.int32, (blk, blk), 1)
                    tok_pos = first + lax.broadcasted_iota(jnp.int32, (blk, blk), 0)
                    seen = (key_pos >= twice(start[...])) & (key_pos <= tok_pos)
                    bias[...] = jnp.where(seen, 0.0, BIG_NEGATIVE)
                    for even, odd in pairs_at:
                        s = dot(qm[even.start:odd.stop, :], k_t)
                        keep(even, s[:blk] + bias[...])
                        keep(odd, s[blk:] + bias[...])

                return carry

            lax.fori_loop(0, steps, scores, 0)
            top[...] = jnp.broadcast_to(jnp.max(top[...], axis=1, keepdims=True), top.shape)

            def outputs(step, carry):
                pair = pair_hi - step
                rows = pl.ds(pl.multiple_of((pair - base) * blk, blk), blk)
                vv = v2[rows, :]
                for even, odd in pairs_at:
                    at = slice(even.start, odd.stop)
                    eb = jnp.exp(score[step, at, :] - twice(top[at, :])).astype(BF16)
                    probs[kept * pairs + step, at, :] = eb
                    o_acc[at, :] = o_acc[at, :] + dot(eb, vv)
                return carry

            lax.fori_loop(0, steps, outputs, 0)
            for a, pair_at in enumerate(pairs_at):
                o2 = q_in[q_rows, lanes_of(h0, a, width)].astype(F32)
                out = []
                scaled = []
                for side, at in enumerate(pair_at):
                    inv = 1.0 / o_acc[at, 2 * HD:]
                    out.append(o_acc[at, 0:2 * HD] * inv)
                    mine = jnp.where(left if side == 0 else jnp.logical_not(left), o2, 0.0) * inv
                    inner[kept, at, :] = jnp.broadcast_to(
                        jnp.sum(mine * out[side], axis=1, keepdims=True), (blk, 2 * HD)
                    )
                    scaled.append(mine)
                    om[kept, at, :] = mine.astype(BF16)
                res[q_rows, lanes_of(h0, a)] = jnp.where(left, out[0], out[1]).astype(BF16)
                o2t = jnp.transpose(scaled[0] + scaled[1]).astype(BF16)
                ot[:, pair_at[0]] = o2t[:HD]
                ot[:, pair_at[1]] = o2t[HD:]

            def value_grad(step, carry):
                rows = pl.ds(pl.multiple_of((pair_hi - step - base) * blk, blk), blk)
                acc_v[:, rows] = acc_v[:, rows] + dot(ot[...], probs[kept * pairs + step])
                return carry

            lax.fori_loop(0, steps, value_grad, 0)
        return carry

    lax.fori_loop(0, 2, block, 0)
    send_back(acc_v, own_ref, back_refs, rows_all)
    for r in range(PLANE):
        out_refs[r][...] = res[pl.ds(pl.multiple_of((place ^ r) * tok, tok), tok), :]


def backward_kernel(idx_ref, seq_ref, *rest, back, heads, per_pass):
    in_refs = rest[:PLANE]
    kv_refs = rest[PLANE:PLANE + back + 1]
    probs, om, inner = rest[PLANE + back + 1:PLANE + back + 4]
    rest = rest[PLANE + back + 4:]
    out_refs = rest[:PLANE]
    own_ref = rest[PLANE]
    back_refs = rest[PLANE + 1:PLANE + 1 + back]
    q_in, res, k2, v2t, qt, dscore, q_acc, acc_k = rest[PLANE + 1 + back:]
    tok = in_refs[0].shape[0]
    rows_all = PLANE * tok
    blk = rows_all // 2
    passes = heads // per_pass
    pairs = 2 * back + 1
    plane = idx_ref[0] // PLANE
    place = idx_ref[0] % PLANE
    base = (plane - back) * 2

    gather_queries(in_refs, place, q_in)
    lower = lax.broadcasted_iota(jnp.int32, (tok, 2 * HD), 1) < HD
    for at, part in key_blocks(kv_refs, place, tok, back):
        k2[at, :] = jnp.where(lower, part, pltpu.roll(part, HD, 1)).astype(BF16)
        value_t = jnp.transpose(part).astype(BF16)[HD:]
        v2t[:, at] = jnp.concatenate([value_t, value_t], axis=0)
    acc_k[...] = jnp.zeros_like(acc_k)
    left = lax.broadcasted_iota(jnp.int32, (blk, 2 * HD), 1) < HD
    pairs_at = head_pairs(per_pass, blk)

    def block(b, carry):
        pair_hi = plane * 2 + b
        steps = pair_hi - first_of(pair_hi * blk, seq_ref) // blk + 1
        q_rows = pl.ds(pl.multiple_of(b * blk, blk), blk)

        for h0 in range(0, heads, per_pass):
            kept = b * passes + h0 // per_pass
            for a, (even, odd) in enumerate(pairs_at):
                q2t = jnp.transpose(q_in[q_rows, lanes_of(h0, a)].astype(F32)).astype(BF16)
                qt[:, even] = q2t[:HD]
                qt[:, odd] = q2t[HD:]
            q_acc[...] = jnp.zeros_like(q_acc)

            def gradients(step, carry):
                rows = pl.ds(pl.multiple_of((pair_hi - step - base) * blk, blk), blk)
                kk = k2[rows, :]
                v_t = v2t[:, rows]
                for even, odd in pairs_at:
                    at = slice(even.start, odd.stop)
                    dp = dot(om[kept, at, :], v_t)
                    e = probs[kept * pairs + step, at, :].astype(F32)
                    ds = (e * (dp - twice(inner[kept, at, :]))).astype(BF16)
                    dscore[at, :] = ds
                    q_acc[at, :] = q_acc[at, :] + dot(ds, kk)
                acc_k[:, rows] = acc_k[:, rows] + dot(qt[...], dscore[...])
                return carry

            lax.fori_loop(0, steps, gradients, 0)
            for a, (even, odd) in enumerate(pairs_at):
                qg = jnp.where(left, q_acc[even, :], q_acc[odd, :]) * SCALE
                res[q_rows, lanes_of(h0, a)] = qg.astype(BF16)
        return carry

    lax.fori_loop(0, 2, block, 0)
    send_back(acc_k, own_ref, back_refs, rows_all)
    for r in range(PLANE):
        out_refs[r][...] = res[pl.ds(pl.multiple_of((place ^ r) * tok, tok), tok), :]


def attention_sizes(q_oc, kvs):
    tok, width2 = q_oc[0].shape
    rows = PLANE * tok
    back = len(kvs) - 1
    heads = width2 // 2 // HD
    blk = rows // 2
    pairs = 2 * back + 1
    per_pass = heads
    while per_pass > 2 and pairs * blk * per_pass * blk * 4 > 12 * 2**20:
        per_pass //= 2
    return tok, width2, rows, back, heads, blk, pairs, per_pass


def kernel_params(name, held, flops):
    return dict(
        name=name,
        compiler_params=pltpu.CompilerParams(vmem_limit_bytes=min(60 * 2**20, held)),
        cost_estimate=pl.CostEstimate(flops=flops, bytes_accessed=2**20, transcendentals=0),
    )


def forward(idx, seq, q_oc, kvs):
    tok, width2, rows, back, heads, blk, pairs, per_pass = attention_sizes(q_oc, kvs)
    cols = per_pass * blk
    keys = rows * (back + 1)
    kept = 2 * heads // per_pass
    held = pairs * blk * cols * 4 + kept * pairs * blk * cols * 2 + 16 * 2**20
    return pl.pallas_call(
        functools.partial(forward_kernel, back=back, heads=heads, per_pass=per_pass),
        out_shape=(
            [jax.ShapeDtypeStruct((tok, width2 // 2), BF16)] * PLANE
            + [jax.ShapeDtypeStruct((HD, rows), F32)]
            + [jax.ShapeDtypeStruct((HD, rows), BF16)] * back
            + [
                jax.ShapeDtypeStruct((kept * pairs, cols, blk), BF16),
                jax.ShapeDtypeStruct((kept, cols, 2 * HD), BF16),
                jax.ShapeDtypeStruct((kept, cols, 2 * HD), F32),
            ]
        ),
        in_specs=[whole(SMEM)] * 2 + [whole(VMEM)] * (PLANE + len(kvs)),
        out_specs=[whole(VMEM)] * (PLANE + 1 + back + 3),
        scratch_shapes=[
            VMEM((rows, width2), BF16),
            VMEM((rows, width2 // 2), BF16),
            VMEM((2 * HD, keys), BF16),
            VMEM((keys, 4 * HD), BF16),
            VMEM((cols, 2 * HD), BF16),
            VMEM((HD, cols), BF16),
            VMEM((blk, 2 * HD), jnp.int32),
            VMEM((blk, blk), F32),
            VMEM((pairs, cols, blk), F32),
            VMEM((cols, 4 * HD), F32),
            VMEM((cols, 2 * HD), F32),
            VMEM((HD, keys), F32),
        ],
        **kernel_params("forward", held, 20 * keys * rows * width2 // 2),
    )(idx, seq, *q_oc, *kvs)


def backward(idx, seq, q_oc, kvs, probs, om, inner):
    tok, width2, rows, back, heads, blk, pairs, per_pass = attention_sizes(q_oc, kvs)
    cols = per_pass * blk
    keys = rows * (back + 1)
    held = probs.size * 2 + 16 * 2**20
    return pl.pallas_call(
        functools.partial(backward_kernel, back=back, heads=heads, per_pass=per_pass),
        out_shape=(
            [jax.ShapeDtypeStruct((tok, width2 // 2), BF16)] * PLANE
            + [jax.ShapeDtypeStruct((HD, rows), F32)]
            + [jax.ShapeDtypeStruct((HD, rows), BF16)] * back
        ),
        in_specs=[whole(SMEM)] * 2 + [whole(VMEM)] * (PLANE + len(kvs) + 3),
        out_specs=[whole(VMEM)] * (PLANE + 1 + back),
        scratch_shapes=[
            VMEM((rows, width2), BF16),
            VMEM((rows, width2 // 2), BF16),
            VMEM((keys, 2 * HD), BF16),
            VMEM((2 * HD, keys), BF16),
            VMEM((HD, cols), BF16),
            VMEM((cols, blk), BF16),
            VMEM((cols, 2 * HD), F32),
            VMEM((HD, keys), F32),
        ],
        **kernel_params("backward", held, keys * rows),
    )(idx, seq, *q_oc, *kvs, probs, om, inner)


def sum_kernel(idx_ref, own_ref, *rest, back):
    got_refs = rest[:back]
    cot_ref = rest[back]
    part_refs = rest[back + 1:back + 1 + PLANE]
    total = rest[back + 1 + PLANE]
    tok = part_refs[0].shape[1]
    place = idx_ref[0] % PLANE
    summed = own_ref[...]
    for got in got_refs:
        summed = summed + got[...].astype(F32)
    total[0:HD, :] = summed.astype(BF16)
    total[HD:2 * HD, :] = cot_ref[...]
    for r in range(PLANE):
        part_refs[r][...] = total[:, pl.ds(pl.multiple_of((place ^ r) * tok, tok), tok)]


def wv_kernel(idx_ref, own_ref, *refs, back, n_ctx):
    got_refs, hidden_refs = refs[:back], refs[back:back + PLANE]
    cot_ref, wv_ref = refs[back + PLANE:]
    tok, features = hidden_refs[0].shape
    place = idx_ref[0] % PLANE
    summed = own_ref[...]
    for got in got_refs:
        summed = summed + got[...].astype(F32)
    cot_ref[...] = summed.astype(BF16)
    wv = jnp.zeros((HD, features), F32)
    for r in range(PLANE):
        at = pl.ds(pl.multiple_of((place ^ r) * tok, tok), tok)
        wv = wv + dot(cot_ref[:, at], hidden_refs[r][...])
    wv = jnp.transpose(wv)
    rows = features // n_ctx
    if wv_ref.shape[2] == 2 * HD:
        for d in range(n_ctx):
            one = wv[d * rows:(d + 1) * rows]
            wv_ref[d] = jnp.concatenate([one[:rows // 2], one[rows // 2:]], axis=1).astype(BF16)
    else:
        for d in range(n_ctx):
            wv_ref[d] = wv[d * rows:(d + 1) * rows].astype(BF16)


def results_kernel(idx_ref, *refs):
    in_refs, out_refs = refs[:-2], refs[-2:]
    place = idx_ref[0] % PLANE
    lanes = in_refs[0].shape[1]
    for i, ref in enumerate(in_refs):
        at = pl.ds(pl.multiple_of((place ^ (i % PLANE)) * lanes, lanes), lanes)
        out_refs[i // PLANE][:, at] = ref[...]


def finish_kernel(idx_ref, weight_ref, *rest):
    part_refs = rest[:PLANE]
    kg_ref, xg_ref, parts = rest[PLANE:]
    place = idx_ref[0] % PLANE
    for r in range(PLANE):
        parts[place ^ r] = jnp.transpose(part_refs[r][...].astype(F32)).astype(BF16)
    kg_ref[...] = jnp.concatenate([parts[g, :, 0:HD] for g in range(PLANE)], axis=1)
    value_cot = jnp.concatenate([parts[g, :, HD:2 * HD] for g in range(PLANE)], axis=1)
    xg_ref[...] = lax.dot_general(
        value_cot, weight_ref[...], (((1,), (1,)), ((), ())), preferred_element_type=F32
    ).astype(BF16)


def wv_sum_kernel(wv_ref, out_ref):
    n_ctx, depth, lanes = wv_ref.shape
    sums = []
    for g in range(PLANE):
        total = wv_ref[g].astype(F32)
        for d in range(g + PLANE, n_ctx, PLANE):
            total = total + wv_ref[d].astype(F32)
        sums.append(total)
    for side in range(lanes // HD):
        out_ref[side * depth:(side + 1) * depth, :] = jnp.concatenate(
            [total[:, side * HD:(side + 1) * HD] for total in sums], axis=1
        )


def shifted(x, by):
    n = lax.axis_size("ctx")
    return lax.ppermute(x, "ctx", [(i, i + by) for i in range(n) if 0 <= i + by < n])


def crossed(x, by):
    n = lax.axis_size("ctx")
    return lax.ppermute(x, "ctx", [(i, i ^ by) for i in range(n)])


def in_plane(x):
    n = lax.axis_size("ctx")
    planes = [list(range(i, i + PLANE)) for i in range(0, n, PLANE)]
    return lax.all_to_all(x, "ctx", 0, 0, axis_index_groups=planes, tiled=True)


def shards(
    queries, keys, hidden, value_weight, out_grad, new_logp, old_logp, rewards, group_ids, seq_lengths
):
    n_ctx = lax.axis_size("ctx")
    tok, width = queries.shape
    kv_width = keys.shape[1]
    features = hidden.shape[1]
    back = n_ctx // 2 // PLANE
    ctx = lax.axis_index("ctx").astype(jnp.int32)
    idx = ctx.reshape(1)
    lanes = width // PLANE
    plane_rows = PLANE * tok

    q_oc = pl.pallas_call(
        queries_kernel,
        out_shape=[jax.ShapeDtypeStruct((tok, 2 * lanes), BF16)] * PLANE,
        in_specs=[whole(SMEM)] * 4 + [whole(VMEM)] * 4,
        out_specs=[whole(VMEM)] * PLANE,
        **small("queries"),
    )(idx, seq_lengths, group_ids, rewards, new_logp[None, :], old_logp[None, :], queries, out_grad)
    keys, q_oc = lax.optimization_barrier((keys, list(q_oc)))
    kv = pl.pallas_call(
        values_kernel,
        out_shape=[jax.ShapeDtypeStruct((tok, 2 * HD), BF16)] * PLANE,
        in_specs=[whole(SMEM)] + [whole(VMEM)] * 3,
        out_specs=[whole(VMEM)] * PLANE,
        scratch_shapes=[VMEM((PLANE, tok, 2 * HD), BF16)],
        **small("values"),
    )(idx, hidden, value_weight, keys)

    q_oc = [q_oc[0]] + [crossed(q_oc[r], r) for r in range(1, PLANE)]
    kv = [kv[0]] + [crossed(kv[r], r) for r in range(1, PLANE)]
    kv = pl.pallas_call(
        join_kernel,
        out_shape=jax.ShapeDtypeStruct((plane_rows, 2 * HD), BF16),
        in_specs=[whole(VMEM)] * PLANE,
        out_specs=whole(VMEM),
        **small("join"),
    )(*kv)
    kvs = [kv] + [shifted(kv, w * PLANE) for w in range(1, back + 1)]
    late_hidden, q_oc = lax.optimization_barrier((hidden, q_oc))
    hidden_y = crossed(late_hidden, 2)
    hidden_c = crossed(late_hidden, 1)

    outs = list(forward(idx, seq_lengths, q_oc, kvs))
    attn, own_v, backs_v = outs[:PLANE], outs[PLANE], outs[PLANE + 1:PLANE + 1 + back]
    probs, om, inner = outs[PLANE + 1 + back:]
    hidden_c, probs = lax.optimization_barrier((hidden_c, probs))
    got_v = [shifted(backs_v[w - 1], -w * PLANE) for w in range(1, back + 1)]
    attn = [attn[0], attn[1]] + [crossed(attn[r], r) for r in range(2, PLANE)]
    outs = list(backward(idx, seq_lengths, q_oc, kvs, probs, om, inner))
    outs, got_v, attn, hidden_y = lax.optimization_barrier((outs, got_v, attn, hidden_y))
    hidden_cy = crossed(hidden_y, 1)
    qg, own_k, backs_k = outs[:PLANE], outs[PLANE], outs[PLANE + 1:]
    got_k = [shifted(backs_k[w - 1], -w * PLANE) for w in range(1, back + 1)]
    rows = features // n_ctx
    packed = (rows // 2) % 8 == 0
    piece = (rows // 2, 2 * HD) if packed else (rows, HD)
    cot, wv = pl.pallas_call(
        functools.partial(wv_kernel, back=back, n_ctx=n_ctx),
        out_shape=[
            jax.ShapeDtypeStruct((HD, plane_rows), BF16),
            jax.ShapeDtypeStruct((n_ctx,) + piece, BF16),
        ],
        in_specs=[whole(SMEM)] + [whole(VMEM)] * (1 + back + PLANE),
        out_specs=[whole(VMEM)] * 2,
        **small("wv"),
    )(idx, own_v, *got_v, hidden, hidden_c, hidden_y, hidden_cy)
    wv, qg, attn[1] = lax.optimization_barrier((wv, qg, attn[1]))
    attn[1] = crossed(attn[1], 1)
    qg = [qg[0]] + [crossed(qg[r], r) for r in range(1, PLANE)]
    parts = pl.pallas_call(
        functools.partial(sum_kernel, back=back),
        out_shape=[jax.ShapeDtypeStruct((2 * HD, tok), BF16)] * PLANE,
        in_specs=[whole(SMEM)] + [whole(VMEM)] * (2 + back),
        out_specs=[whole(VMEM)] * PLANE,
        scratch_shapes=[VMEM((2 * HD, plane_rows), BF16)],
        **small("sum"),
    )(idx, own_k, *got_k, cot)
    parts = [parts[0]] + [crossed(parts[r], r) for r in range(1, PLANE)]
    wv = lax.all_to_all(wv, "ctx", 0, 0, tiled=True)
    attn, q_grad = pl.pallas_call(
        results_kernel,
        out_shape=[jax.ShapeDtypeStruct((tok, width), BF16)] * 2,
        in_specs=[whole(SMEM)] + [whole(VMEM)] * (2 * PLANE),
        out_specs=[whole(VMEM)] * 2,
        **small("results"),
    )(idx, *attn, *qg)
    k_grad, x_grad = pl.pallas_call(
        finish_kernel,
        out_shape=[
            jax.ShapeDtypeStruct((tok, kv_width), BF16),
            jax.ShapeDtypeStruct((tok, features), BF16),
        ],
        in_specs=[whole(SMEM)] + [whole(VMEM)] * (1 + PLANE),
        out_specs=[whole(VMEM)] * 2,
        scratch_shapes=[VMEM((PLANE, tok, 2 * HD), BF16)],
        **small("finish"),
    )(idx, value_weight, *parts)

    wv_grad = pl.pallas_call(
        wv_sum_kernel,
        out_shape=jax.ShapeDtypeStruct((rows, kv_width), F32),
        in_specs=[whole(VMEM)],
        out_specs=whole(VMEM),
        **small("wv_sum"),
    )(wv)
    return (attn, q_grad, k_grad, x_grad, wv_grad)


def solution(mesh):
    rows = P(("groups", "ctx"), None)
    flat = P(("groups", "ctx"))
    placed = (rows, rows, rows, P(), rows, flat, flat, P("groups"), P("groups"), P("groups"))
    return jax.shard_map(
        shards, mesh=mesh, in_specs=placed, out_specs=(rows,) * 5, check_vma=False
    )
```

```python
import functools
import math

import jax
import jax.numpy as jnp
from jax import lax
from jax.experimental import pallas as pl
from jax.experimental.pallas import tpu as pltpu
from jax.sharding import PartitionSpec as P

HD = 64
PLANE = 4
SCALE = 1.0 / math.sqrt(HD)
BIG_NEGATIVE = -1e30
VMEM = pltpu.VMEM
SMEM = pltpu.SMEM
BF16 = jnp.bfloat16
F32 = jnp.float32


def dot(a, b):
    return lax.dot_general(a, b, (((1,), (0,)), ((), ())), preferred_element_type=F32)


def whole(space):
    return pl.BlockSpec(memory_space=space)


def small(name, flops=10**6, mib=12):
    return dict(
        name=name,
        compiler_params=pltpu.CompilerParams(vmem_limit_bytes=mib * 2**20),
        cost_estimate=pl.CostEstimate(flops=flops, bytes_accessed=2**16, transcendentals=0),
    )


def token_weights(idx, tok, seq_ref, rew_ref, gid_ref, new_ref, old_ref):
    nseq = seq_ref.shape[0]
    pos = idx * tok + lax.broadcasted_iota(jnp.int32, (1, tok), 1)
    reward = jnp.zeros(pos.shape, F32)
    total = jnp.zeros(pos.shape, F32)
    count = jnp.ones(pos.shape, F32)
    begin = jnp.int32(0)
    for i in range(nseq):
        gsum = F32(0)
        gcount = F32(0)
        for j in range(nseq):
            same = gid_ref[j] == gid_ref[i]
            gsum = gsum + jnp.where(same, rew_ref[j], 0.0)
            gcount = gcount + jnp.where(same, 1.0, 0.0)
        here = pos >= begin
        reward = jnp.where(here, rew_ref[i], reward)
        total = jnp.where(here, gsum, total)
        count = jnp.where(here, gcount, count)
        begin = begin + seq_ref[i]
    return (total / count - reward) * jnp.exp(new_ref[...] - old_ref[...])


def prepare_kernel(
    idx_ref, seq_ref, gid_ref, rew_ref, new_ref, old_ref, hidden_hbm, weight_hbm, keys_hbm, q_hbm, og_hbm, *rest
):
    kv_refs, q_refs = rest[:PLANE], rest[PLANE:2 * PLANE]
    parts, hidden, weight, keys, q_in, og_in, sems = rest[2 * PLANE:]
    _, tok, lanes = q_in.shape
    place = idx_ref[0] % PLANE
    depth = hidden.shape[1] // PLANE
    value_copies = []
    query_copies = []
    for c in range(PLANE):
        at = pl.ds(c * depth, depth)
        value_copies.append((
            pltpu.make_async_copy(weight_hbm.at[at, :], weight.at[at, :], sems.at[0, c]),
            pltpu.make_async_copy(hidden_hbm.at[:, at], hidden.at[:, at], sems.at[1, c]),
        ))
        at = pl.ds(pl.multiple_of((place ^ c) * lanes, lanes), lanes)
        query_copies.append((
            pltpu.make_async_copy(q_hbm.at[:, at], q_in.at[c], sems.at[2, c]),
            pltpu.make_async_copy(og_hbm.at[:, at], og_in.at[c], sems.at[3, c]),
        ))
    key_copy = pltpu.make_async_copy(keys_hbm, keys, sems.at[4, 0])
    for pair in value_copies:
        for copy in pair:
            copy.start()
    key_copy.start()
    for pair in query_copies:
        for copy in pair:
            copy.start()
    token = token_weights(idx_ref[0], tok, seq_ref, rew_ref, gid_ref, new_ref, old_ref)
    token = jnp.transpose(jnp.broadcast_to(token, (tok, tok)))[:, 0:1]
    values = jnp.zeros((hidden.shape[0], weight.shape[1]), F32)
    for c, pair in enumerate(value_copies):
        for copy in pair:
            copy.wait()
        at = slice(c * depth, (c + 1) * depth)
        values = values + dot(hidden[:, at], weight[at, :])
    values = values.astype(BF16)
    key_copy.wait()
    for g in range(PLANE):
        at = slice(g * HD, (g + 1) * HD)
        parts[g] = jnp.concatenate([keys[:, at], values[:, at]], axis=1)
    for r, pair in enumerate(query_copies):
        kv_refs[r][...] = parts[place ^ r]
        for copy in pair:
            copy.wait()
        q_refs[r][:, 0:lanes] = (q_in[r].astype(F32) * SCALE).astype(BF16)
        q_refs[r][:, lanes:2 * lanes] = (og_in[r].astype(F32) * token).astype(BF16)


def join_kernel(*refs):
    tok = refs[0].shape[0]
    for r in range(PLANE):
        refs[PLANE][r * tok:(r + 1) * tok, :] = refs[r][...]


def twice(x):
    return jnp.concatenate([x, x], axis=1)


def first_of(position, seq_ref):
    start = position * 0
    begin = jnp.int32(0)
    for i in range(seq_ref.shape[0]):
        start = jnp.where(position >= begin, begin, start)
        begin = begin + seq_ref[i]
    return start


def head_pairs(per_pass, blk):
    return [
        (slice(2 * a * blk, (2 * a + 1) * blk), slice((2 * a + 1) * blk, (2 * a + 2) * blk))
        for a in range(per_pass // 2)
    ]


def lanes_of(h0, a, offset=0):
    return slice(offset + (h0 + 2 * a) * HD, offset + (h0 + 2 * a + 2) * HD)


def gather_queries(in_refs, place, q_in):
    tok = in_refs[0].shape[0]
    for r in range(PLANE):
        q_in[pl.ds(pl.multiple_of((place ^ r) * tok, tok), tok), :] = in_refs[r][...]


def key_blocks(kv_refs, place, tok, back):
    for w in range(back + 1):
        for r in range(PLANE):
            at = pl.ds(pl.multiple_of(((back - w) * PLANE + (place ^ r)) * tok, tok), tok)
            yield at, kv_refs[w][r * tok:(r + 1) * tok, :].astype(F32)


def send_back(acc, own_ref, back_refs, rows_all):
    back = len(back_refs)
    own_ref[...] = acc[:, back * rows_all:]
    for w in range(1, back + 1):
        back_refs[w - 1][...] = acc[:, (back - w) * rows_all:(back - w + 1) * rows_all].astype(BF16)


def forward_kernel(idx_ref, seq_ref, *rest, back, heads, per_pass):
    in_refs = rest[:PLANE]
    kv_refs = rest[PLANE:PLANE + back + 1]
    rest = rest[PLANE + back + 1:]
    out_refs = rest[:PLANE]
    own_ref = rest[PLANE]
    back_refs = rest[PLANE + 1:PLANE + 1 + back]
    probs, om, inner, q_in, res, k2t, v2, qm, ot, start, bias, score, o_acc, top, acc_v = rest[PLANE + 1 + back:]
    tok = in_refs[0].shape[0]
    rows_all = PLANE * tok
    blk = rows_all // 2
    width = heads * HD
    passes = heads // per_pass
    pairs = 2 * back + 1
    plane = idx_ref[0] // PLANE
    place = idx_ref[0] % PLANE
    base = (plane - back) * 2

    gather_queries(in_refs, place, q_in)
    lower = lax.broadcasted_iota(jnp.int32, (tok, 2 * HD), 1) < HD
    for at, part in key_blocks(kv_refs, place, tok, back):
        v2[at, 0:2 * HD] = jnp.where(lower, pltpu.roll(part, HD, 1), part).astype(BF16)
        key_t = jnp.transpose(part).astype(BF16)[:HD]
        k2t[:, at] = jnp.concatenate([key_t, key_t], axis=0)
    v2[:, 2 * HD:] = jnp.ones((v2.shape[0], 2 * HD), BF16)
    acc_v[...] = jnp.zeros_like(acc_v)
    left = lax.broadcasted_iota(jnp.int32, (blk, 2 * HD), 1) < HD
    pairs_at = head_pairs(per_pass, blk)

    def block(b, carry):
        pair_hi = plane * 2 + b
        first = pair_hi * blk
        start[...] = first_of(first + lax.broadcasted_iota(jnp.int32, (blk, 2 * HD), 0), seq_ref)
        start_hi = first_of(first + blk - 1, seq_ref)
        steps = pair_hi - first_of(first, seq_ref) // blk + 1
        q_rows = pl.ds(pl.multiple_of(b * blk, blk), blk)

        for h0 in range(0, heads, per_pass):
            kept = b * passes + h0 // per_pass
            for a, (even, odd) in enumerate(pairs_at):
                q2 = q_in[q_rows, lanes_of(h0, a)]
                qm[even, :] = jnp.where(left, q2, jnp.zeros_like(q2))
                qm[odd, :] = jnp.where(left, jnp.zeros_like(q2), q2)

            def scores(step, carry):
                pair = pair_hi - step
                cols_k = pl.ds(pl.multiple_of((pair - base) * blk, blk), blk)
                whole_first = isinstance(step, int)
                inside = pair * blk >= start_hi

                def keep(at, s):
                    score[step, at, :] = s
                    most = jnp.maximum(s[:, :2 * HD], s[:, 2 * HD:])
                    top[at, :] = most if whole_first else jnp.maximum(top[at, :], most)

                def all_seen():
                    k_t = k2t[:, cols_k]
                    for even, odd in pairs_at:
                        at = slice(even.start, odd.stop)
                        keep(at, dot(qm[at, :], k_t))

                def some_seen():
                    k_t = k2t[:, cols_k]
                    key_pos = pair * blk + lax.broadcasted_iota(jnp.int32, (blk, blk), 1)
                    tok_pos = first + lax.broadcasted_iota(jnp.int32, (blk, blk), 0)
                    seen = (key_pos >= twice(start[...])) & (key_pos <= tok_pos)
                    bias[...] = jnp.where(seen, 0.0, BIG_NEGATIVE)
                    for even, odd in pairs_at:
                        s = dot(qm[even.start:odd.stop, :], k_t)
                        keep(even, s[:blk] + bias[...])
                        keep(odd, s[blk:] + bias[...])

                if whole_first:
                    some_seen()
                else:
                    pl.when(inside)(all_seen)
                    pl.when(jnp.logical_not(inside))(some_seen)
                return carry

            scores(0, 0)
            lax.fori_loop(1, steps, scores, 0)
            top[...] = jnp.broadcast_to(jnp.max(top[...], axis=1, keepdims=True), top.shape)

            def outputs(step, carry):
                pair = pair_hi - step
                rows = pl.ds(pl.multiple_of((pair - base) * blk, blk), blk)
                vv = v2[rows, :]
                for even, odd in pairs_at:
                    at = slice(even.start, odd.stop)
                    eb = jnp.exp(score[step, at, :] - twice(top[at, :])).astype(BF16)
                    probs[kept * pairs + step, at, :] = eb
                    out = dot(eb, vv)
                    o_acc[at, :] = out if isinstance(step, int) else o_acc[at, :] + out
                return carry

            outputs(0, 0)
            lax.fori_loop(1, steps, outputs, 0)
            for a, pair_at in enumerate(pairs_at):
                o2 = q_in[q_rows, lanes_of(h0, a, width)].astype(F32)
                out = []
                scaled = []
                for side, at in enumerate(pair_at):
                    inv = 1.0 / o_acc[at, 2 * HD:]
                    out.append(o_acc[at, 0:2 * HD] * inv)
                    mine = jnp.where(left if side == 0 else jnp.logical_not(left), o2, 0.0) * inv
                    inner[kept, at, :] = jnp.broadcast_to(
                        jnp.sum(mine * out[side], axis=1, keepdims=True), (blk, 2 * HD)
                    )
                    scaled.append(mine)
                    om[kept, at, :] = mine.astype(BF16)
                res[q_rows, lanes_of(h0, a)] = jnp.where(left, out[0], out[1]).astype(BF16)
                o2t = jnp.transpose(scaled[0] + scaled[1]).astype(BF16)
                ot[:, pair_at[0]] = o2t[:HD]
                ot[:, pair_at[1]] = o2t[HD:]

            def value_grad(step, carry):
                rows = pl.ds(pl.multiple_of((pair_hi - step - base) * blk, blk), blk)
                acc_v[:, rows] = acc_v[:, rows] + dot(ot[...], probs[kept * pairs + step])
                return carry

            lax.fori_loop(0, steps, value_grad, 0)
        return carry

    lax.fori_loop(0, 2, block, 0)
    send_back(acc_v, own_ref, back_refs, rows_all)
    for r in range(PLANE):
        out_refs[r][...] = res[pl.ds(pl.multiple_of((place ^ r) * tok, tok), tok), :]


def backward_kernel(idx_ref, seq_ref, *rest, back, heads, per_pass):
    in_refs = rest[:PLANE]
    kv_refs = rest[PLANE:PLANE + back + 1]
    probs, om, inner = rest[PLANE + back + 1:PLANE + back + 4]
    rest = rest[PLANE + back + 4:]
    out_refs = rest[:PLANE]
    own_ref = rest[PLANE]
    back_refs = rest[PLANE + 1:PLANE + 1 + back]
    q_in, res, k2, v2t, qt, dscore, q_acc, acc_k = rest[PLANE + 1 + back:]
    tok = in_refs[0].shape[0]
    rows_all = PLANE * tok
    blk = rows_all // 2
    passes = heads // per_pass
    pairs = 2 * back + 1
    plane = idx_ref[0] // PLANE
    place = idx_ref[0] % PLANE
    base = (plane - back) * 2

    gather_queries(in_refs, place, q_in)
    lower = lax.broadcasted_iota(jnp.int32, (tok, 2 * HD), 1) < HD
    for at, part in key_blocks(kv_refs, place, tok, back):
        k2[at, :] = jnp.where(lower, part, pltpu.roll(part, HD, 1)).astype(BF16)
        value_t = jnp.transpose(part).astype(BF16)[HD:]
        v2t[:, at] = jnp.concatenate([value_t, value_t], axis=0)
    acc_k[...] = jnp.zeros_like(acc_k)
    left = lax.broadcasted_iota(jnp.int32, (blk, 2 * HD), 1) < HD
    pairs_at = head_pairs(per_pass, blk)

    def block(b, carry):
        pair_hi = plane * 2 + b
        steps = pair_hi - first_of(pair_hi * blk, seq_ref) // blk + 1
        q_rows = pl.ds(pl.multiple_of(b * blk, blk), blk)

        for h0 in range(0, heads, per_pass):
            kept = b * passes + h0 // per_pass
            for a, (even, odd) in enumerate(pairs_at):
                q2t = jnp.transpose(q_in[q_rows, lanes_of(h0, a)].astype(F32)).astype(BF16)
                qt[:, even] = q2t[:HD]
                qt[:, odd] = q2t[HD:]
            def gradients(step, carry):
                rows = pl.ds(pl.multiple_of((pair_hi - step - base) * blk, blk), blk)
                kk = k2[rows, :]
                v_t = v2t[:, rows]
                for even, odd in pairs_at:
                    at = slice(even.start, odd.stop)
                    dp = dot(om[kept, at, :], v_t)
                    e = probs[kept * pairs + step, at, :].astype(F32)
                    ds = (e * (dp - twice(inner[kept, at, :]))).astype(BF16)
                    dscore[at, :] = ds
                    dq = dot(ds, kk)
                    q_acc[at, :] = dq if isinstance(step, int) else q_acc[at, :] + dq
                acc_k[:, rows] = acc_k[:, rows] + dot(qt[...], dscore[...])
                return carry

            gradients(0, 0)
            lax.fori_loop(1, steps, gradients, 0)
            for a, (even, odd) in enumerate(pairs_at):
                qg = jnp.where(left, q_acc[even, :], q_acc[odd, :]) * SCALE
                res[q_rows, lanes_of(h0, a)] = qg.astype(BF16)
        return carry

    lax.fori_loop(0, 2, block, 0)
    send_back(acc_k, own_ref, back_refs, rows_all)
    for r in range(PLANE):
        out_refs[r][...] = res[pl.ds(pl.multiple_of((place ^ r) * tok, tok), tok), :]


def attention_sizes(q_oc, kvs):
    tok, width2 = q_oc[0].shape
    rows = PLANE * tok
    back = len(kvs) - 1
    heads = width2 // 2 // HD
    blk = rows // 2
    pairs = 2 * back + 1
    per_pass = heads
    while per_pass > 2 and pairs * blk * per_pass * blk * 4 > 12 * 2**20:
        per_pass //= 2
    return tok, width2, rows, back, heads, blk, pairs, per_pass


def kernel_params(name, held, flops):
    return dict(
        name=name,
        compiler_params=pltpu.CompilerParams(vmem_limit_bytes=min(60 * 2**20, held)),
        cost_estimate=pl.CostEstimate(flops=flops, bytes_accessed=2**20, transcendentals=0),
    )


def forward(idx, seq, q_oc, kvs):
    tok, width2, rows, back, heads, blk, pairs, per_pass = attention_sizes(q_oc, kvs)
    cols = per_pass * blk
    keys = rows * (back + 1)
    kept = 2 * heads // per_pass
    held = pairs * blk * cols * 4 + kept * pairs * blk * cols * 2 + 16 * 2**20
    return pl.pallas_call(
        functools.partial(forward_kernel, back=back, heads=heads, per_pass=per_pass),
        out_shape=(
            [jax.ShapeDtypeStruct((tok, width2 // 2), BF16)] * PLANE
            + [jax.ShapeDtypeStruct((HD, rows), F32)]
            + [jax.ShapeDtypeStruct((HD, rows), BF16)] * back
            + [
                jax.ShapeDtypeStruct((kept * pairs, cols, blk), BF16),
                jax.ShapeDtypeStruct((kept, cols, 2 * HD), BF16),
                jax.ShapeDtypeStruct((kept, cols, 2 * HD), F32),
            ]
        ),
        in_specs=[whole(SMEM)] * 2 + [whole(VMEM)] * (PLANE + len(kvs)),
        out_specs=[whole(VMEM)] * (PLANE + 1 + back + 3),
        scratch_shapes=[
            VMEM((rows, width2), BF16),
            VMEM((rows, width2 // 2), BF16),
            VMEM((2 * HD, keys), BF16),
            VMEM((keys, 4 * HD), BF16),
            VMEM((cols, 2 * HD), BF16),
            VMEM((HD, cols), BF16),
            VMEM((blk, 2 * HD), jnp.int32),
            VMEM((blk, blk), F32),
            VMEM((pairs, cols, blk), F32),
            VMEM((cols, 4 * HD), F32),
            VMEM((cols, 2 * HD), F32),
            VMEM((HD, keys), F32),
        ],
        **kernel_params("forward", held, 20 * keys * rows * width2 // 2),
    )(idx, seq, *q_oc, *kvs)


def backward(idx, seq, q_oc, kvs, probs, om, inner):
    tok, width2, rows, back, heads, blk, pairs, per_pass = attention_sizes(q_oc, kvs)
    cols = per_pass * blk
    keys = rows * (back + 1)
    held = probs.size * 2 + 16 * 2**20
    return pl.pallas_call(
        functools.partial(backward_kernel, back=back, heads=heads, per_pass=per_pass),
        out_shape=(
            [jax.ShapeDtypeStruct((tok, width2 // 2), BF16)] * PLANE
            + [jax.ShapeDtypeStruct((HD, rows), F32)]
            + [jax.ShapeDtypeStruct((HD, rows), BF16)] * back
        ),
        in_specs=[whole(SMEM)] * 2 + [whole(VMEM)] * (PLANE + len(kvs) + 3),
        out_specs=[whole(VMEM)] * (PLANE + 1 + back),
        scratch_shapes=[
            VMEM((rows, width2), BF16),
            VMEM((rows, width2 // 2), BF16),
            VMEM((keys, 2 * HD), BF16),
            VMEM((2 * HD, keys), BF16),
            VMEM((HD, cols), BF16),
            VMEM((cols, blk), BF16),
            VMEM((cols, 2 * HD), F32),
            VMEM((HD, keys), F32),
        ],
        **kernel_params("backward", held, keys * rows),
    )(idx, seq, *q_oc, *kvs, probs, om, inner)


def sum_kernel(idx_ref, own_ref, *rest, back):
    got_refs = rest[:back]
    cot_ref = rest[back]
    part_refs = rest[back + 1:back + 1 + PLANE]
    total = rest[back + 1 + PLANE]
    tok = part_refs[0].shape[1]
    place = idx_ref[0] % PLANE
    summed = own_ref[...]
    for got in got_refs:
        summed = summed + got[...].astype(F32)
    total[0:HD, :] = summed.astype(BF16)
    total[HD:2 * HD, :] = cot_ref[...]
    for r in range(PLANE):
        part_refs[r][...] = total[:, pl.ds(pl.multiple_of((place ^ r) * tok, tok), tok)]


def wv_kernel(idx_ref, own_ref, *refs, back, n_ctx):
    got_refs, hidden_refs = refs[:back], refs[back:back + PLANE]
    cot_ref, wv_ref = refs[back + PLANE:]
    tok, features = hidden_refs[0].shape
    place = idx_ref[0] % PLANE
    summed = own_ref[...]
    for got in got_refs:
        summed = summed + got[...].astype(F32)
    cot_ref[...] = summed.astype(BF16)
    wv = jnp.zeros((HD, features), F32)
    for r in range(PLANE):
        at = pl.ds(pl.multiple_of((place ^ r) * tok, tok), tok)
        wv = wv + dot(cot_ref[:, at], hidden_refs[r][...])
    wv = jnp.transpose(wv)
    rows = features // n_ctx
    if wv_ref.shape[2] == 2 * HD:
        for d in range(n_ctx):
            one = wv[d * rows:(d + 1) * rows]
            wv_ref[d] = jnp.concatenate([one[:rows // 2], one[rows // 2:]], axis=1).astype(BF16)
    else:
        for d in range(n_ctx):
            wv_ref[d] = wv[d * rows:(d + 1) * rows].astype(BF16)


def results_kernel(idx_ref, *refs):
    in_refs, out_refs = refs[:-2], refs[-2:]
    place = idx_ref[0] % PLANE
    lanes = in_refs[0].shape[1]
    for i, ref in enumerate(in_refs):
        at = pl.ds(pl.multiple_of((place ^ (i % PLANE)) * lanes, lanes), lanes)
        out_refs[i // PLANE][:, at] = ref[...]


def finish_kernel(idx_ref, weight_ref, *rest):
    part_refs = rest[:PLANE]
    kg_ref, xg_ref, parts = rest[PLANE:]
    place = idx_ref[0] % PLANE
    for r in range(PLANE):
        parts[place ^ r] = jnp.transpose(part_refs[r][...].astype(F32)).astype(BF16)
    kg_ref[...] = jnp.concatenate([parts[g, :, 0:HD] for g in range(PLANE)], axis=1)
    value_cot = jnp.concatenate([parts[g, :, HD:2 * HD] for g in range(PLANE)], axis=1)
    xg_ref[...] = lax.dot_general(
        value_cot, weight_ref[...], (((1,), (1,)), ((), ())), preferred_element_type=F32
    ).astype(BF16)


def wv_sum_kernel(wv_ref, out_ref):
    n_ctx, depth, lanes = wv_ref.shape
    sums = []
    for g in range(PLANE):
        total = wv_ref[g].astype(F32)
        for d in range(g + PLANE, n_ctx, PLANE):
            total = total + wv_ref[d].astype(F32)
        sums.append(total)
    for side in range(lanes // HD):
        out_ref[side * depth:(side + 1) * depth, :] = jnp.concatenate(
            [total[:, side * HD:(side + 1) * HD] for total in sums], axis=1
        )


def shifted(x, by):
    n = lax.axis_size("ctx")
    return lax.ppermute(x, "ctx", [(i, i + by) for i in range(n) if 0 <= i + by < n])


def crossed(x, by):
    n = lax.axis_size("ctx")
    return lax.ppermute(x, "ctx", [(i, i ^ by) for i in range(n)])


def in_plane(x):
    n = lax.axis_size("ctx")
    planes = [list(range(i, i + PLANE)) for i in range(0, n, PLANE)]
    return lax.all_to_all(x, "ctx", 0, 0, axis_index_groups=planes, tiled=True)


def shards(
    queries, keys, hidden, value_weight, out_grad, new_logp, old_logp, rewards, group_ids, seq_lengths
):
    n_ctx = lax.axis_size("ctx")
    tok, width = queries.shape
    kv_width = keys.shape[1]
    features = hidden.shape[1]
    back = n_ctx // 2 // PLANE
    ctx = lax.axis_index("ctx").astype(jnp.int32)
    idx = ctx.reshape(1)
    lanes = width // PLANE
    plane_rows = PLANE * tok

    outs = pl.pallas_call(
        prepare_kernel,
        out_shape=[jax.ShapeDtypeStruct((tok, 2 * HD), BF16)] * PLANE
        + [jax.ShapeDtypeStruct((tok, 2 * lanes), BF16)] * PLANE,
        in_specs=[whole(SMEM)] * 4 + [whole(VMEM)] * 2 + [whole(pltpu.HBM)] * 5,
        out_specs=[whole(VMEM)] * (2 * PLANE),
        scratch_shapes=[
            VMEM((PLANE, tok, 2 * HD), BF16),
            VMEM(hidden.shape, BF16),
            VMEM(value_weight.shape, BF16),
            VMEM(keys.shape, BF16),
            VMEM((PLANE, tok, lanes), BF16),
            VMEM((PLANE, tok, lanes), BF16),
            pltpu.SemaphoreType.DMA((5, PLANE)),
        ],
        **small("prepare", mib=60),
    )(
        idx, seq_lengths, group_ids, rewards, new_logp[None, :], old_logp[None, :],
        hidden, value_weight, keys, queries, out_grad,
    )
    kv, q_oc = list(outs[:PLANE]), list(outs[PLANE:])

    q_oc = [q_oc[0]] + [crossed(q_oc[r], r) for r in range(1, PLANE)]
    kv = [kv[0]] + [crossed(kv[r], r) for r in range(1, PLANE)]
    kv = pl.pallas_call(
        join_kernel,
        out_shape=jax.ShapeDtypeStruct((plane_rows, 2 * HD), BF16),
        in_specs=[whole(VMEM)] * PLANE,
        out_specs=whole(VMEM),
        **small("join", 10**10),
    )(*kv)
    kvs = [kv] + [shifted(kv, w * PLANE) for w in range(1, back + 1)]
    late_hidden, q_oc = lax.optimization_barrier((hidden, q_oc))
    hidden_y = crossed(late_hidden, 2)
    hidden_c = crossed(late_hidden, 1)

    outs = list(forward(idx, seq_lengths, q_oc, kvs))
    attn, own_v, backs_v = outs[:PLANE], outs[PLANE], outs[PLANE + 1:PLANE + 1 + back]
    probs, om, inner = outs[PLANE + 1 + back:]
    hidden_c, probs = lax.optimization_barrier((hidden_c, probs))
    got_v = [shifted(backs_v[w - 1], -w * PLANE) for w in range(1, back + 1)]
    attn = [attn[0], attn[1]] + [crossed(attn[r], r) for r in range(2, PLANE)]
    outs = list(backward(idx, seq_lengths, q_oc, kvs, probs, om, inner))
    outs, got_v, attn, hidden_y = lax.optimization_barrier((outs, got_v, attn, hidden_y))
    hidden_cy = crossed(hidden_y, 1)
    qg, own_k, backs_k = outs[:PLANE], outs[PLANE], outs[PLANE + 1:]
    got_k = [shifted(backs_k[w - 1], -w * PLANE) for w in range(1, back + 1)]
    rows = features // n_ctx
    packed = (rows // 2) % 8 == 0
    piece = (rows // 2, 2 * HD) if packed else (rows, HD)
    cot, wv = pl.pallas_call(
        functools.partial(wv_kernel, back=back, n_ctx=n_ctx),
        out_shape=[
            jax.ShapeDtypeStruct((HD, plane_rows), BF16),
            jax.ShapeDtypeStruct((n_ctx,) + piece, BF16),
        ],
        in_specs=[whole(SMEM)] + [whole(VMEM)] * (1 + back + PLANE),
        out_specs=[whole(VMEM)] * 2,
        **small("wv"),
    )(idx, own_v, *got_v, hidden, hidden_c, hidden_y, hidden_cy)
    wv, qg[1], attn[1] = lax.optimization_barrier((wv, qg[1], attn[1]))
    attn[1] = crossed(attn[1], 1)
    qg = [qg[0]] + [crossed(qg[r], r) for r in range(1, PLANE)]
    parts = pl.pallas_call(
        functools.partial(sum_kernel, back=back),
        out_shape=[jax.ShapeDtypeStruct((2 * HD, tok), BF16)] * PLANE,
        in_specs=[whole(SMEM)] + [whole(VMEM)] * (2 + back),
        out_specs=[whole(VMEM)] * PLANE,
        scratch_shapes=[VMEM((2 * HD, plane_rows), BF16)],
        **small("sum", 10**10),
    )(idx, own_k, *got_k, cot)
    parts = [parts[0]] + [crossed(parts[r], r) for r in range(1, PLANE)]
    wv = lax.all_to_all(wv, "ctx", 0, 0, tiled=True)
    attn, q_grad = pl.pallas_call(
        results_kernel,
        out_shape=[jax.ShapeDtypeStruct((tok, width), BF16)] * 2,
        in_specs=[whole(SMEM)] + [whole(VMEM)] * (2 * PLANE),
        out_specs=[whole(VMEM)] * 2,
        **small("results", 10**9),
    )(idx, *attn, *qg)
    k_grad, x_grad = pl.pallas_call(
        finish_kernel,
        out_shape=[
            jax.ShapeDtypeStruct((tok, kv_width), BF16),
            jax.ShapeDtypeStruct((tok, features), BF16),
        ],
        in_specs=[whole(SMEM)] + [whole(VMEM)] * (1 + PLANE),
        out_specs=[whole(VMEM)] * 2,
        scratch_shapes=[VMEM((PLANE, tok, 2 * HD), BF16)],
        **small("finish"),
    )(idx, value_weight, *parts)

    wv_grad = pl.pallas_call(
        wv_sum_kernel,
        out_shape=jax.ShapeDtypeStruct((rows, kv_width), F32),
        in_specs=[whole(VMEM)],
        out_specs=whole(VMEM),
        **small("wv_sum", 10**10),
    )(wv)
    return (attn, q_grad, k_grad, x_grad, wv_grad)


def solution(mesh):
    rows = P(("groups", "ctx"), None)
    flat = P(("groups", "ctx"))
    placed = (rows, rows, rows, P(), rows, flat, flat, P("groups"), P("groups"), P("groups"))
    return jax.shard_map(
        shards, mesh=mesh, in_specs=placed, out_specs=(rows,) * 5, check_vma=False
    )
```

```python
import functools
import math

import jax
import jax.numpy as jnp
from jax import lax
from jax.experimental import pallas as pl
from jax.experimental.pallas import tpu as pltpu
from jax.sharding import PartitionSpec as P

HD = 64
PLANE = 4
SCALE = 1.0 / math.sqrt(HD)
BIG_NEGATIVE = -1e30
VMEM = pltpu.VMEM
SMEM = pltpu.SMEM
BF16 = jnp.bfloat16
F32 = jnp.float32


def dot(a, b):
    return lax.dot_general(a, b, (((1,), (0,)), ((), ())), preferred_element_type=F32)


def whole(space):
    return pl.BlockSpec(memory_space=space)


def small(name, flops=10**6, mib=12):
    return dict(
        name=name,
        compiler_params=pltpu.CompilerParams(vmem_limit_bytes=mib * 2**20),
        cost_estimate=pl.CostEstimate(flops=flops, bytes_accessed=2**16, transcendentals=0),
    )


def token_weights(idx, tok, seq_ref, rew_ref, gid_ref, new_ref, old_ref):
    nseq = seq_ref.shape[0]
    pos = idx * tok + lax.broadcasted_iota(jnp.int32, (1, tok), 1)
    reward = jnp.zeros(pos.shape, F32)
    total = jnp.zeros(pos.shape, F32)
    count = jnp.ones(pos.shape, F32)
    begin = jnp.int32(0)
    for i in range(nseq):
        gsum = F32(0)
        gcount = F32(0)
        for j in range(nseq):
            same = gid_ref[j] == gid_ref[i]
            gsum = gsum + jnp.where(same, rew_ref[j], 0.0)
            gcount = gcount + jnp.where(same, 1.0, 0.0)
        here = pos >= begin
        reward = jnp.where(here, rew_ref[i], reward)
        total = jnp.where(here, gsum, total)
        count = jnp.where(here, gcount, count)
        begin = begin + seq_ref[i]
    return (total / count - reward) * jnp.exp(new_ref[...] - old_ref[...])


def prepare_kernel(
    idx_ref, seq_ref, gid_ref, rew_ref, new_ref, old_ref, hidden_hbm, weight_hbm, keys_hbm, q_hbm, og_hbm, *rest
):
    kv_refs, q_refs = rest[:PLANE], rest[PLANE:2 * PLANE]
    parts, hidden, weight, keys, q_in, og_in, sems = rest[2 * PLANE:]
    _, tok, lanes = q_in.shape
    place = idx_ref[0] % PLANE
    depth = hidden.shape[1] // PLANE
    value_copies = []
    query_copies = []
    for c in range(PLANE):
        at = pl.ds(c * depth, depth)
        value_copies.append((
            pltpu.make_async_copy(weight_hbm.at[at, :], weight.at[at, :], sems.at[0, c]),
            pltpu.make_async_copy(hidden_hbm.at[:, at], hidden.at[:, at], sems.at[1, c]),
        ))
        at = pl.ds(pl.multiple_of((place ^ c) * lanes, lanes), lanes)
        query_copies.append((
            pltpu.make_async_copy(q_hbm.at[:, at], q_in.at[c], sems.at[2, c]),
            pltpu.make_async_copy(og_hbm.at[:, at], og_in.at[c], sems.at[3, c]),
        ))
    key_copy = pltpu.make_async_copy(keys_hbm, keys, sems.at[4, 0])
    for pair in value_copies:
        for copy in pair:
            copy.start()
    key_copy.start()
    for pair in query_copies:
        for copy in pair:
            copy.start()
    token = token_weights(idx_ref[0], tok, seq_ref, rew_ref, gid_ref, new_ref, old_ref)
    token = jnp.transpose(jnp.broadcast_to(token, (tok, tok)))[:, 0:1]
    values = jnp.zeros((hidden.shape[0], weight.shape[1]), F32)
    for c, pair in enumerate(value_copies):
        for copy in pair:
            copy.wait()
        at = slice(c * depth, (c + 1) * depth)
        values = values + dot(hidden[:, at], weight[at, :])
    values = values.astype(BF16)
    key_copy.wait()
    for g in range(PLANE):
        at = slice(g * HD, (g + 1) * HD)
        parts[g] = jnp.concatenate([keys[:, at], values[:, at]], axis=1)
    for r, pair in enumerate(query_copies):
        kv_refs[r][...] = parts[place ^ r]
        for copy in pair:
            copy.wait()
        q_refs[r][:, 0:lanes] = (q_in[r].astype(F32) * SCALE).astype(BF16)
        q_refs[r][:, lanes:2 * lanes] = (og_in[r].astype(F32) * token).astype(BF16)


def join_kernel(*refs):
    tok = refs[0].shape[0]
    for r in range(PLANE):
        refs[PLANE][r * tok:(r + 1) * tok, :] = refs[r][...]


def twice(x):
    return jnp.concatenate([x, x], axis=1)


def first_of(position, seq_ref):
    start = position * 0
    begin = jnp.int32(0)
    for i in range(seq_ref.shape[0]):
        start = jnp.where(position >= begin, begin, start)
        begin = begin + seq_ref[i]
    return start


def head_pairs(per_pass, blk):
    return [
        (slice(2 * a * blk, (2 * a + 1) * blk), slice((2 * a + 1) * blk, (2 * a + 2) * blk))
        for a in range(per_pass // 2)
    ]


def lanes_of(h0, a, offset=0):
    return slice(offset + (h0 + 2 * a) * HD, offset + (h0 + 2 * a + 2) * HD)


def gather_queries(in_refs, place, q_in):
    tok = in_refs[0].shape[0]
    for r in range(PLANE):
        q_in[pl.ds(pl.multiple_of((place ^ r) * tok, tok), tok), :] = in_refs[r][...]


def key_blocks(kv_refs, place, tok, back):
    for w in range(back + 1):
        for r in range(PLANE):
            at = pl.ds(pl.multiple_of(((back - w) * PLANE + (place ^ r)) * tok, tok), tok)
            yield at, kv_refs[w][r * tok:(r + 1) * tok, :].astype(F32)


def send_back(acc, own_ref, back_refs, rows_all):
    back = len(back_refs)
    own_ref[...] = acc[:, back * rows_all:]
    for w in range(1, back + 1):
        back_refs[w - 1][...] = acc[:, (back - w) * rows_all:(back - w + 1) * rows_all].astype(BF16)


def forward_kernel(idx_ref, seq_ref, *rest, back, heads, per_pass):
    in_refs = rest[:PLANE]
    kv_refs = rest[PLANE:PLANE + back + 1]
    rest = rest[PLANE + back + 1:]
    out_refs = rest[:PLANE]
    own_ref = rest[PLANE]
    back_refs = rest[PLANE + 1:PLANE + 1 + back]
    probs, om, inner, q_in, res, k2t, v2, qm, ot, start, bias, score, o_acc, top, acc_v = rest[PLANE + 1 + back:]
    tok = in_refs[0].shape[0]
    rows_all = PLANE * tok
    blk = rows_all // 2
    width = heads * HD
    passes = heads // per_pass
    pairs = 2 * back + 1
    plane = idx_ref[0] // PLANE
    place = idx_ref[0] % PLANE
    base = (plane - back) * 2

    gather_queries(in_refs, place, q_in)
    lower = lax.broadcasted_iota(jnp.int32, (tok, 2 * HD), 1) < HD
    for at, part in key_blocks(kv_refs, place, tok, back):
        v2[at, 0:2 * HD] = jnp.where(lower, pltpu.roll(part, HD, 1), part).astype(BF16)
        key_t = jnp.transpose(part).astype(BF16)[:HD]
        k2t[:, at] = jnp.concatenate([key_t, key_t], axis=0)
    v2[:, 2 * HD:] = jnp.ones((v2.shape[0], 2 * HD), BF16)
    acc_v[...] = jnp.zeros_like(acc_v)
    left = lax.broadcasted_iota(jnp.int32, (blk, 2 * HD), 1) < HD
    pairs_at = head_pairs(per_pass, blk)

    def block(b, carry):
        pair_hi = plane * 2 + b
        first = pair_hi * blk
        start[...] = first_of(first + lax.broadcasted_iota(jnp.int32, (blk, 2 * HD), 0), seq_ref)
        start_hi = first_of(first + blk - 1, seq_ref)
        steps = pair_hi - first_of(first, seq_ref) // blk + 1
        q_rows = pl.ds(pl.multiple_of(b * blk, blk), blk)

        for h0 in range(0, heads, per_pass):
            kept = b * passes + h0 // per_pass
            for a, (even, odd) in enumerate(pairs_at):
                q2 = q_in[q_rows, lanes_of(h0, a)]
                qm[even, :] = jnp.where(left, q2, jnp.zeros_like(q2))
                qm[odd, :] = jnp.where(left, jnp.zeros_like(q2), q2)

            def scores(step, carry):
                pair = pair_hi - step
                cols_k = pl.ds(pl.multiple_of((pair - base) * blk, blk), blk)
                whole_first = isinstance(step, int)
                inside = pair * blk >= start_hi

                def keep(at, s):
                    score[step, at, :] = s
                    most = jnp.maximum(s[:, :2 * HD], s[:, 2 * HD:])
                    top[at, :] = most if whole_first else jnp.maximum(top[at, :], most)

                def all_seen():
                    k_t = k2t[:, cols_k]
                    for even, odd in pairs_at:
                        at = slice(even.start, odd.stop)
                        keep(at, dot(qm[at, :], k_t))

                def some_seen():
                    k_t = k2t[:, cols_k]
                    key_pos = pair * blk + lax.broadcasted_iota(jnp.int32, (blk, blk), 1)
                    tok_pos = first + lax.broadcasted_iota(jnp.int32, (blk, blk), 0)
                    seen = (key_pos >= twice(start[...])) & (key_pos <= tok_pos)
                    bias[...] = jnp.where(seen, 0.0, BIG_NEGATIVE)
                    for even, odd in pairs_at:
                        s = dot(qm[even.start:odd.stop, :], k_t)
                        keep(even, s[:blk] + bias[...])
                        keep(odd, s[blk:] + bias[...])

                if whole_first:
                    some_seen()
                else:
                    pl.when(inside)(all_seen)
                    pl.when(jnp.logical_not(inside))(some_seen)
                return carry

            scores(0, 0)
            lax.fori_loop(1, steps, scores, 0)
            top[...] = jnp.broadcast_to(jnp.max(top[...], axis=1, keepdims=True), top.shape)

            def outputs(step, carry):
                pair = pair_hi - step
                rows = pl.ds(pl.multiple_of((pair - base) * blk, blk), blk)
                vv = v2[rows, :]
                for even, odd in pairs_at:
                    at = slice(even.start, odd.stop)
                    eb = jnp.exp(score[step, at, :] - twice(top[at, :])).astype(BF16)
                    probs[kept * pairs + step, at, :] = eb
                    out = dot(eb, vv)
                    o_acc[at, :] = out if isinstance(step, int) else o_acc[at, :] + out
                return carry

            outputs(0, 0)
            lax.fori_loop(1, steps, outputs, 0)
            for a, pair_at in enumerate(pairs_at):
                o2 = q_in[q_rows, lanes_of(h0, a, width)].astype(F32)
                out = []
                scaled = []
                for side, at in enumerate(pair_at):
                    inv = 1.0 / o_acc[at, 2 * HD:]
                    out.append(o_acc[at, 0:2 * HD] * inv)
                    mine = jnp.where(left if side == 0 else jnp.logical_not(left), o2, 0.0) * inv
                    inner[kept, at, :] = jnp.broadcast_to(
                        jnp.sum(mine * out[side], axis=1, keepdims=True), (blk, 2 * HD)
                    )
                    scaled.append(mine)
                    om[kept, at, :] = mine.astype(BF16)
                res[q_rows, lanes_of(h0, a)] = jnp.where(left, out[0], out[1]).astype(BF16)
                o2t = jnp.transpose(scaled[0] + scaled[1]).astype(BF16)
                ot[:, pair_at[0]] = o2t[:HD]
                ot[:, pair_at[1]] = o2t[HD:]

            def value_grad(step, carry):
                rows = pl.ds(pl.multiple_of((pair_hi - step - base) * blk, blk), blk)
                acc_v[:, rows] = acc_v[:, rows] + dot(ot[...], probs[kept * pairs + step])
                return carry

            lax.fori_loop(0, steps, value_grad, 0)
        return carry

    lax.fori_loop(0, 2, block, 0)
    send_back(acc_v, own_ref, back_refs, rows_all)
    for r in range(PLANE):
        out_refs[r][...] = res[pl.ds(pl.multiple_of((place ^ r) * tok, tok), tok), :]


def backward_kernel(idx_ref, seq_ref, *rest, back, heads, per_pass):
    in_refs = rest[:PLANE]
    kv_refs = rest[PLANE:PLANE + back + 1]
    probs, om, inner, attn_ref = rest[PLANE + back + 1:PLANE + back + 5]
    rest = rest[PLANE + back + 5:]
    out_refs = rest[:PLANE]
    own_ref = rest[PLANE]
    back_refs = rest[PLANE + 1:PLANE + 1 + back]
    q_in, res, k2, v2t, qt, dscore, q_acc, acc_k = rest[PLANE + 1 + back:]
    tok = in_refs[0].shape[0]
    rows_all = PLANE * tok
    blk = rows_all // 2
    passes = heads // per_pass
    pairs = 2 * back + 1
    plane = idx_ref[0] // PLANE
    place = idx_ref[0] % PLANE
    base = (plane - back) * 2

    gather_queries(in_refs, place, q_in)
    lower = lax.broadcasted_iota(jnp.int32, (tok, 2 * HD), 1) < HD
    for at, part in key_blocks(kv_refs, place, tok, back):
        k2[at, :] = jnp.where(lower, part, pltpu.roll(part, HD, 1)).astype(BF16)
        value_t = jnp.transpose(part).astype(BF16)[HD:]
        v2t[:, at] = jnp.concatenate([value_t, value_t], axis=0)
    acc_k[...] = jnp.zeros_like(acc_k)
    left = lax.broadcasted_iota(jnp.int32, (blk, 2 * HD), 1) < HD
    pairs_at = head_pairs(per_pass, blk)

    def block(b, carry):
        pair_hi = plane * 2 + b
        steps = pair_hi - first_of(pair_hi * blk, seq_ref) // blk + 1
        q_rows = pl.ds(pl.multiple_of(b * blk, blk), blk)

        for h0 in range(0, heads, per_pass):
            kept = b * passes + h0 // per_pass
            for a, (even, odd) in enumerate(pairs_at):
                q2t = jnp.transpose(q_in[q_rows, lanes_of(h0, a)].astype(F32)).astype(BF16)
                qt[:, even] = q2t[:HD]
                qt[:, odd] = q2t[HD:]
            def gradients(step, carry):
                rows = pl.ds(pl.multiple_of((pair_hi - step - base) * blk, blk), blk)
                kk = k2[rows, :]
                v_t = v2t[:, rows]
                for even, odd in pairs_at:
                    at = slice(even.start, odd.stop)
                    dp = dot(om[kept, at, :], v_t)
                    e = probs[kept * pairs + step, at, :].astype(F32)
                    ds = (e * (dp - twice(inner[kept, at, :]))).astype(BF16)
                    dscore[at, :] = ds
                    dq = dot(ds, kk)
                    q_acc[at, :] = dq if isinstance(step, int) else q_acc[at, :] + dq
                acc_k[:, rows] = acc_k[:, rows] + dot(qt[...], dscore[...])
                return carry

            gradients(0, 0)
            lax.fori_loop(1, steps, gradients, 0)
            for a, (even, odd) in enumerate(pairs_at):
                qg = jnp.where(left, q_acc[even, :], q_acc[odd, :]) * SCALE
                res[q_rows, lanes_of(h0, a)] = qg.astype(BF16)
        return carry

    lax.fori_loop(0, 2, block, 0)
    send_back(acc_k, own_ref, back_refs, rows_all)
    for r in range(PLANE):
        mine = res[pl.ds(pl.multiple_of((place ^ r) * tok, tok), tok), :]
        if r == 1:
            mine = jnp.concatenate([attn_ref[...], mine], axis=1)
        out_refs[r][...] = mine


def attention_sizes(q_oc, kvs):
    tok, width2 = q_oc[0].shape
    rows = PLANE * tok
    back = len(kvs) - 1
    heads = width2 // 2 // HD
    blk = rows // 2
    pairs = 2 * back + 1
    per_pass = heads
    while per_pass > 2 and pairs * blk * per_pass * blk * 4 > 12 * 2**20:
        per_pass //= 2
    return tok, width2, rows, back, heads, blk, pairs, per_pass


def kernel_params(name, held, flops):
    return dict(
        name=name,
        compiler_params=pltpu.CompilerParams(vmem_limit_bytes=min(60 * 2**20, held)),
        cost_estimate=pl.CostEstimate(flops=flops, bytes_accessed=2**20, transcendentals=0),
    )


def forward(idx, seq, q_oc, kvs):
    tok, width2, rows, back, heads, blk, pairs, per_pass = attention_sizes(q_oc, kvs)
    cols = per_pass * blk
    keys = rows * (back + 1)
    kept = 2 * heads // per_pass
    held = pairs * blk * cols * 4 + kept * pairs * blk * cols * 2 + 16 * 2**20
    return pl.pallas_call(
        functools.partial(forward_kernel, back=back, heads=heads, per_pass=per_pass),
        out_shape=(
            [jax.ShapeDtypeStruct((tok, width2 // 2), BF16)] * PLANE
            + [jax.ShapeDtypeStruct((HD, rows), F32)]
            + [jax.ShapeDtypeStruct((HD, rows), BF16)] * back
            + [
                jax.ShapeDtypeStruct((kept * pairs, cols, blk), BF16),
                jax.ShapeDtypeStruct((kept, cols, 2 * HD), BF16),
                jax.ShapeDtypeStruct((kept, cols, 2 * HD), F32),
            ]
        ),
        in_specs=[whole(SMEM)] * 2 + [whole(VMEM)] * (PLANE + len(kvs)),
        out_specs=[whole(VMEM)] * (PLANE + 1 + back + 3),
        scratch_shapes=[
            VMEM((rows, width2), BF16),
            VMEM((rows, width2 // 2), BF16),
            VMEM((2 * HD, keys), BF16),
            VMEM((keys, 4 * HD), BF16),
            VMEM((cols, 2 * HD), BF16),
            VMEM((HD, cols), BF16),
            VMEM((blk, 2 * HD), jnp.int32),
            VMEM((blk, blk), F32),
            VMEM((pairs, cols, blk), F32),
            VMEM((cols, 4 * HD), F32),
            VMEM((cols, 2 * HD), F32),
            VMEM((HD, keys), F32),
        ],
        **kernel_params("forward", held, 20 * keys * rows * width2 // 2),
    )(idx, seq, *q_oc, *kvs)


def backward(idx, seq, q_oc, kvs, probs, om, inner, attn):
    tok, width2, rows, back, heads, blk, pairs, per_pass = attention_sizes(q_oc, kvs)
    cols = per_pass * blk
    keys = rows * (back + 1)
    held = probs.size * 2 + 16 * 2**20
    return pl.pallas_call(
        functools.partial(backward_kernel, back=back, heads=heads, per_pass=per_pass),
        out_shape=(
            [jax.ShapeDtypeStruct((tok, width2 if r == 1 else width2 // 2), BF16) for r in range(PLANE)]
            + [jax.ShapeDtypeStruct((HD, rows), F32)]
            + [jax.ShapeDtypeStruct((HD, rows), BF16)] * back
        ),
        in_specs=[whole(SMEM)] * 2 + [whole(VMEM)] * (PLANE + len(kvs) + 4),
        out_specs=[whole(VMEM)] * (PLANE + 1 + back),
        scratch_shapes=[
            VMEM((rows, width2), BF16),
            VMEM((rows, width2 // 2), BF16),
            VMEM((keys, 2 * HD), BF16),
            VMEM((2 * HD, keys), BF16),
            VMEM((HD, cols), BF16),
            VMEM((cols, blk), BF16),
            VMEM((cols, 2 * HD), F32),
            VMEM((HD, keys), F32),
        ],
        **kernel_params("backward", held, keys * rows),
    )(idx, seq, *q_oc, *kvs, probs, om, inner, attn)


def sum_kernel(idx_ref, own_ref, *rest, back):
    got_refs = rest[:back]
    cot_ref = rest[back]
    part_refs = rest[back + 1:back + 1 + PLANE]
    total = rest[back + 1 + PLANE]
    tok = part_refs[0].shape[1]
    place = idx_ref[0] % PLANE
    summed = own_ref[...]
    for got in got_refs:
        summed = summed + got[...].astype(F32)
    total[0:HD, :] = summed.astype(BF16)
    total[HD:2 * HD, :] = cot_ref[...]
    for r in range(PLANE):
        part_refs[r][...] = total[:, pl.ds(pl.multiple_of((place ^ r) * tok, tok), tok)]


def wv_kernel(idx_ref, own_ref, *refs, back, n_ctx):
    got_refs, hidden_refs = refs[:back], refs[back:back + PLANE]
    cot_ref, wv_ref = refs[back + PLANE:]
    tok, features = hidden_refs[0].shape
    place = idx_ref[0] % PLANE
    summed = own_ref[...]
    for got in got_refs:
        summed = summed + got[...].astype(F32)
    cot_ref[...] = summed.astype(BF16)
    wv = jnp.zeros((HD, features), F32)
    for r in range(PLANE):
        at = pl.ds(pl.multiple_of((place ^ r) * tok, tok), tok)
        wv = wv + dot(cot_ref[:, at], hidden_refs[r][...])
    wv = jnp.transpose(wv)
    rows = features // n_ctx
    if wv_ref.shape[2] == 2 * HD:
        for d in range(n_ctx):
            one = wv[d * rows:(d + 1) * rows]
            wv_ref[d] = jnp.concatenate([one[:rows // 2], one[rows // 2:]], axis=1).astype(BF16)
    else:
        for d in range(n_ctx):
            wv_ref[d] = wv[d * rows:(d + 1) * rows].astype(BF16)


def results_kernel(idx_ref, *refs):
    in_refs, out_refs = refs[:-2], refs[-2:]
    place = idx_ref[0] % PLANE
    lanes = in_refs[0].shape[1]
    for i, ref in enumerate(in_refs):
        r = i % PLANE
        at = pl.ds(pl.multiple_of((place ^ r) * lanes, lanes), lanes)
        mine = ref[...]
        if r == 1:
            mine = mine[:, (i // PLANE) * lanes:(i // PLANE + 1) * lanes]
        out_refs[i // PLANE][:, at] = mine


def finish_kernel(idx_ref, weight_ref, *rest):
    part_refs = rest[:PLANE]
    kg_ref, xg_ref, parts = rest[PLANE:]
    place = idx_ref[0] % PLANE
    for r in range(PLANE):
        parts[place ^ r] = jnp.transpose(part_refs[r][...].astype(F32)).astype(BF16)
    kg_ref[...] = jnp.concatenate([parts[g, :, 0:HD] for g in range(PLANE)], axis=1)
    value_cot = jnp.concatenate([parts[g, :, HD:2 * HD] for g in range(PLANE)], axis=1)
    xg_ref[...] = lax.dot_general(
        value_cot, weight_ref[...], (((1,), (1,)), ((), ())), preferred_element_type=F32
    ).astype(BF16)


def wv_sum_kernel(wv_ref, out_ref):
    n_ctx, depth, lanes = wv_ref.shape
    sums = []
    for g in range(PLANE):
        total = wv_ref[g].astype(F32)
        for d in range(g + PLANE, n_ctx, PLANE):
            total = total + wv_ref[d].astype(F32)
        sums.append(total)
    for side in range(lanes // HD):
        out_ref[side * depth:(side + 1) * depth, :] = jnp.concatenate(
            [total[:, side * HD:(side + 1) * HD] for total in sums], axis=1
        )


def shifted(x, by):
    n = lax.axis_size("ctx")
    return lax.ppermute(x, "ctx", [(i, i + by) for i in range(n) if 0 <= i + by < n])


def crossed(x, by):
    n = lax.axis_size("ctx")
    return lax.ppermute(x, "ctx", [(i, i ^ by) for i in range(n)])


def in_plane(x):
    n = lax.axis_size("ctx")
    planes = [list(range(i, i + PLANE)) for i in range(0, n, PLANE)]
    return lax.all_to_all(x, "ctx", 0, 0, axis_index_groups=planes, tiled=True)


def shards(
    queries, keys, hidden, value_weight, out_grad, new_logp, old_logp, rewards, group_ids, seq_lengths
):
    n_ctx = lax.axis_size("ctx")
    tok, width = queries.shape
    kv_width = keys.shape[1]
    features = hidden.shape[1]
    back = n_ctx // 2 // PLANE
    ctx = lax.axis_index("ctx").astype(jnp.int32)
    idx = ctx.reshape(1)
    lanes = width // PLANE
    plane_rows = PLANE * tok

    outs = pl.pallas_call(
        prepare_kernel,
        out_shape=[jax.ShapeDtypeStruct((tok, 2 * HD), BF16)] * PLANE
        + [jax.ShapeDtypeStruct((tok, 2 * lanes), BF16)] * PLANE,
        in_specs=[whole(SMEM)] * 4 + [whole(VMEM)] * 2 + [whole(pltpu.HBM)] * 5,
        out_specs=[whole(VMEM)] * (2 * PLANE),
        scratch_shapes=[
            VMEM((PLANE, tok, 2 * HD), BF16),
            VMEM(hidden.shape, BF16),
            VMEM(value_weight.shape, BF16),
            VMEM(keys.shape, BF16),
            VMEM((PLANE, tok, lanes), BF16),
            VMEM((PLANE, tok, lanes), BF16),
            pltpu.SemaphoreType.DMA((5, PLANE)),
        ],
        **small("prepare", mib=60),
    )(
        idx, seq_lengths, group_ids, rewards, new_logp[None, :], old_logp[None, :],
        hidden, value_weight, keys, queries, out_grad,
    )
    kv, q_oc = list(outs[:PLANE]), list(outs[PLANE:])

    q_oc = [q_oc[0]] + [crossed(q_oc[r], r) for r in range(1, PLANE)]
    kv = [kv[0]] + [crossed(kv[r], r) for r in range(1, PLANE)]
    kv = pl.pallas_call(
        join_kernel,
        out_shape=jax.ShapeDtypeStruct((plane_rows, 2 * HD), BF16),
        in_specs=[whole(VMEM)] * PLANE,
        out_specs=whole(VMEM),
        **small("join", 10**10),
    )(*kv)
    kvs = [kv] + [shifted(kv, w * PLANE) for w in range(1, back + 1)]
    late_hidden, q_oc[1] = lax.optimization_barrier((hidden, q_oc[1]))
    hidden_c = crossed(late_hidden, 1)
    late_hidden, q_oc, hidden_c = lax.optimization_barrier((hidden, q_oc, hidden_c))
    hidden_y = crossed(late_hidden, 2)

    outs = list(forward(idx, seq_lengths, q_oc, kvs))
    attn, own_v, backs_v = outs[:PLANE], outs[PLANE], outs[PLANE + 1:PLANE + 1 + back]
    probs, om, inner = outs[PLANE + 1 + back:]
    got_v = [shifted(backs_v[w - 1], -w * PLANE) for w in range(1, back + 1)]
    attn = [attn[0], attn[1]] + [crossed(attn[r], r) for r in range(2, PLANE)]
    outs = list(backward(idx, seq_lengths, q_oc, kvs, probs, om, inner, attn[1]))
    outs, got_v, attn, hidden_y = lax.optimization_barrier((outs, got_v, attn, hidden_y))
    hidden_cy = crossed(hidden_y, 1)
    qg, own_k, backs_k = outs[:PLANE], outs[PLANE], outs[PLANE + 1:]
    got_k = [shifted(backs_k[w - 1], -w * PLANE) for w in range(1, back + 1)]
    rows = features // n_ctx
    packed = (rows // 2) % 8 == 0
    piece = (rows // 2, 2 * HD) if packed else (rows, HD)
    cot, wv = pl.pallas_call(
        functools.partial(wv_kernel, back=back, n_ctx=n_ctx),
        out_shape=[
            jax.ShapeDtypeStruct((HD, plane_rows), BF16),
            jax.ShapeDtypeStruct((n_ctx,) + piece, BF16),
        ],
        in_specs=[whole(SMEM)] + [whole(VMEM)] * (1 + back + PLANE),
        out_specs=[whole(VMEM)] * 2,
        **small("wv"),
    )(idx, own_v, *got_v, hidden, hidden_c, hidden_y, hidden_cy)
    wv, qg[1] = lax.optimization_barrier((wv, qg[1]))
    qg = [qg[0]] + [crossed(qg[r], r) for r in range(1, PLANE)]
    attn[1] = qg[1]
    parts = pl.pallas_call(
        functools.partial(sum_kernel, back=back),
        out_shape=[jax.ShapeDtypeStruct((2 * HD, tok), BF16)] * PLANE,
        in_specs=[whole(SMEM)] + [whole(VMEM)] * (2 + back),
        out_specs=[whole(VMEM)] * PLANE,
        scratch_shapes=[VMEM((2 * HD, plane_rows), BF16)],
        **small("sum", 10**10),
    )(idx, own_k, *got_k, cot)
    attn, q_grad = pl.pallas_call(
        results_kernel,
        out_shape=[jax.ShapeDtypeStruct((tok, width), BF16)] * 2,
        in_specs=[whole(SMEM)] + [whole(VMEM)] * (2 * PLANE),
        out_specs=[whole(VMEM)] * 2,
        **small("results", 10**9),
    )(idx, *attn, *qg)
    parts, attn, q_grad = lax.optimization_barrier((list(parts), attn, q_grad))
    parts = [parts[0]] + [crossed(parts[r], r) for r in range(1, PLANE)]
    wv = lax.all_to_all(wv, "ctx", 0, 0, tiled=True)
    k_grad, x_grad = pl.pallas_call(
        finish_kernel,
        out_shape=[
            jax.ShapeDtypeStruct((tok, kv_width), BF16),
            jax.ShapeDtypeStruct((tok, features), BF16),
        ],
        in_specs=[whole(SMEM)] + [whole(VMEM)] * (1 + PLANE),
        out_specs=[whole(VMEM)] * 2,
        scratch_shapes=[VMEM((PLANE, tok, 2 * HD), BF16)],
        **small("finish"),
    )(idx, value_weight, *parts)

    wv_grad = pl.pallas_call(
        wv_sum_kernel,
        out_shape=jax.ShapeDtypeStruct((rows, kv_width), F32),
        in_specs=[whole(VMEM)],
        out_specs=whole(VMEM),
        **small("wv_sum", 10**10),
    )(wv)
    return (attn, q_grad, k_grad, x_grad, wv_grad)


def solution(mesh):
    rows = P(("groups", "ctx"), None)
    flat = P(("groups", "ctx"))
    placed = (rows, rows, rows, P(), rows, flat, flat, P("groups"), P("groups"), P("groups"))
    return jax.shard_map(
        shards, mesh=mesh, in_specs=placed, out_specs=(rows,) * 5, check_vma=False
    )
```

```python
import functools
import math

import jax
import jax.numpy as jnp
from jax import lax
from jax.experimental import pallas as pl
from jax.experimental.pallas import tpu as pltpu
from jax.sharding import PartitionSpec as P

HD = 64
PLANE = 4
SCALE = 1.0 / math.sqrt(HD)
BIG_NEGATIVE = -1e30
VMEM = pltpu.VMEM
SMEM = pltpu.SMEM
BF16 = jnp.bfloat16
F32 = jnp.float32


def dot(a, b):
    return lax.dot_general(a, b, (((1,), (0,)), ((), ())), preferred_element_type=F32)


def whole(space):
    return pl.BlockSpec(memory_space=space)


def small(name, flops=10**6, mib=12):
    return dict(
        name=name,
        compiler_params=pltpu.CompilerParams(vmem_limit_bytes=mib * 2**20),
        cost_estimate=pl.CostEstimate(flops=flops, bytes_accessed=2**16, transcendentals=0),
    )


def token_weights(idx, tok, seq_ref, rew_ref, gid_ref, new_ref, old_ref):
    nseq = seq_ref.shape[0]
    pos = idx * tok + lax.broadcasted_iota(jnp.int32, (1, tok), 1)
    reward = jnp.zeros(pos.shape, F32)
    total = jnp.zeros(pos.shape, F32)
    count = jnp.ones(pos.shape, F32)
    begin = jnp.int32(0)
    for i in range(nseq):
        gsum = F32(0)
        gcount = F32(0)
        for j in range(nseq):
            same = gid_ref[j] == gid_ref[i]
            gsum = gsum + jnp.where(same, rew_ref[j], 0.0)
            gcount = gcount + jnp.where(same, 1.0, 0.0)
        here = pos >= begin
        reward = jnp.where(here, rew_ref[i], reward)
        total = jnp.where(here, gsum, total)
        count = jnp.where(here, gcount, count)
        begin = begin + seq_ref[i]
    return (total / count - reward) * jnp.exp(new_ref[...] - old_ref[...])


def prepare_kernel(
    idx_ref, seq_ref, gid_ref, rew_ref, new_ref, old_ref, hidden_hbm, weight_hbm, keys_hbm, q_hbm, og_hbm, *rest
):
    kv_refs, q_refs = rest[:PLANE], rest[PLANE:2 * PLANE]
    parts, hidden, weight, keys, q_in, og_in, q_out, sems = rest[2 * PLANE:]
    _, tok, lanes = q_in.shape
    place = idx_ref[0] % PLANE
    depth = hidden.shape[1] // PLANE
    value_copies = []
    query_copies = []
    for c in range(PLANE):
        at = pl.ds(c * depth, depth)
        value_copies.append((
            pltpu.make_async_copy(weight_hbm.at[at, :], weight.at[at, :], sems.at[0, c]),
            pltpu.make_async_copy(hidden_hbm.at[:, at], hidden.at[:, at], sems.at[1, c]),
        ))
        at = pl.ds(pl.multiple_of((place ^ c) * lanes, lanes), lanes)
        query_copies.append((
            pltpu.make_async_copy(q_hbm.at[:, at], q_in.at[c], sems.at[2, c]),
            pltpu.make_async_copy(og_hbm.at[:, at], og_in.at[c], sems.at[3, c]),
        ))
    key_copy = pltpu.make_async_copy(keys_hbm, keys, sems.at[4, 0])
    for pair in value_copies:
        for copy in pair:
            copy.start()
    key_copy.start()
    for pair in query_copies:
        for copy in pair:
            copy.start()
    token = token_weights(idx_ref[0], tok, seq_ref, rew_ref, gid_ref, new_ref, old_ref)
    token = jnp.transpose(jnp.broadcast_to(token, (tok, tok)))[:, 0:1]
    values = jnp.zeros((hidden.shape[0], weight.shape[1]), F32)
    for c, pair in enumerate(value_copies):
        for copy in pair:
            copy.wait()
        at = slice(c * depth, (c + 1) * depth)
        values = values + dot(hidden[:, at], weight[at, :])
    values = values.astype(BF16)
    key_copy.wait()
    for g in range(PLANE):
        at = slice(g * HD, (g + 1) * HD)
        parts[g] = jnp.concatenate([keys[:, at], values[:, at]], axis=1)
    results = [pltpu.make_async_copy(parts.at[place ^ r], kv_refs[r], sems.at[5, r]) for r in range(PLANE)]
    for copy in results:
        copy.start()
    for r, pair in enumerate(query_copies):
        for copy in pair:
            copy.wait()
        q_out[r, :, 0:lanes] = (q_in[r].astype(F32) * SCALE).astype(BF16)
        q_out[r, :, lanes:2 * lanes] = (og_in[r].astype(F32) * token).astype(BF16)
        results.append(pltpu.make_async_copy(q_out.at[r], q_refs[r], sems.at[6, r]))
        results[-1].start()
    for copy in results:
        copy.wait()


def join_kernel(*refs):
    tok = refs[0].shape[0]
    for r in range(PLANE):
        refs[PLANE][r * tok:(r + 1) * tok, :] = refs[r][...]


def twice(x):
    return jnp.concatenate([x, x], axis=1)


def first_of(position, seq_ref):
    start = position * 0
    begin = jnp.int32(0)
    for i in range(seq_ref.shape[0]):
        start = jnp.where(position >= begin, begin, start)
        begin = begin + seq_ref[i]
    return start


def in_twos(steps, begin, two, one):
    def body(i, carry):
        two(2 * i)
        return carry

    lax.fori_loop(begin, steps // 2, body, 0)
    pl.when(steps % 2 == 1)(lambda: one(steps - 1))


def head_pairs(per_pass, blk):
    return [
        (slice(2 * a * blk, (2 * a + 1) * blk), slice((2 * a + 1) * blk, (2 * a + 2) * blk))
        for a in range(per_pass // 2)
    ]


def lanes_of(h0, a, offset=0):
    return slice(offset + (h0 + 2 * a) * HD, offset + (h0 + 2 * a + 2) * HD)


def gather_queries(in_refs, place, q_in):
    tok = in_refs[0].shape[0]
    for r in range(PLANE):
        q_in[pl.ds(pl.multiple_of((place ^ r) * tok, tok), tok), :] = in_refs[r][...]


def key_blocks(kv_refs, place, tok, back):
    for w in range(back + 1):
        for r in range(PLANE):
            at = pl.ds(pl.multiple_of(((back - w) * PLANE + (place ^ r)) * tok, tok), tok)
            yield at, kv_refs[w][r * tok:(r + 1) * tok, :].astype(F32)


def send_back(acc, own_ref, back_refs, rows_all):
    back = len(back_refs)
    own_ref[...] = acc[:, back * rows_all:]
    for w in range(1, back + 1):
        back_refs[w - 1][...] = acc[:, (back - w) * rows_all:(back - w + 1) * rows_all].astype(BF16)


def forward_kernel(idx_ref, seq_ref, *rest, back, heads, per_pass):
    in_refs = rest[:PLANE]
    kv_refs = rest[PLANE:PLANE + back + 1]
    rest = rest[PLANE + back + 1:]
    out_refs = rest[:PLANE]
    own_ref = rest[PLANE]
    back_refs = rest[PLANE + 1:PLANE + 1 + back]
    probs, om, inner, q_in, res, k2t, v2, qm, ot, start, bias, score, o_acc, top, acc_v = rest[PLANE + 1 + back:]
    tok = in_refs[0].shape[0]
    rows_all = PLANE * tok
    blk = rows_all // 2
    width = heads * HD
    passes = heads // per_pass
    pairs = 2 * back + 1
    plane = idx_ref[0] // PLANE
    place = idx_ref[0] % PLANE
    base = (plane - back) * 2

    gather_queries(in_refs, place, q_in)
    lower = lax.broadcasted_iota(jnp.int32, (tok, 2 * HD), 1) < HD
    for at, part in key_blocks(kv_refs, place, tok, back):
        v2[at, 0:2 * HD] = jnp.where(lower, pltpu.roll(part, HD, 1), part).astype(BF16)
        key_t = jnp.transpose(part).astype(BF16)[:HD]
        k2t[:, at] = jnp.concatenate([key_t, key_t], axis=0)
    v2[:, 2 * HD:] = jnp.ones((v2.shape[0], 2 * HD), BF16)
    acc_v[...] = jnp.zeros_like(acc_v)
    left = lax.broadcasted_iota(jnp.int32, (blk, 2 * HD), 1) < HD
    pairs_at = head_pairs(per_pass, blk)

    def block(b, carry):
        pair_hi = plane * 2 + b
        first = pair_hi * blk
        start[...] = first_of(first + lax.broadcasted_iota(jnp.int32, (blk, 2 * HD), 0), seq_ref)
        start_hi = first_of(first + blk - 1, seq_ref)
        steps = jnp.maximum(pair_hi - first_of(first, seq_ref) // blk + 1, 2)
        q_rows = pl.ds(pl.multiple_of(b * blk, blk), blk)

        for h0 in range(0, heads, per_pass):
            kept = b * passes + h0 // per_pass
            for a, (even, odd) in enumerate(pairs_at):
                q2 = q_in[q_rows, lanes_of(h0, a)]
                qm[even, :] = jnp.where(left, q2, jnp.zeros_like(q2))
                qm[odd, :] = jnp.where(left, jnp.zeros_like(q2), q2)

            def scores(step, count, first_time=False, edges=True):
                k_t = [
                    k2t[:, pl.ds(pl.multiple_of((pair_hi - step - c - base) * blk, blk), blk)] for c in range(count)
                ]
                if edges:
                    for c in range(count):
                        key_pos = (pair_hi - step - c) * blk + lax.broadcasted_iota(jnp.int32, (blk, blk), 1)
                        tok_pos = first + lax.broadcasted_iota(jnp.int32, (blk, blk), 0)
                        seen = (key_pos >= twice(start[...])) & (key_pos <= tok_pos)
                        bias[c] = jnp.where(seen, 0.0, BIG_NEGATIVE)
                for even, odd in pairs_at:
                    at = slice(even.start, odd.stop)
                    most = None if first_time else top[at, :]
                    for c in range(count):
                        s = dot(qm[at, :], k_t[c])
                        if edges:
                            s = s + jnp.concatenate([bias[c], bias[c]], axis=0)
                        score[step + c, at, :] = s
                        one = jnp.maximum(s[:, :2 * HD], s[:, 2 * HD:])
                        most = one if most is None else jnp.maximum(most, one)
                    top[at, :] = most

            def outputs(step, count, first_time=False):
                vv = v2[pl.ds(pl.multiple_of((pair_hi - step - count + 1 - base) * blk, blk), count * blk), :]
                for even, odd in pairs_at:
                    at = slice(even.start, odd.stop)
                    most = twice(top[at, :])
                    ebs = []
                    for c in reversed(range(count)):
                        eb = jnp.exp(score[step + c, at, :] - most).astype(BF16)
                        probs[kept * pairs + step + c, at, :] = eb
                        ebs.append(eb)
                    out = dot(jnp.concatenate(ebs, axis=1), vv)
                    o_acc[at, :] = out if first_time else o_acc[at, :] + out

            def value_grad(step, count):
                for c in range(count):
                    rows = pl.ds(pl.multiple_of((pair_hi - step - c - base) * blk, blk), blk)
                    acc_v[:, rows] = acc_v[:, rows] + dot(ot[...], probs[kept * pairs + step + c])

            def more_scores(step):
                inside = (pair_hi - step - 1) * blk >= start_hi
                pl.when(inside)(functools.partial(scores, step, 2, edges=False))
                pl.when(jnp.logical_not(inside))(functools.partial(scores, step, 2))

            scores(0, 2, first_time=True)
            in_twos(steps, 1, more_scores, functools.partial(scores, count=1))
            top[...] = jnp.broadcast_to(jnp.max(top[...], axis=1, keepdims=True), top.shape)
            outputs(0, 2, first_time=True)
            in_twos(steps, 1, functools.partial(outputs, count=2), functools.partial(outputs, count=1))
            for a, pair_at in enumerate(pairs_at):
                o2 = q_in[q_rows, lanes_of(h0, a, width)].astype(F32)
                out = []
                scaled = []
                for side, at in enumerate(pair_at):
                    inv = 1.0 / o_acc[at, 2 * HD:]
                    out.append(o_acc[at, 0:2 * HD] * inv)
                    mine = jnp.where(left if side == 0 else jnp.logical_not(left), o2, 0.0) * inv
                    inner[kept, at, :] = jnp.broadcast_to(
                        jnp.sum(mine * out[side], axis=1, keepdims=True), (blk, 2 * HD)
                    )
                    scaled.append(mine)
                    om[kept, at, :] = mine.astype(BF16)
                res[q_rows, lanes_of(h0, a)] = jnp.where(left, out[0], out[1]).astype(BF16)
                o2t = jnp.transpose(scaled[0] + scaled[1]).astype(BF16)
                ot[:, pair_at[0]] = o2t[:HD]
                ot[:, pair_at[1]] = o2t[HD:]

            in_twos(steps, 0, functools.partial(value_grad, count=2), functools.partial(value_grad, count=1))
        return carry

    lax.fori_loop(0, 2, block, 0)
    send_back(acc_v, own_ref, back_refs, rows_all)
    for r in range(PLANE):
        out_refs[r][...] = res[pl.ds(pl.multiple_of((place ^ r) * tok, tok), tok), :]


def backward_kernel(idx_ref, seq_ref, *rest, back, heads, per_pass):
    in_refs = rest[:PLANE]
    kv_refs = rest[PLANE:PLANE + back + 1]
    probs, om, inner, attn_ref = rest[PLANE + back + 1:PLANE + back + 5]
    rest = rest[PLANE + back + 5:]
    out_refs = rest[:PLANE]
    own_ref = rest[PLANE]
    back_refs = rest[PLANE + 1:PLANE + 1 + back]
    q_in, res, k2, v2t, qt, dscore, q_acc, acc_k = rest[PLANE + 1 + back:]
    tok = in_refs[0].shape[0]
    rows_all = PLANE * tok
    blk = rows_all // 2
    passes = heads // per_pass
    pairs = 2 * back + 1
    plane = idx_ref[0] // PLANE
    place = idx_ref[0] % PLANE
    base = (plane - back) * 2

    gather_queries(in_refs, place, q_in)
    lower = lax.broadcasted_iota(jnp.int32, (tok, 2 * HD), 1) < HD
    for at, part in key_blocks(kv_refs, place, tok, back):
        k2[at, :] = jnp.where(lower, part, pltpu.roll(part, HD, 1)).astype(BF16)
        value_t = jnp.transpose(part).astype(BF16)[HD:]
        v2t[:, at] = jnp.concatenate([value_t, value_t], axis=0)
    acc_k[...] = jnp.zeros_like(acc_k)
    left = lax.broadcasted_iota(jnp.int32, (blk, 2 * HD), 1) < HD
    pairs_at = head_pairs(per_pass, blk)

    def block(b, carry):
        pair_hi = plane * 2 + b
        steps = jnp.maximum(pair_hi - first_of(pair_hi * blk, seq_ref) // blk + 1, 2)
        q_rows = pl.ds(pl.multiple_of(b * blk, blk), blk)

        for h0 in range(0, heads, per_pass):
            kept = b * passes + h0 // per_pass
            for a, (even, odd) in enumerate(pairs_at):
                q2t = jnp.transpose(q_in[q_rows, lanes_of(h0, a)].astype(F32)).astype(BF16)
                qt[:, even] = q2t[:HD]
                qt[:, odd] = q2t[HD:]
            def gradients(step, count, first_time=False):
                lowest = pair_hi - step - count + 1 - base
                kk = k2[pl.ds(pl.multiple_of(lowest * blk, blk), count * blk), :]
                rows = [pl.ds(pl.multiple_of((pair_hi - step - c - base) * blk, blk), blk) for c in range(count)]
                v_t = [v2t[:, at] for at in rows]
                for even, odd in pairs_at:
                    at = slice(even.start, odd.stop)
                    shift = twice(inner[kept, at, :])
                    each = []
                    for c in reversed(range(count)):
                        e = probs[kept * pairs + step + c, at, :].astype(F32)
                        ds = (e * (dot(om[kept, at, :], v_t[c]) - shift)).astype(BF16)
                        dscore[c, at, :] = ds
                        each.append(ds)
                    dq = dot(jnp.concatenate(each, axis=1), kk)
                    q_acc[at, :] = dq if first_time else q_acc[at, :] + dq
                for c in range(count):
                    acc_k[:, rows[c]] = acc_k[:, rows[c]] + dot(qt[...], dscore[c])

            gradients(0, 2, first_time=True)
            in_twos(steps, 1, functools.partial(gradients, count=2), functools.partial(gradients, count=1))
            for a, (even, odd) in enumerate(pairs_at):
                qg = jnp.where(left, q_acc[even, :], q_acc[odd, :]) * SCALE
                res[q_rows, lanes_of(h0, a)] = qg.astype(BF16)
        return carry

    lax.fori_loop(0, 2, block, 0)
    send_back(acc_k, own_ref, back_refs, rows_all)
    for r in range(PLANE):
        mine = res[pl.ds(pl.multiple_of((place ^ r) * tok, tok), tok), :]
        if r == 1:
            mine = jnp.concatenate([attn_ref[...], mine], axis=1)
        out_refs[r][...] = mine


def attention_sizes(q_oc, kvs):
    tok, width2 = q_oc[0].shape
    rows = PLANE * tok
    back = len(kvs) - 1
    heads = width2 // 2 // HD
    blk = rows // 2
    pairs = 2 * back + 1
    per_pass = heads
    while per_pass > 2 and pairs * blk * per_pass * blk * 4 > 12 * 2**20:
        per_pass //= 2
    return tok, width2, rows, back, heads, blk, pairs, per_pass


def kernel_params(name, held, flops):
    return dict(
        name=name,
        compiler_params=pltpu.CompilerParams(vmem_limit_bytes=min(60 * 2**20, held)),
        cost_estimate=pl.CostEstimate(flops=flops, bytes_accessed=2**20, transcendentals=0),
    )


def forward(idx, seq, q_oc, kvs):
    tok, width2, rows, back, heads, blk, pairs, per_pass = attention_sizes(q_oc, kvs)
    cols = per_pass * blk
    keys = rows * (back + 1)
    kept = 2 * heads // per_pass
    held = pairs * blk * cols * 4 + kept * pairs * blk * cols * 2 + 16 * 2**20
    return pl.pallas_call(
        functools.partial(forward_kernel, back=back, heads=heads, per_pass=per_pass),
        out_shape=(
            [jax.ShapeDtypeStruct((tok, width2 // 2), BF16)] * PLANE
            + [jax.ShapeDtypeStruct((HD, rows), F32)]
            + [jax.ShapeDtypeStruct((HD, rows), BF16)] * back
            + [
                jax.ShapeDtypeStruct((kept * pairs, cols, blk), BF16),
                jax.ShapeDtypeStruct((kept, cols, 2 * HD), BF16),
                jax.ShapeDtypeStruct((kept, cols, 2 * HD), F32),
            ]
        ),
        in_specs=[whole(SMEM)] * 2 + [whole(VMEM)] * (PLANE + len(kvs)),
        out_specs=[whole(VMEM)] * (PLANE + 1 + back + 3),
        scratch_shapes=[
            VMEM((rows, width2), BF16),
            VMEM((rows, width2 // 2), BF16),
            VMEM((2 * HD, keys), BF16),
            VMEM((keys, 4 * HD), BF16),
            VMEM((cols, 2 * HD), BF16),
            VMEM((HD, cols), BF16),
            VMEM((blk, 2 * HD), jnp.int32),
            VMEM((2, blk, blk), F32),
            VMEM((pairs, cols, blk), F32),
            VMEM((cols, 4 * HD), F32),
            VMEM((cols, 2 * HD), F32),
            VMEM((HD, keys), F32),
        ],
        **kernel_params("forward", held, 20 * keys * rows * width2 // 2),
    )(idx, seq, *q_oc, *kvs)


def backward(idx, seq, q_oc, kvs, probs, om, inner, attn):
    tok, width2, rows, back, heads, blk, pairs, per_pass = attention_sizes(q_oc, kvs)
    cols = per_pass * blk
    keys = rows * (back + 1)
    held = probs.size * 2 + 16 * 2**20
    return pl.pallas_call(
        functools.partial(backward_kernel, back=back, heads=heads, per_pass=per_pass),
        out_shape=(
            [jax.ShapeDtypeStruct((tok, width2 if r == 1 else width2 // 2), BF16) for r in range(PLANE)]
            + [jax.ShapeDtypeStruct((HD, rows), F32)]
            + [jax.ShapeDtypeStruct((HD, rows), BF16)] * back
        ),
        in_specs=[whole(SMEM)] * 2 + [whole(VMEM)] * (PLANE + len(kvs) + 4),
        out_specs=[whole(VMEM)] * (PLANE + 1 + back),
        scratch_shapes=[
            VMEM((rows, width2), BF16),
            VMEM((rows, width2 // 2), BF16),
            VMEM((keys, 2 * HD), BF16),
            VMEM((2 * HD, keys), BF16),
            VMEM((HD, cols), BF16),
            VMEM((2, cols, blk), BF16),
            VMEM((cols, 2 * HD), F32),
            VMEM((HD, keys), F32),
        ],
        **kernel_params("backward", held, keys * rows),
    )(idx, seq, *q_oc, *kvs, probs, om, inner, attn)


def sum_kernel(idx_ref, own_ref, *rest, back):
    got_refs = rest[:back]
    cot_ref, res_ref = rest[back:back + 2]
    part_refs = rest[back + 2:back + 2 + PLANE]
    total = rest[back + 2 + PLANE]
    tok = part_refs[0].shape[1]
    place = idx_ref[0] % PLANE
    summed = own_ref[...]
    for got in got_refs:
        summed = summed + got[...].astype(F32)
    total[0:HD, :] = summed.astype(BF16)
    total[HD:2 * HD, :] = cot_ref[...]
    for r in range(PLANE):
        part_refs[r][:, 0:tok] = total[:, pl.ds(pl.multiple_of((place ^ r) * tok, tok), tok)]
    part_refs[1][:, tok:] = res_ref[...]


def wv_kernel(idx_ref, own_ref, *refs, back, n_ctx):
    got_refs, hidden_refs = refs[:back], refs[back:back + PLANE]
    cot_ref, wv_ref = refs[back + PLANE:]
    tok, features = hidden_refs[0].shape
    place = idx_ref[0] % PLANE
    summed = own_ref[...]
    for got in got_refs:
        summed = summed + got[...].astype(F32)
    cot_ref[...] = summed.astype(BF16)
    wv = jnp.zeros((HD, features), F32)
    for r in range(PLANE):
        at = pl.ds(pl.multiple_of((place ^ r) * tok, tok), tok)
        wv = wv + dot(cot_ref[:, at], hidden_refs[r][...])
    wv = jnp.transpose(wv)
    rows = features // n_ctx
    if wv_ref.shape[2] == 2 * HD:
        for d in range(n_ctx):
            one = wv[d * rows:(d + 1) * rows]
            wv_ref[d] = jnp.concatenate([one[:rows // 2], one[rows // 2:]], axis=1).astype(BF16)
    else:
        for d in range(n_ctx):
            wv_ref[d] = wv[d * rows:(d + 1) * rows].astype(BF16)


def results_kernel(idx_ref, part_ref, *refs):
    in_refs, out_refs = refs[:-2], refs[-2:]
    place = idx_ref[0] % PLANE
    lanes = in_refs[0].shape[1]
    tok = part_ref.shape[1] - 2 * lanes
    for i, out_ref in enumerate(out_refs):
        rest = list(in_refs[i * (PLANE - 1):(i + 1) * (PLANE - 1)])
        for r in range(PLANE):
            at = pl.ds(pl.multiple_of((place ^ r) * lanes, lanes), lanes)
            if r == 1:
                out_ref[:, at] = part_ref[:, tok + i * lanes:tok + (i + 1) * lanes]
            else:
                out_ref[:, at] = rest.pop(0)[...]


def finish_kernel(idx_ref, weight_ref, *rest):
    part_refs = rest[:PLANE]
    kg_ref, xg_ref, parts = rest[PLANE:]
    place = idx_ref[0] % PLANE
    for r in range(PLANE):
        tok = part_refs[0].shape[1]
        parts[place ^ r] = jnp.transpose(part_refs[r][:, 0:tok].astype(F32)).astype(BF16)
    kg_ref[...] = jnp.concatenate([parts[g, :, 0:HD] for g in range(PLANE)], axis=1)
    value_cot = jnp.concatenate([parts[g, :, HD:2 * HD] for g in range(PLANE)], axis=1)
    xg_ref[...] = lax.dot_general(
        value_cot, weight_ref[...], (((1,), (1,)), ((), ())), preferred_element_type=F32
    ).astype(BF16)


def wv_sum_kernel(wv_ref, out_ref):
    n_ctx, depth, lanes = wv_ref.shape
    sums = []
    for g in range(PLANE):
        total = wv_ref[g].astype(F32)
        for d in range(g + PLANE, n_ctx, PLANE):
            total = total + wv_ref[d].astype(F32)
        sums.append(total)
    for side in range(lanes // HD):
        out_ref[side * depth:(side + 1) * depth, :] = jnp.concatenate(
            [total[:, side * HD:(side + 1) * HD] for total in sums], axis=1
        )


def shifted(x, by):
    n = lax.axis_size("ctx")
    return lax.ppermute(x, "ctx", [(i, i + by) for i in range(n) if 0 <= i + by < n])


def crossed(x, by):
    n = lax.axis_size("ctx")
    return lax.ppermute(x, "ctx", [(i, i ^ by) for i in range(n)])


def in_plane(x):
    n = lax.axis_size("ctx")
    planes = [list(range(i, i + PLANE)) for i in range(0, n, PLANE)]
    return lax.all_to_all(x, "ctx", 0, 0, axis_index_groups=planes, tiled=True)


def shards(
    queries, keys, hidden, value_weight, out_grad, new_logp, old_logp, rewards, group_ids, seq_lengths
):
    n_ctx = lax.axis_size("ctx")
    tok, width = queries.shape
    kv_width = keys.shape[1]
    features = hidden.shape[1]
    back = n_ctx // 2 // PLANE
    ctx = lax.axis_index("ctx").astype(jnp.int32)
    idx = ctx.reshape(1)
    lanes = width // PLANE
    plane_rows = PLANE * tok

    outs = pl.pallas_call(
        prepare_kernel,
        out_shape=[jax.ShapeDtypeStruct((tok, 2 * HD), BF16)] * PLANE
        + [jax.ShapeDtypeStruct((tok, 2 * lanes), BF16)] * PLANE,
        in_specs=[whole(SMEM)] * 4 + [whole(VMEM)] * 2 + [whole(pltpu.HBM)] * 5,
        out_specs=[whole(pltpu.HBM)] * (2 * PLANE),
        scratch_shapes=[
            VMEM((PLANE, tok, 2 * HD), BF16),
            VMEM(hidden.shape, BF16),
            VMEM(value_weight.shape, BF16),
            VMEM(keys.shape, BF16),
            VMEM((PLANE, tok, lanes), BF16),
            VMEM((PLANE, tok, lanes), BF16),
            VMEM((PLANE, tok, 2 * lanes), BF16),
            pltpu.SemaphoreType.DMA((7, PLANE)),
        ],
        **small("prepare", mib=60),
    )(
        idx, seq_lengths, group_ids, rewards, new_logp[None, :], old_logp[None, :],
        hidden, value_weight, keys, queries, out_grad,
    )
    kv, q_oc = list(outs[:PLANE]), list(outs[PLANE:])

    q_oc = [q_oc[0]] + [crossed(q_oc[r], r) for r in range(1, PLANE)]
    kv = [kv[0]] + [crossed(kv[r], r) for r in range(1, PLANE)]
    kv = pl.pallas_call(
        join_kernel,
        out_shape=jax.ShapeDtypeStruct((plane_rows, 2 * HD), BF16),
        in_specs=[whole(VMEM)] * PLANE,
        out_specs=whole(VMEM),
        **small("join", 10**10),
    )(*kv)
    kvs = [kv] + [shifted(kv, w * PLANE) for w in range(1, back + 1)]
    late_hidden, q_oc[1] = lax.optimization_barrier((hidden, q_oc[1]))
    hidden_c = crossed(late_hidden, 1)
    late_hidden, q_oc, hidden_c = lax.optimization_barrier((hidden, q_oc, hidden_c))
    hidden_y = crossed(late_hidden, 2)

    outs = list(forward(idx, seq_lengths, q_oc, kvs))
    attn, own_v, backs_v = outs[:PLANE], outs[PLANE], outs[PLANE + 1:PLANE + 1 + back]
    probs, om, inner = outs[PLANE + 1 + back:]
    got_v = [shifted(backs_v[w - 1], -w * PLANE) for w in range(1, back + 1)]
    attn = [attn[0], attn[1]] + [crossed(attn[r], r) for r in range(2, PLANE)]
    outs = list(backward(idx, seq_lengths, q_oc, kvs, probs, om, inner, attn[1]))
    outs, got_v, attn, hidden_y = lax.optimization_barrier((outs, got_v, attn, hidden_y))
    hidden_cy = crossed(hidden_y, 1)
    qg, own_k, backs_k = outs[:PLANE], outs[PLANE], outs[PLANE + 1:]
    got_k = [shifted(backs_k[w - 1], -w * PLANE) for w in range(1, back + 1)]
    rows = features // n_ctx
    packed = (rows // 2) % 8 == 0
    piece = (rows // 2, 2 * HD) if packed else (rows, HD)
    cot, wv = pl.pallas_call(
        functools.partial(wv_kernel, back=back, n_ctx=n_ctx),
        out_shape=[
            jax.ShapeDtypeStruct((HD, plane_rows), BF16),
            jax.ShapeDtypeStruct((n_ctx,) + piece, BF16),
        ],
        in_specs=[whole(SMEM)] + [whole(VMEM)] * (1 + back + PLANE),
        out_specs=[whole(VMEM)] * 2,
        **small("wv"),
    )(idx, own_v, *got_v, hidden, hidden_c, hidden_y, hidden_cy)
    qg = [qg[0], qg[1]] + [crossed(qg[r], r) for r in range(2, PLANE)]
    parts = pl.pallas_call(
        functools.partial(sum_kernel, back=back),
        out_shape=[
            jax.ShapeDtypeStruct((2 * HD, tok + 2 * lanes if r == 1 else tok), BF16) for r in range(PLANE)
        ],
        in_specs=[whole(SMEM)] + [whole(VMEM)] * (3 + back),
        out_specs=[whole(VMEM)] * PLANE,
        scratch_shapes=[VMEM((2 * HD, plane_rows), BF16)],
        **small("sum", 10**10),
    )(idx, own_k, *got_k, cot, qg[1])
    parts, qg[2:] = lax.optimization_barrier((list(parts), qg[2:]))
    parts = [parts[0]] + [crossed(parts[r], r) for r in range(1, PLANE)]
    attn, q_grad = pl.pallas_call(
        results_kernel,
        out_shape=[jax.ShapeDtypeStruct((tok, width), BF16)] * 2,
        in_specs=[whole(SMEM)] + [whole(VMEM)] * (2 * PLANE - 1),
        out_specs=[whole(VMEM)] * 2,
        **small("results", 10**9),
    )(idx, parts[1], attn[0], *attn[2:], qg[0], *qg[2:])
    wv = lax.all_to_all(wv, "ctx", 0, 0, tiled=True)
    k_grad, x_grad = pl.pallas_call(
        finish_kernel,
        out_shape=[
            jax.ShapeDtypeStruct((tok, kv_width), BF16),
            jax.ShapeDtypeStruct((tok, features), BF16),
        ],
        in_specs=[whole(SMEM)] + [whole(VMEM)] * (1 + PLANE),
        out_specs=[whole(VMEM)] * 2,
        scratch_shapes=[VMEM((PLANE, tok, 2 * HD), BF16)],
        **small("finish"),
    )(idx, value_weight, *parts)

    wv_grad = pl.pallas_call(
        wv_sum_kernel,
        out_shape=jax.ShapeDtypeStruct((rows, kv_width), F32),
        in_specs=[whole(VMEM)],
        out_specs=whole(VMEM),
        **small("wv_sum", 10**10),
    )(wv)
    return (attn, q_grad, k_grad, x_grad, wv_grad)


def solution(mesh):
    rows = P(("groups", "ctx"), None)
    flat = P(("groups", "ctx"))
    placed = (rows, rows, rows, P(), rows, flat, flat, P("groups"), P("groups"), P("groups"))
    return jax.shard_map(
        shards, mesh=mesh, in_specs=placed, out_specs=(rows,) * 5, check_vma=False
    )
```

```python
import functools
import math

import jax
import jax.numpy as jnp
from jax import lax
from jax.experimental import pallas as pl
from jax.experimental.pallas import tpu as pltpu
from jax.sharding import PartitionSpec as P

HD = 64
PLANE = 4
SCALE = 1.0 / math.sqrt(HD)
BIG_NEGATIVE = -1e30
VMEM = pltpu.VMEM
SMEM = pltpu.SMEM
BF16 = jnp.bfloat16
F32 = jnp.float32


def dot(a, b):
    return lax.dot_general(a, b, (((1,), (0,)), ((), ())), preferred_element_type=F32)


def whole(space):
    return pl.BlockSpec(memory_space=space)


def small(name, flops=10**6, mib=12):
    return dict(
        name=name,
        compiler_params=pltpu.CompilerParams(vmem_limit_bytes=mib * 2**20),
        cost_estimate=pl.CostEstimate(flops=flops, bytes_accessed=2**16, transcendentals=0),
    )


def token_weights(idx, tok, seq_ref, rew_ref, gid_ref, new_ref, old_ref):
    nseq = seq_ref.shape[0]
    pos = idx * tok + lax.broadcasted_iota(jnp.int32, (1, tok), 1)
    reward = jnp.zeros(pos.shape, F32)
    total = jnp.zeros(pos.shape, F32)
    count = jnp.ones(pos.shape, F32)
    begin = jnp.int32(0)
    for i in range(nseq):
        gsum = F32(0)
        gcount = F32(0)
        for j in range(nseq):
            same = gid_ref[j] == gid_ref[i]
            gsum = gsum + jnp.where(same, rew_ref[j], 0.0)
            gcount = gcount + jnp.where(same, 1.0, 0.0)
        here = pos >= begin
        reward = jnp.where(here, rew_ref[i], reward)
        total = jnp.where(here, gsum, total)
        count = jnp.where(here, gcount, count)
        begin = begin + seq_ref[i]
    return (total / count - reward) * jnp.exp(new_ref[...] - old_ref[...])


def prepare_kernel(
    idx_ref, seq_hbm, gid_hbm, rew_hbm, new_hbm, old_hbm, hidden_hbm, weight_hbm, keys_hbm, q_hbm, og_hbm, *rest
):
    kv_refs, q_refs = rest[:PLANE], rest[PLANE:2 * PLANE]
    (parts, hidden, weight, keys, q_in, og_in, q_out, seq_ref, gid_ref, rew_ref, new_ref, old_ref, sems,
     scalar_sems) = rest[2 * PLANE:]
    _, tok, lanes = q_in.shape
    place = idx_ref[0] % PLANE
    depth = hidden.shape[1] // PLANE
    value_copies = []
    query_copies = []
    for c in range(PLANE):
        at = pl.ds(c * depth, depth)
        value_copies.append((
            pltpu.make_async_copy(weight_hbm.at[at, :], weight.at[at, :], sems.at[0, c]),
            pltpu.make_async_copy(hidden_hbm.at[:, at], hidden.at[:, at], sems.at[1, c]),
        ))
        at = pl.ds(pl.multiple_of((place ^ c) * lanes, lanes), lanes)
        query_copies.append((
            pltpu.make_async_copy(q_hbm.at[:, at], q_in.at[c], sems.at[2, c]),
            pltpu.make_async_copy(og_hbm.at[:, at], og_in.at[c], sems.at[3, c]),
        ))
    key_copy = pltpu.make_async_copy(keys_hbm, keys, sems.at[4, 0])
    for pair in value_copies:
        for copy in pair:
            copy.start()
    key_copy.start()
    for pair in query_copies:
        for copy in pair:
            copy.start()
    scalars = [
        pltpu.make_async_copy(source, target, scalar_sems.at[i])
        for i, (source, target) in enumerate((
            (seq_hbm, seq_ref), (gid_hbm, gid_ref), (rew_hbm, rew_ref), (new_hbm, new_ref), (old_hbm, old_ref)
        ))
    ]
    for copy in scalars:
        copy.start()
    for copy in scalars:
        copy.wait()
    token = token_weights(idx_ref[0], tok, seq_ref, rew_ref, gid_ref, new_ref, old_ref)
    token = jnp.transpose(jnp.broadcast_to(token, (tok, tok)))[:, 0:1]
    values = jnp.zeros((hidden.shape[0], weight.shape[1]), F32)
    for c, pair in enumerate(value_copies):
        for copy in pair:
            copy.wait()
        at = slice(c * depth, (c + 1) * depth)
        values = values + dot(hidden[:, at], weight[at, :])
    values = values.astype(BF16)
    key_copy.wait()
    for g in range(PLANE):
        at = slice(g * HD, (g + 1) * HD)
        parts[g] = jnp.concatenate([keys[:, at], values[:, at]], axis=1)
    results = [pltpu.make_async_copy(parts.at[place ^ r], kv_refs[r], sems.at[5, r]) for r in range(PLANE)]
    for copy in results:
        copy.start()
    for r, pair in enumerate(query_copies):
        for copy in pair:
            copy.wait()
        q_out[r, :, 0:lanes] = (q_in[r].astype(F32) * SCALE).astype(BF16)
        q_out[r, :, lanes:2 * lanes] = (og_in[r].astype(F32) * token).astype(BF16)
        results.append(pltpu.make_async_copy(q_out.at[r], q_refs[r], sems.at[6, r]))
        results[-1].start()
    for copy in results:
        copy.wait()


def join_kernel(*refs):
    tok = refs[0].shape[0]
    for r in range(PLANE):
        refs[PLANE][r * tok:(r + 1) * tok, :] = refs[r][...]


def twice(x):
    return jnp.concatenate([x, x], axis=1)


def first_of(position, seq_ref):
    start = position * 0
    begin = jnp.int32(0)
    for i in range(seq_ref.shape[0]):
        start = jnp.where(position >= begin, begin, start)
        begin = begin + seq_ref[i]
    return start


def in_twos(steps, begin, two, one):
    def body(i, carry):
        two(2 * i)
        return carry

    lax.fori_loop(begin, steps // 2, body, 0)
    pl.when(steps % 2 == 1)(lambda: one(steps - 1))


def head_pairs(per_pass, blk):
    return [
        (slice(2 * a * blk, (2 * a + 1) * blk), slice((2 * a + 1) * blk, (2 * a + 2) * blk))
        for a in range(per_pass // 2)
    ]


def lanes_of(h0, a, offset=0):
    return slice(offset + (h0 + 2 * a) * HD, offset + (h0 + 2 * a + 2) * HD)


def gather_queries(in_refs, place, q_in):
    tok = in_refs[0].shape[0]
    for r in range(PLANE):
        q_in[pl.ds(pl.multiple_of((place ^ r) * tok, tok), tok), :] = in_refs[r][...]


def key_blocks(kv_refs, place, tok, back):
    for w in range(back + 1):
        for r in range(PLANE):
            at = pl.ds(pl.multiple_of(((back - w) * PLANE + (place ^ r)) * tok, tok), tok)
            yield at, kv_refs[w][r * tok:(r + 1) * tok, :].astype(F32)


def send_back(acc, own_ref, back_refs, rows_all):
    back = len(back_refs)
    own_ref[...] = acc[:, back * rows_all:]
    for w in range(1, back + 1):
        back_refs[w - 1][...] = acc[:, (back - w) * rows_all:(back - w + 1) * rows_all].astype(BF16)


def forward_kernel(idx_ref, seq_ref, *rest, back, heads, per_pass):
    in_refs = rest[:PLANE]
    kv_refs = rest[PLANE:PLANE + back + 1]
    rest = rest[PLANE + back + 1:]
    out_refs = rest[:PLANE]
    own_ref = rest[PLANE]
    back_refs = rest[PLANE + 1:PLANE + 1 + back]
    probs, om, inner, q_in, res, k2t, v2, qm, ot, start, bias, score, o_acc, top, acc_v = rest[PLANE + 1 + back:]
    tok = in_refs[0].shape[0]
    rows_all = PLANE * tok
    blk = rows_all // 2
    width = heads * HD
    passes = heads // per_pass
    pairs = 2 * back + 1
    plane = idx_ref[0] // PLANE
    place = idx_ref[0] % PLANE
    base = (plane - back) * 2

    gather_queries(in_refs, place, q_in)
    lower = lax.broadcasted_iota(jnp.int32, (tok, 2 * HD), 1) < HD
    for at, part in key_blocks(kv_refs, place, tok, back):
        v2[at, 0:2 * HD] = jnp.where(lower, pltpu.roll(part, HD, 1), part).astype(BF16)
        key_t = jnp.transpose(part).astype(BF16)[:HD]
        k2t[:, at] = jnp.concatenate([key_t, key_t], axis=0)
    v2[:, 2 * HD:] = jnp.ones((v2.shape[0], 2 * HD), BF16)
    acc_v[...] = jnp.zeros_like(acc_v)
    left = lax.broadcasted_iota(jnp.int32, (blk, 2 * HD), 1) < HD
    pairs_at = head_pairs(per_pass, blk)

    def block(b, carry):
        pair_hi = plane * 2 + b
        first = pair_hi * blk
        start[...] = first_of(first + lax.broadcasted_iota(jnp.int32, (blk, 2 * HD), 0), seq_ref)
        start_hi = first_of(first + blk - 1, seq_ref)
        steps = jnp.clip(pair_hi - first_of(first, seq_ref) // blk + 1, 2, pairs)
        q_rows = pl.ds(pl.multiple_of(b * blk, blk), blk)

        for h0 in range(0, heads, per_pass):
            kept = b * passes + h0 // per_pass
            for a, (even, odd) in enumerate(pairs_at):
                q2 = q_in[q_rows, lanes_of(h0, a)]
                qm[even, :] = jnp.where(left, q2, jnp.zeros_like(q2))
                qm[odd, :] = jnp.where(left, jnp.zeros_like(q2), q2)

            def scores(step, count, first_time=False, edges=True):
                k_t = [
                    k2t[:, pl.ds(pl.multiple_of((pair_hi - step - c - base) * blk, blk), blk)] for c in range(count)
                ]
                if edges:
                    for c in range(count):
                        key_pos = (pair_hi - step - c) * blk + lax.broadcasted_iota(jnp.int32, (blk, blk), 1)
                        tok_pos = first + lax.broadcasted_iota(jnp.int32, (blk, blk), 0)
                        seen = (key_pos >= twice(start[...])) & (key_pos <= tok_pos)
                        bias[c] = jnp.where(seen, 0.0, BIG_NEGATIVE)
                for even, odd in pairs_at:
                    at = slice(even.start, odd.stop)
                    most = None if first_time else top[at, :]
                    for c in range(count):
                        s = dot(qm[at, :], k_t[c])
                        if edges:
                            s = s + jnp.concatenate([bias[c], bias[c]], axis=0)
                        score[step + c, at, :] = s
                        one = jnp.maximum(s[:, :2 * HD], s[:, 2 * HD:])
                        most = one if most is None else jnp.maximum(most, one)
                    top[at, :] = most

            def outputs(step, count, first_time=False):
                vv = v2[pl.ds(pl.multiple_of((pair_hi - step - count + 1 - base) * blk, blk), count * blk), :]
                for even, odd in pairs_at:
                    at = slice(even.start, odd.stop)
                    most = twice(top[at, :])
                    ebs = []
                    for c in reversed(range(count)):
                        eb = jnp.exp(score[step + c, at, :] - most).astype(BF16)
                        probs[kept * pairs + step + c, at, :] = eb
                        ebs.append(eb)
                    out = dot(jnp.concatenate(ebs, axis=1), vv)
                    o_acc[at, :] = out if first_time else o_acc[at, :] + out

            def value_grad(step, count):
                for c in range(count):
                    rows = pl.ds(pl.multiple_of((pair_hi - step - c - base) * blk, blk), blk)
                    acc_v[:, rows] = acc_v[:, rows] + dot(ot[...], probs[kept * pairs + step + c])

            def more_scores(step):
                inside = (pair_hi - step - 1) * blk >= start_hi
                pl.when(inside)(functools.partial(scores, step, 2, edges=False))
                pl.when(jnp.logical_not(inside))(functools.partial(scores, step, 2))

            scores(0, 2, first_time=True)
            in_twos(steps, 1, more_scores, functools.partial(scores, count=1))
            top[...] = jnp.broadcast_to(jnp.max(top[...], axis=1, keepdims=True), top.shape)
            outputs(0, 2, first_time=True)
            in_twos(steps, 1, functools.partial(outputs, count=2), functools.partial(outputs, count=1))
            for a, pair_at in enumerate(pairs_at):
                o2 = q_in[q_rows, lanes_of(h0, a, width)].astype(F32)
                out = []
                scaled = []
                for side, at in enumerate(pair_at):
                    inv = 1.0 / o_acc[at, 2 * HD:]
                    out.append(o_acc[at, 0:2 * HD] * inv)
                    mine = jnp.where(left if side == 0 else jnp.logical_not(left), o2, 0.0) * inv
                    inner[kept, at, :] = jnp.broadcast_to(
                        jnp.sum(mine * out[side], axis=1, keepdims=True), (blk, 2 * HD)
                    )
                    scaled.append(mine)
                    om[kept, at, :] = mine.astype(BF16)
                res[q_rows, lanes_of(h0, a)] = jnp.where(left, out[0], out[1]).astype(BF16)
                o2t = jnp.transpose(scaled[0] + scaled[1]).astype(BF16)
                ot[:, pair_at[0]] = o2t[:HD]
                ot[:, pair_at[1]] = o2t[HD:]

            in_twos(steps, 0, functools.partial(value_grad, count=2), functools.partial(value_grad, count=1))
        return carry

    lax.fori_loop(0, 2, block, 0)
    send_back(acc_v, own_ref, back_refs, rows_all)
    for r in range(PLANE):
        out_refs[r][...] = res[pl.ds(pl.multiple_of((place ^ r) * tok, tok), tok), :]


def backward_kernel(idx_ref, seq_ref, *rest, back, heads, per_pass):
    in_refs = rest[:PLANE]
    kv_refs = rest[PLANE:PLANE + back + 1]
    probs, om, inner, attn_ref = rest[PLANE + back + 1:PLANE + back + 5]
    rest = rest[PLANE + back + 5:]
    out_refs = rest[:PLANE]
    own_ref = rest[PLANE]
    back_refs = rest[PLANE + 1:PLANE + 1 + back]
    q_in, res, k2, v2t, qt, dscore, q_acc, acc_k = rest[PLANE + 1 + back:]
    tok = in_refs[0].shape[0]
    rows_all = PLANE * tok
    blk = rows_all // 2
    passes = heads // per_pass
    pairs = 2 * back + 1
    plane = idx_ref[0] // PLANE
    place = idx_ref[0] % PLANE
    base = (plane - back) * 2

    gather_queries(in_refs, place, q_in)
    lower = lax.broadcasted_iota(jnp.int32, (tok, 2 * HD), 1) < HD
    for at, part in key_blocks(kv_refs, place, tok, back):
        k2[at, :] = jnp.where(lower, part, pltpu.roll(part, HD, 1)).astype(BF16)
        value_t = jnp.transpose(part).astype(BF16)[HD:]
        v2t[:, at] = jnp.concatenate([value_t, value_t], axis=0)
    acc_k[...] = jnp.zeros_like(acc_k)
    left = lax.broadcasted_iota(jnp.int32, (blk, 2 * HD), 1) < HD
    pairs_at = head_pairs(per_pass, blk)

    def block(b, carry):
        pair_hi = plane * 2 + b
        steps = jnp.clip(pair_hi - first_of(pair_hi * blk, seq_ref) // blk + 1, 2, pairs)
        q_rows = pl.ds(pl.multiple_of(b * blk, blk), blk)

        for h0 in range(0, heads, per_pass):
            kept = b * passes + h0 // per_pass
            for a, (even, odd) in enumerate(pairs_at):
                q2t = jnp.transpose(q_in[q_rows, lanes_of(h0, a)].astype(F32)).astype(BF16)
                qt[:, even] = q2t[:HD]
                qt[:, odd] = q2t[HD:]
            def gradients(step, count, first_time=False):
                lowest = pair_hi - step - count + 1 - base
                kk = k2[pl.ds(pl.multiple_of(lowest * blk, blk), count * blk), :]
                rows = [pl.ds(pl.multiple_of((pair_hi - step - c - base) * blk, blk), blk) for c in range(count)]
                v_t = [v2t[:, at] for at in rows]
                for even, odd in pairs_at:
                    at = slice(even.start, odd.stop)
                    shift = twice(inner[kept, at, :])
                    each = []
                    for c in reversed(range(count)):
                        e = probs[kept * pairs + step + c, at, :].astype(F32)
                        ds = (e * (dot(om[kept, at, :], v_t[c]) - shift)).astype(BF16)
                        dscore[c, at, :] = ds
                        each.append(ds)
                    dq = dot(jnp.concatenate(each, axis=1), kk)
                    q_acc[at, :] = dq if first_time else q_acc[at, :] + dq
                for c in range(count):
                    acc_k[:, rows[c]] = acc_k[:, rows[c]] + dot(qt[...], dscore[c])

            gradients(0, 2, first_time=True)
            in_twos(steps, 1, functools.partial(gradients, count=2), functools.partial(gradients, count=1))
            for a, (even, odd) in enumerate(pairs_at):
                qg = jnp.where(left, q_acc[even, :], q_acc[odd, :]) * SCALE
                res[q_rows, lanes_of(h0, a)] = qg.astype(BF16)
        return carry

    lax.fori_loop(0, 2, block, 0)
    send_back(acc_k, own_ref, back_refs, rows_all)
    for r in range(PLANE):
        mine = res[pl.ds(pl.multiple_of((place ^ r) * tok, tok), tok), :]
        if r == 1:
            mine = jnp.concatenate([attn_ref[...], mine], axis=1)
        out_refs[r][...] = mine


def attention_sizes(q_oc, kvs):
    tok, width2 = q_oc[0].shape
    rows = PLANE * tok
    back = len(kvs) - 1
    heads = width2 // 2 // HD
    blk = rows // 2
    pairs = 2 * back + 1
    per_pass = heads
    while per_pass > 2 and pairs * blk * per_pass * blk * 4 > 12 * 2**20:
        per_pass //= 2
    return tok, width2, rows, back, heads, blk, pairs, per_pass


def kernel_params(name, held, flops):
    return dict(
        name=name,
        compiler_params=pltpu.CompilerParams(vmem_limit_bytes=min(60 * 2**20, held)),
        cost_estimate=pl.CostEstimate(flops=flops, bytes_accessed=2**20, transcendentals=0),
    )


def forward(idx, seq, q_oc, kvs):
    tok, width2, rows, back, heads, blk, pairs, per_pass = attention_sizes(q_oc, kvs)
    cols = per_pass * blk
    keys = rows * (back + 1)
    kept = 2 * heads // per_pass
    held = pairs * blk * cols * 4 + kept * pairs * blk * cols * 2 + 16 * 2**20
    return pl.pallas_call(
        functools.partial(forward_kernel, back=back, heads=heads, per_pass=per_pass),
        out_shape=(
            [jax.ShapeDtypeStruct((tok, width2 // 2), BF16)] * PLANE
            + [jax.ShapeDtypeStruct((HD, rows), F32)]
            + [jax.ShapeDtypeStruct((HD, rows), BF16)] * back
            + [
                jax.ShapeDtypeStruct((kept * pairs, cols, blk), BF16),
                jax.ShapeDtypeStruct((kept, cols, 2 * HD), BF16),
                jax.ShapeDtypeStruct((kept, cols, 2 * HD), F32),
            ]
        ),
        in_specs=[whole(SMEM)] * 2 + [whole(VMEM)] * (PLANE + len(kvs)),
        out_specs=[whole(VMEM)] * (PLANE + 1 + back + 3),
        scratch_shapes=[
            VMEM((rows, width2), BF16),
            VMEM((rows, width2 // 2), BF16),
            VMEM((2 * HD, keys), BF16),
            VMEM((keys, 4 * HD), BF16),
            VMEM((cols, 2 * HD), BF16),
            VMEM((HD, cols), BF16),
            VMEM((blk, 2 * HD), jnp.int32),
            VMEM((2, blk, blk), F32),
            VMEM((pairs, cols, blk), F32),
            VMEM((cols, 4 * HD), F32),
            VMEM((cols, 2 * HD), F32),
            VMEM((HD, keys), F32),
        ],
        **kernel_params("forward", held, 20 * keys * rows * width2 // 2),
    )(idx, seq, *q_oc, *kvs)


def backward(idx, seq, q_oc, kvs, probs, om, inner, attn):
    tok, width2, rows, back, heads, blk, pairs, per_pass = attention_sizes(q_oc, kvs)
    cols = per_pass * blk
    keys = rows * (back + 1)
    held = probs.size * 2 + 16 * 2**20
    return pl.pallas_call(
        functools.partial(backward_kernel, back=back, heads=heads, per_pass=per_pass),
        out_shape=(
            [jax.ShapeDtypeStruct((tok, width2 if r == 1 else width2 // 2), BF16) for r in range(PLANE)]
            + [jax.ShapeDtypeStruct((HD, rows), F32)]
            + [jax.ShapeDtypeStruct((HD, rows), BF16)] * back
        ),
        in_specs=[whole(SMEM)] * 2 + [whole(VMEM)] * (PLANE + len(kvs) + 4),
        out_specs=[whole(VMEM)] * (PLANE + 1 + back),
        scratch_shapes=[
            VMEM((rows, width2), BF16),
            VMEM((rows, width2 // 2), BF16),
            VMEM((keys, 2 * HD), BF16),
            VMEM((2 * HD, keys), BF16),
            VMEM((HD, cols), BF16),
            VMEM((2, cols, blk), BF16),
            VMEM((cols, 2 * HD), F32),
            VMEM((HD, keys), F32),
        ],
        **kernel_params("backward", held, keys * rows),
    )(idx, seq, *q_oc, *kvs, probs, om, inner, attn)


def sum_kernel(idx_ref, own_ref, *rest, back):
    got_refs = rest[:back]
    cot_ref, res_ref = rest[back:back + 2]
    part_refs = rest[back + 2:back + 2 + PLANE]
    total = rest[back + 2 + PLANE]
    tok = part_refs[0].shape[1]
    place = idx_ref[0] % PLANE
    summed = own_ref[...]
    for got in got_refs:
        summed = summed + got[...].astype(F32)
    total[0:HD, :] = summed.astype(BF16)
    total[HD:2 * HD, :] = cot_ref[...]
    for r in range(PLANE):
        part_refs[r][:, 0:tok] = total[:, pl.ds(pl.multiple_of((place ^ r) * tok, tok), tok)]
    part_refs[1][:, tok:] = res_ref[...]


def wv_kernel(idx_ref, own_ref, *refs, back, n_ctx):
    got_refs, hidden_refs = refs[:back], refs[back:back + PLANE]
    cot_ref, wv_ref = refs[back + PLANE:]
    tok, features = hidden_refs[0].shape
    place = idx_ref[0] % PLANE
    summed = own_ref[...]
    for got in got_refs:
        summed = summed + got[...].astype(F32)
    cot_ref[...] = summed.astype(BF16)
    wv = jnp.zeros((HD, features), F32)
    for r in range(PLANE):
        at = pl.ds(pl.multiple_of((place ^ r) * tok, tok), tok)
        wv = wv + dot(cot_ref[:, at], hidden_refs[r][...])
    rows = features // n_ctx
    if wv_ref.shape[2] == 2 * HD:
        wv = jnp.transpose(wv.astype(BF16))
        for d in range(n_ctx):
            one = wv[d * rows:(d + 1) * rows]
            wv_ref[d] = jnp.concatenate([one[:rows // 2], one[rows // 2:]], axis=1)
    else:
        wv = jnp.transpose(wv)
        for d in range(n_ctx):
            wv_ref[d] = wv[d * rows:(d + 1) * rows].astype(BF16)


def results_kernel(idx_ref, part_ref, *refs):
    in_refs, out_refs = refs[:-2], refs[-2:]
    place = idx_ref[0] % PLANE
    lanes = in_refs[0].shape[1]
    tok = part_ref.shape[1] - 2 * lanes
    for i, out_ref in enumerate(out_refs):
        rest = list(in_refs[i * (PLANE - 1):(i + 1) * (PLANE - 1)])
        for r in range(PLANE):
            at = pl.ds(pl.multiple_of((place ^ r) * lanes, lanes), lanes)
            if r == 1:
                out_ref[:, at] = part_ref[:, tok + i * lanes:tok + (i + 1) * lanes]
            else:
                out_ref[:, at] = rest.pop(0)[...]


def finish_kernel(idx_ref, weight_ref, *rest):
    part_refs = rest[:PLANE]
    kg_ref, xg_ref, parts = rest[PLANE:]
    place = idx_ref[0] % PLANE
    for r in range(PLANE):
        tok = part_refs[0].shape[1]
        parts[place ^ r] = jnp.transpose(part_refs[r][:, 0:tok].astype(F32)).astype(BF16)
    kg_ref[...] = jnp.concatenate([parts[g, :, 0:HD] for g in range(PLANE)], axis=1)
    value_cot = jnp.concatenate([parts[g, :, HD:2 * HD] for g in range(PLANE)], axis=1)
    xg_ref[...] = lax.dot_general(
        value_cot, weight_ref[...], (((1,), (1,)), ((), ())), preferred_element_type=F32
    ).astype(BF16)


def wv_sum_kernel(wv_ref, out_ref):
    n_ctx, depth, lanes = wv_ref.shape
    sums = []
    for g in range(PLANE):
        total = wv_ref[g].astype(F32)
        for d in range(g + PLANE, n_ctx, PLANE):
            total = total + wv_ref[d].astype(F32)
        sums.append(total)
    for side in range(lanes // HD):
        out_ref[side * depth:(side + 1) * depth, :] = jnp.concatenate(
            [total[:, side * HD:(side + 1) * HD] for total in sums], axis=1
        )


def shifted(x, by):
    n = lax.axis_size("ctx")
    return lax.ppermute(x, "ctx", [(i, i + by) for i in range(n) if 0 <= i + by < n])


def crossed(x, by):
    n = lax.axis_size("ctx")
    return lax.ppermute(x, "ctx", [(i, i ^ by) for i in range(n)])


def in_plane(x):
    n = lax.axis_size("ctx")
    planes = [list(range(i, i + PLANE)) for i in range(0, n, PLANE)]
    return lax.all_to_all(x, "ctx", 0, 0, axis_index_groups=planes, tiled=True)


def shards(
    queries, keys, hidden, value_weight, out_grad, new_logp, old_logp, rewards, group_ids, seq_lengths
):
    n_ctx = lax.axis_size("ctx")
    tok, width = queries.shape
    kv_width = keys.shape[1]
    features = hidden.shape[1]
    back = n_ctx // 2 // PLANE
    ctx = lax.axis_index("ctx").astype(jnp.int32)
    idx = ctx.reshape(1)
    lanes = width // PLANE
    plane_rows = PLANE * tok

    outs = pl.pallas_call(
        prepare_kernel,
        out_shape=[jax.ShapeDtypeStruct((tok, 2 * HD), BF16)] * PLANE
        + [jax.ShapeDtypeStruct((tok, 2 * lanes), BF16)] * PLANE,
        in_specs=[whole(SMEM)] + [whole(pltpu.HBM)] * 10,
        out_specs=[whole(pltpu.HBM)] * (2 * PLANE),
        scratch_shapes=[
            VMEM((PLANE, tok, 2 * HD), BF16),
            VMEM(hidden.shape, BF16),
            VMEM(value_weight.shape, BF16),
            VMEM(keys.shape, BF16),
            VMEM((PLANE, tok, lanes), BF16),
            VMEM((PLANE, tok, lanes), BF16),
            VMEM((PLANE, tok, 2 * lanes), BF16),
            SMEM(seq_lengths.shape, jnp.int32),
            SMEM(group_ids.shape, jnp.int32),
            SMEM(rewards.shape, F32),
            VMEM((1, tok), F32),
            VMEM((1, tok), F32),
            pltpu.SemaphoreType.DMA((7, PLANE)),
            pltpu.SemaphoreType.DMA((5,)),
        ],
        **small("prepare", mib=60),
    )(
        idx, seq_lengths, group_ids, rewards, new_logp[None, :], old_logp[None, :],
        hidden, value_weight, keys, queries, out_grad,
    )
    kv, q_oc = list(outs[:PLANE]), list(outs[PLANE:])

    q_oc = [q_oc[0]] + [crossed(q_oc[r], r) for r in range(1, PLANE)]
    kv = [kv[0]] + [crossed(kv[r], r) for r in range(1, PLANE)]
    kv = pl.pallas_call(
        join_kernel,
        out_shape=jax.ShapeDtypeStruct((plane_rows, 2 * HD), BF16),
        in_specs=[whole(VMEM)] * PLANE,
        out_specs=whole(VMEM),
        **small("join", 10**10),
    )(*kv)
    kvs = [kv] + [shifted(kv, w * PLANE) for w in range(1, back + 1)]
    late_hidden, q_oc[1] = lax.optimization_barrier((hidden, q_oc[1]))
    hidden_c = crossed(late_hidden, 1)
    late_hidden, q_oc, hidden_c = lax.optimization_barrier((hidden, q_oc, hidden_c))
    hidden_y = crossed(late_hidden, 2)

    outs = list(forward(idx, seq_lengths, q_oc, kvs))
    attn, own_v, backs_v = outs[:PLANE], outs[PLANE], outs[PLANE + 1:PLANE + 1 + back]
    probs, om, inner = outs[PLANE + 1 + back:]
    got_v = [shifted(backs_v[w - 1], -w * PLANE) for w in range(1, back + 1)]
    attn = [attn[0], attn[1]] + [crossed(attn[r], r) for r in range(2, PLANE)]
    outs = list(backward(idx, seq_lengths, q_oc, kvs, probs, om, inner, attn[1]))
    outs, got_v, attn, hidden_y = lax.optimization_barrier((outs, got_v, attn, hidden_y))
    hidden_cy = crossed(hidden_y, 1)
    qg, own_k, backs_k = outs[:PLANE], outs[PLANE], outs[PLANE + 1:]
    got_k = [shifted(backs_k[w - 1], -w * PLANE) for w in range(1, back + 1)]
    rows = features // n_ctx
    packed = (rows // 2) % 16 == 0
    piece = (rows // 2, 2 * HD) if packed else (rows, HD)
    cot, wv = pl.pallas_call(
        functools.partial(wv_kernel, back=back, n_ctx=n_ctx),
        out_shape=[
            jax.ShapeDtypeStruct((HD, plane_rows), BF16),
            jax.ShapeDtypeStruct((n_ctx,) + piece, BF16),
        ],
        in_specs=[whole(SMEM)] + [whole(VMEM)] * (1 + back + PLANE),
        out_specs=[whole(VMEM)] * 2,
        **small("wv"),
    )(idx, own_v, *got_v, hidden, hidden_c, hidden_y, hidden_cy)
    qg = [qg[0], qg[1]] + [crossed(qg[r], r) for r in range(2, PLANE)]
    parts = pl.pallas_call(
        functools.partial(sum_kernel, back=back),
        out_shape=[
            jax.ShapeDtypeStruct((2 * HD, tok + 2 * lanes if r == 1 else tok), BF16) for r in range(PLANE)
        ],
        in_specs=[whole(SMEM)] + [whole(VMEM)] * (3 + back),
        out_specs=[whole(VMEM)] * PLANE,
        scratch_shapes=[VMEM((2 * HD, plane_rows), BF16)],
        **small("sum", 10**10),
    )(idx, own_k, *got_k, cot, qg[1])
    parts, qg[2:] = lax.optimization_barrier((list(parts), qg[2:]))
    parts = [parts[0]] + [crossed(parts[r], r) for r in range(1, PLANE)]
    attn, q_grad = pl.pallas_call(
        results_kernel,
        out_shape=[jax.ShapeDtypeStruct((tok, width), BF16)] * 2,
        in_specs=[whole(SMEM)] + [whole(VMEM)] * (2 * PLANE - 1),
        out_specs=[whole(VMEM)] * 2,
        **small("results", 10**9),
    )(idx, parts[1], attn[0], *attn[2:], qg[0], *qg[2:])
    wv = lax.all_to_all(wv, "ctx", 0, 0, tiled=True)
    k_grad, x_grad = pl.pallas_call(
        finish_kernel,
        out_shape=[
            jax.ShapeDtypeStruct((tok, kv_width), BF16),
            jax.ShapeDtypeStruct((tok, features), BF16),
        ],
        in_specs=[whole(SMEM)] + [whole(VMEM)] * (1 + PLANE),
        out_specs=[whole(VMEM)] * 2,
        scratch_shapes=[VMEM((PLANE, tok, 2 * HD), BF16)],
        **small("finish"),
    )(idx, value_weight, *parts)

    wv_grad = pl.pallas_call(
        wv_sum_kernel,
        out_shape=jax.ShapeDtypeStruct((rows, kv_width), F32),
        in_specs=[whole(VMEM)],
        out_specs=whole(VMEM),
        **small("wv_sum", 10**10),
    )(wv)
    return (attn, q_grad, k_grad, x_grad, wv_grad)


def solution(mesh):
    rows = P(("groups", "ctx"), None)
    flat = P(("groups", "ctx"))
    placed = (rows, rows, rows, P(), rows, flat, flat, P("groups"), P("groups"), P("groups"))
    return jax.shard_map(
        shards, mesh=mesh, in_specs=placed, out_specs=(rows,) * 5, check_vma=False
    )
```

```python
import functools
import math

import jax
import jax.numpy as jnp
from jax import lax
from jax.experimental import pallas as pl
from jax.experimental.pallas import tpu as pltpu
from jax.sharding import PartitionSpec as P

HD = 64
PLANE = 4
SCALE = 1.0 / math.sqrt(HD)
BIG_NEGATIVE = -1e30
VMEM = pltpu.VMEM
SMEM = pltpu.SMEM
BF16 = jnp.bfloat16
F32 = jnp.float32


def dot(a, b):
    return lax.dot_general(a, b, (((1,), (0,)), ((), ())), preferred_element_type=F32)


def whole(space):
    return pl.BlockSpec(memory_space=space)


def small(name, flops=10**6, mib=12):
    return dict(
        name=name,
        compiler_params=pltpu.CompilerParams(vmem_limit_bytes=mib * 2**20),
        cost_estimate=pl.CostEstimate(flops=flops, bytes_accessed=2**16, transcendentals=0),
    )


def token_weights(idx, tok, seq_ref, rew_ref, gid_ref, new_ref, old_ref):
    nseq = seq_ref.shape[0]
    pos = idx * tok + lax.broadcasted_iota(jnp.int32, (1, tok), 1)
    reward = jnp.zeros(pos.shape, F32)
    total = jnp.zeros(pos.shape, F32)
    count = jnp.ones(pos.shape, F32)
    begin = jnp.int32(0)
    for i in range(nseq):
        gsum = F32(0)
        gcount = F32(0)
        for j in range(nseq):
            same = gid_ref[j] == gid_ref[i]
            gsum = gsum + jnp.where(same, rew_ref[j], 0.0)
            gcount = gcount + jnp.where(same, 1.0, 0.0)
        here = pos >= begin
        reward = jnp.where(here, rew_ref[i], reward)
        total = jnp.where(here, gsum, total)
        count = jnp.where(here, gcount, count)
        begin = begin + seq_ref[i]
    return (total / count - reward) * jnp.exp(new_ref[...] - old_ref[...])


def prepare_kernel(
    idx_ref, seq_hbm, gid_hbm, rew_hbm, new_hbm, old_hbm, hidden_hbm, weight_hbm, keys_hbm, q_hbm, og_hbm, *rest
):
    kv_refs, q_refs = rest[:PLANE], rest[PLANE:2 * PLANE]
    (parts, hidden, weight, keys, q_in, og_in, q_out, seq_ref, gid_ref, rew_ref, new_ref, old_ref, sems,
     scalar_sems) = rest[2 * PLANE:]
    _, tok, lanes = q_in.shape
    place = idx_ref[0] % PLANE
    depth = hidden.shape[1] // PLANE
    value_copies = []
    query_copies = []
    for c in range(PLANE):
        at = pl.ds(c * depth, depth)
        value_copies.append((
            pltpu.make_async_copy(weight_hbm.at[at, :], weight.at[at, :], sems.at[0, c]),
            pltpu.make_async_copy(hidden_hbm.at[:, at], hidden.at[:, at], sems.at[1, c]),
        ))
        at = pl.ds(pl.multiple_of((place ^ c) * lanes, lanes), lanes)
        query_copies.append((
            pltpu.make_async_copy(q_hbm.at[:, at], q_in.at[c], sems.at[2, c]),
            pltpu.make_async_copy(og_hbm.at[:, at], og_in.at[c], sems.at[3, c]),
        ))
    key_copy = pltpu.make_async_copy(keys_hbm, keys, sems.at[4, 0])
    for pair in value_copies:
        for copy in pair:
            copy.start()
    key_copy.start()
    for pair in query_copies:
        for copy in pair:
            copy.start()
    scalars = [
        pltpu.make_async_copy(source, target, scalar_sems.at[i])
        for i, (source, target) in enumerate((
            (seq_hbm, seq_ref), (gid_hbm, gid_ref), (rew_hbm, rew_ref), (new_hbm, new_ref), (old_hbm, old_ref)
        ))
    ]
    for copy in scalars:
        copy.start()
    for copy in scalars:
        copy.wait()
    token = token_weights(idx_ref[0], tok, seq_ref, rew_ref, gid_ref, new_ref, old_ref)
    token = jnp.transpose(jnp.broadcast_to(token, (tok, tok)))[:, 0:1]
    values = jnp.zeros((hidden.shape[0], weight.shape[1]), F32)
    for c, pair in enumerate(value_copies):
        for copy in pair:
            copy.wait()
        at = slice(c * depth, (c + 1) * depth)
        values = values + dot(hidden[:, at], weight[at, :])
    values = values.astype(BF16)
    key_copy.wait()
    for g in range(PLANE):
        at = slice(g * HD, (g + 1) * HD)
        parts[g] = jnp.concatenate([keys[:, at], values[:, at]], axis=1)
    results = [pltpu.make_async_copy(parts.at[place ^ r], kv_refs[r], sems.at[5, r]) for r in range(PLANE)]
    for copy in results:
        copy.start()
    for r, pair in enumerate(query_copies):
        for copy in pair:
            copy.wait()
        q_out[r, :, 0:lanes] = (q_in[r].astype(F32) * SCALE).astype(BF16)
        q_out[r, :, lanes:2 * lanes] = (og_in[r].astype(F32) * token).astype(BF16)
        results.append(pltpu.make_async_copy(q_out.at[r], q_refs[r], sems.at[6, r]))
        results[-1].start()
    for copy in results:
        copy.wait()


def join_kernel(*refs):
    tok = refs[0].shape[0]
    for r in range(PLANE):
        refs[PLANE][r * tok:(r + 1) * tok, :] = refs[r][...]


def twice(x):
    return jnp.concatenate([x, x], axis=1)


def first_of(position, seq_ref):
    start = position * 0
    begin = jnp.int32(0)
    for i in range(seq_ref.shape[0]):
        start = jnp.where(position >= begin, begin, start)
        begin = begin + seq_ref[i]
    return start


def in_twos(steps, begin, two, one):
    def body(i, carry):
        two(2 * i)
        return carry

    lax.fori_loop(begin, steps // 2, body, 0)
    pl.when(steps % 2 == 1)(lambda: one(steps - 1))


def head_pairs(per_pass, blk):
    return [
        (slice(2 * a * blk, (2 * a + 1) * blk), slice((2 * a + 1) * blk, (2 * a + 2) * blk))
        for a in range(per_pass // 2)
    ]


def row_groups(per_pass, blk):
    rows = min(per_pass, 4) * blk
    return [slice(i, i + rows) for i in range(0, per_pass * blk, rows)]


def lanes_of(h0, a, offset=0):
    return slice(offset + (h0 + 2 * a) * HD, offset + (h0 + 2 * a + 2) * HD)


def gather_queries(in_refs, place, q_in):
    tok = in_refs[0].shape[0]
    for r in range(PLANE):
        q_in[pl.ds(pl.multiple_of((place ^ r) * tok, tok), tok), :] = in_refs[r][...]


def key_blocks(kv_refs, place, tok, back):
    for w in range(back + 1):
        for r in range(PLANE):
            at = pl.ds(pl.multiple_of(((back - w) * PLANE + (place ^ r)) * tok, tok), tok)
            yield at, kv_refs[w][r * tok:(r + 1) * tok, :].astype(F32)


def send_back(acc, own_ref, back_refs, rows_all):
    back = len(back_refs)
    own_ref[...] = acc[:, back * rows_all:]
    for w in range(1, back + 1):
        back_refs[w - 1][...] = acc[:, (back - w) * rows_all:(back - w + 1) * rows_all].astype(BF16)


def forward_kernel(idx_ref, seq_ref, *rest, back, heads, per_pass):
    in_refs = rest[:PLANE]
    kv_refs = rest[PLANE:PLANE + back + 1]
    rest = rest[PLANE + back + 1:]
    out_refs = rest[:PLANE]
    own_ref = rest[PLANE]
    back_refs = rest[PLANE + 1:PLANE + 1 + back]
    probs, om, inner, q_in, res, k2t, v2, qm, ot, start, bias, score, o_acc, top, acc_v = rest[PLANE + 1 + back:]
    tok = in_refs[0].shape[0]
    rows_all = PLANE * tok
    blk = rows_all // 2
    width = heads * HD
    passes = heads // per_pass
    pairs = 2 * back + 1
    plane = idx_ref[0] // PLANE
    place = idx_ref[0] % PLANE
    base = (plane - back) * 2

    gather_queries(in_refs, place, q_in)
    lower = lax.broadcasted_iota(jnp.int32, (tok, 2 * HD), 1) < HD
    for at, part in key_blocks(kv_refs, place, tok, back):
        v2[at, 0:2 * HD] = jnp.where(lower, pltpu.roll(part, HD, 1), part).astype(BF16)
        key_t = jnp.transpose(part).astype(BF16)[:HD]
        k2t[:, at] = jnp.concatenate([key_t, key_t], axis=0)
    v2[:, 2 * HD:] = jnp.ones((v2.shape[0], 2 * HD), BF16)
    acc_v[...] = jnp.zeros_like(acc_v)
    left = lax.broadcasted_iota(jnp.int32, (blk, 2 * HD), 1) < HD
    pairs_at = head_pairs(per_pass, blk)

    def block(b, carry):
        pair_hi = plane * 2 + b
        first = pair_hi * blk
        start[...] = first_of(first + lax.broadcasted_iota(jnp.int32, (blk, 2 * HD), 0), seq_ref)
        start_hi = first_of(first + blk - 1, seq_ref)
        steps = jnp.clip(pair_hi - first_of(first, seq_ref) // blk + 1, 2, pairs)
        q_rows = pl.ds(pl.multiple_of(b * blk, blk), blk)

        for h0 in range(0, heads, per_pass):
            kept = b * passes + h0 // per_pass
            for a, (even, odd) in enumerate(pairs_at):
                q2 = q_in[q_rows, lanes_of(h0, a)]
                qm[even, :] = jnp.where(left, q2, jnp.zeros_like(q2))
                qm[odd, :] = jnp.where(left, jnp.zeros_like(q2), q2)

            def scores(step, count, first_time=False, edges=True):
                k_t = [
                    k2t[:, pl.ds(pl.multiple_of((pair_hi - step - c - base) * blk, blk), blk)] for c in range(count)
                ]
                if edges:
                    for c in range(count):
                        key_pos = (pair_hi - step - c) * blk + lax.broadcasted_iota(jnp.int32, (blk, blk), 1)
                        tok_pos = first + lax.broadcasted_iota(jnp.int32, (blk, blk), 0)
                        seen = (key_pos >= twice(start[...])) & (key_pos <= tok_pos)
                        bias[c] = jnp.where(seen, 0.0, BIG_NEGATIVE)
                for at in row_groups(per_pass, blk):
                    most = None if first_time else top[at, :]
                    for c in range(count):
                        s = dot(qm[at, :], k_t[c])
                        if edges:
                            s = s + jnp.concatenate([bias[c]] * min(per_pass, 4), axis=0)
                        score[step + c, at, :] = s
                        one = jnp.maximum(s[:, :2 * HD], s[:, 2 * HD:])
                        most = one if most is None else jnp.maximum(most, one)
                    top[at, :] = most

            def outputs(step, count, first_time=False):
                vv = v2[pl.ds(pl.multiple_of((pair_hi - step - count + 1 - base) * blk, blk), count * blk), :]
                for at in row_groups(per_pass, blk):
                    most = twice(top[at, :])
                    ebs = []
                    for c in reversed(range(count)):
                        eb = jnp.exp(score[step + c, at, :] - most).astype(BF16)
                        probs[kept * pairs + step + c, at, :] = eb
                        ebs.append(eb)
                    out = dot(jnp.concatenate(ebs, axis=1), vv)
                    o_acc[at, :] = out if first_time else o_acc[at, :] + out

            def value_grad(step, count):
                for c in range(count):
                    rows = pl.ds(pl.multiple_of((pair_hi - step - c - base) * blk, blk), blk)
                    acc_v[:, rows] = acc_v[:, rows] + dot(ot[...], probs[kept * pairs + step + c])

            def more_scores(step):
                inside = (pair_hi - step - 1) * blk >= start_hi
                pl.when(inside)(functools.partial(scores, step, 2, edges=False))
                pl.when(jnp.logical_not(inside))(functools.partial(scores, step, 2))

            scores(0, 2, first_time=True)
            in_twos(steps, 1, more_scores, functools.partial(scores, count=1))
            top[...] = jnp.broadcast_to(jnp.max(top[...], axis=1, keepdims=True), top.shape)
            outputs(0, 2, first_time=True)
            in_twos(steps, 1, functools.partial(outputs, count=2), functools.partial(outputs, count=1))
            for a, pair_at in enumerate(pairs_at):
                o2 = q_in[q_rows, lanes_of(h0, a, width)].astype(F32)
                out = []
                scaled = []
                for side, at in enumerate(pair_at):
                    inv = 1.0 / o_acc[at, 2 * HD:]
                    out.append(o_acc[at, 0:2 * HD] * inv)
                    mine = jnp.where(left if side == 0 else jnp.logical_not(left), o2, 0.0) * inv
                    inner[kept, at, :] = jnp.broadcast_to(
                        jnp.sum(mine * out[side], axis=1, keepdims=True), (blk, 2 * HD)
                    )
                    scaled.append(mine)
                    om[kept, at, :] = mine.astype(BF16)
                res[q_rows, lanes_of(h0, a)] = jnp.where(left, out[0], out[1]).astype(BF16)
                o2t = jnp.transpose(scaled[0] + scaled[1]).astype(BF16)
                ot[:, pair_at[0]] = o2t[:HD]
                ot[:, pair_at[1]] = o2t[HD:]

            in_twos(steps, 0, functools.partial(value_grad, count=2), functools.partial(value_grad, count=1))
        return carry

    lax.fori_loop(0, 2, block, 0)
    send_back(acc_v, own_ref, back_refs, rows_all)
    for r in range(PLANE):
        out_refs[r][...] = res[pl.ds(pl.multiple_of((place ^ r) * tok, tok), tok), :]


def backward_kernel(idx_ref, seq_ref, *rest, back, heads, per_pass):
    in_refs = rest[:PLANE]
    kv_refs = rest[PLANE:PLANE + back + 1]
    probs, om, inner, attn_ref = rest[PLANE + back + 1:PLANE + back + 5]
    rest = rest[PLANE + back + 5:]
    out_refs = rest[:PLANE]
    own_ref = rest[PLANE]
    back_refs = rest[PLANE + 1:PLANE + 1 + back]
    q_in, res, k2, v2t, qt, dscore, q_acc, acc_k = rest[PLANE + 1 + back:]
    tok = in_refs[0].shape[0]
    rows_all = PLANE * tok
    blk = rows_all // 2
    passes = heads // per_pass
    pairs = 2 * back + 1
    plane = idx_ref[0] // PLANE
    place = idx_ref[0] % PLANE
    base = (plane - back) * 2

    gather_queries(in_refs, place, q_in)
    lower = lax.broadcasted_iota(jnp.int32, (tok, 2 * HD), 1) < HD
    for at, part in key_blocks(kv_refs, place, tok, back):
        k2[at, :] = jnp.where(lower, part, pltpu.roll(part, HD, 1)).astype(BF16)
        value_t = jnp.transpose(part).astype(BF16)[HD:]
        v2t[:, at] = jnp.concatenate([value_t, value_t], axis=0)
    acc_k[...] = jnp.zeros_like(acc_k)
    left = lax.broadcasted_iota(jnp.int32, (blk, 2 * HD), 1) < HD
    pairs_at = head_pairs(per_pass, blk)

    def block(b, carry):
        pair_hi = plane * 2 + b
        steps = jnp.clip(pair_hi - first_of(pair_hi * blk, seq_ref) // blk + 1, 2, pairs)
        q_rows = pl.ds(pl.multiple_of(b * blk, blk), blk)

        for h0 in range(0, heads, per_pass):
            kept = b * passes + h0 // per_pass
            for a, (even, odd) in enumerate(pairs_at):
                q2t = jnp.transpose(q_in[q_rows, lanes_of(h0, a)].astype(F32)).astype(BF16)
                qt[:, even] = q2t[:HD]
                qt[:, odd] = q2t[HD:]
            def gradients(step, count, first_time=False):
                lowest = pair_hi - step - count + 1 - base
                kk = k2[pl.ds(pl.multiple_of(lowest * blk, blk), count * blk), :]
                rows = [pl.ds(pl.multiple_of((pair_hi - step - c - base) * blk, blk), blk) for c in range(count)]
                v_t = [v2t[:, at] for at in rows]
                for at in row_groups(per_pass, blk):
                    shift = twice(inner[kept, at, :])
                    each = []
                    for c in reversed(range(count)):
                        e = probs[kept * pairs + step + c, at, :].astype(F32)
                        ds = (e * (dot(om[kept, at, :], v_t[c]) - shift)).astype(BF16)
                        dscore[c, at, :] = ds
                        each.append(ds)
                    dq = dot(jnp.concatenate(each, axis=1), kk)
                    q_acc[at, :] = dq if first_time else q_acc[at, :] + dq
                for c in range(count):
                    acc_k[:, rows[c]] = acc_k[:, rows[c]] + dot(qt[...], dscore[c])

            gradients(0, 2, first_time=True)
            in_twos(steps, 1, functools.partial(gradients, count=2), functools.partial(gradients, count=1))
            for a, (even, odd) in enumerate(pairs_at):
                qg = jnp.where(left, q_acc[even, :], q_acc[odd, :]) * SCALE
                res[q_rows, lanes_of(h0, a)] = qg.astype(BF16)
        return carry

    lax.fori_loop(0, 2, block, 0)
    send_back(acc_k, own_ref, back_refs, rows_all)
    for r in range(PLANE):
        mine = res[pl.ds(pl.multiple_of((place ^ r) * tok, tok), tok), :]
        if r == 1:
            mine = jnp.concatenate([attn_ref[...], mine], axis=1)
        out_refs[r][...] = mine


def attention_sizes(q_oc, kvs):
    tok, width2 = q_oc[0].shape
    rows = PLANE * tok
    back = len(kvs) - 1
    heads = width2 // 2 // HD
    blk = rows // 2
    pairs = 2 * back + 1
    per_pass = heads
    while per_pass > 2 and pairs * blk * per_pass * blk * 4 > 12 * 2**20:
        per_pass //= 2
    return tok, width2, rows, back, heads, blk, pairs, per_pass


def kernel_params(name, held, flops):
    return dict(
        name=name,
        compiler_params=pltpu.CompilerParams(vmem_limit_bytes=min(60 * 2**20, held)),
        cost_estimate=pl.CostEstimate(flops=flops, bytes_accessed=2**20, transcendentals=0),
    )


def forward(idx, seq, q_oc, kvs):
    tok, width2, rows, back, heads, blk, pairs, per_pass = attention_sizes(q_oc, kvs)
    cols = per_pass * blk
    keys = rows * (back + 1)
    kept = 2 * heads // per_pass
    held = pairs * blk * cols * 4 + kept * pairs * blk * cols * 2 + 16 * 2**20
    return pl.pallas_call(
        functools.partial(forward_kernel, back=back, heads=heads, per_pass=per_pass),
        out_shape=(
            [jax.ShapeDtypeStruct((tok, width2 // 2), BF16)] * PLANE
            + [jax.ShapeDtypeStruct((HD, rows), F32)]
            + [jax.ShapeDtypeStruct((HD, rows), BF16)] * back
            + [
                jax.ShapeDtypeStruct((kept * pairs, cols, blk), BF16),
                jax.ShapeDtypeStruct((kept, cols, 2 * HD), BF16),
                jax.ShapeDtypeStruct((kept, cols, 2 * HD), F32),
            ]
        ),
        in_specs=[whole(SMEM)] * 2 + [whole(VMEM)] * (PLANE + len(kvs)),
        out_specs=[whole(VMEM)] * (PLANE + 1 + back + 3),
        scratch_shapes=[
            VMEM((rows, width2), BF16),
            VMEM((rows, width2 // 2), BF16),
            VMEM((2 * HD, keys), BF16),
            VMEM((keys, 4 * HD), BF16),
            VMEM((cols, 2 * HD), BF16),
            VMEM((HD, cols), BF16),
            VMEM((blk, 2 * HD), jnp.int32),
            VMEM((2, blk, blk), F32),
            VMEM((pairs, cols, blk), F32),
            VMEM((cols, 4 * HD), F32),
            VMEM((cols, 2 * HD), F32),
            VMEM((HD, keys), F32),
        ],
        **kernel_params("forward", held, 20 * keys * rows * width2 // 2),
    )(idx, seq, *q_oc, *kvs)


def backward(idx, seq, q_oc, kvs, probs, om, inner, attn):
    tok, width2, rows, back, heads, blk, pairs, per_pass = attention_sizes(q_oc, kvs)
    cols = per_pass * blk
    keys = rows * (back + 1)
    held = probs.size * 2 + 16 * 2**20
    return pl.pallas_call(
        functools.partial(backward_kernel, back=back, heads=heads, per_pass=per_pass),
        out_shape=(
            [jax.ShapeDtypeStruct((tok, width2 if r == 1 else width2 // 2), BF16) for r in range(PLANE)]
            + [jax.ShapeDtypeStruct((HD, rows), F32)]
            + [jax.ShapeDtypeStruct((HD, rows), BF16)] * back
        ),
        in_specs=[whole(SMEM)] * 2 + [whole(VMEM)] * (PLANE + len(kvs) + 4),
        out_specs=[whole(VMEM)] * (PLANE + 1 + back),
        scratch_shapes=[
            VMEM((rows, width2), BF16),
            VMEM((rows, width2 // 2), BF16),
            VMEM((keys, 2 * HD), BF16),
            VMEM((2 * HD, keys), BF16),
            VMEM((HD, cols), BF16),
            VMEM((2, cols, blk), BF16),
            VMEM((cols, 2 * HD), F32),
            VMEM((HD, keys), F32),
        ],
        **kernel_params("backward", held, keys * rows),
    )(idx, seq, *q_oc, *kvs, probs, om, inner, attn)


def sum_kernel(idx_ref, own_ref, *rest, back):
    got_refs = rest[:back]
    cot_ref, res_ref = rest[back:back + 2]
    part_refs = rest[back + 2:back + 2 + PLANE]
    total = rest[back + 2 + PLANE]
    tok = part_refs[0].shape[1]
    place = idx_ref[0] % PLANE
    summed = own_ref[...]
    for got in got_refs:
        summed = summed + got[...].astype(F32)
    total[0:HD, :] = summed.astype(BF16)
    total[HD:2 * HD, :] = cot_ref[...]
    for r in range(PLANE):
        part_refs[r][:, 0:tok] = total[:, pl.ds(pl.multiple_of((place ^ r) * tok, tok), tok)]
    part_refs[1][:, tok:] = res_ref[...]


def wv_kernel(idx_ref, own_ref, *refs, back, n_ctx):
    got_refs, hidden_refs = refs[:back], refs[back:back + PLANE]
    cot_ref, wv_ref = refs[back + PLANE:]
    tok, features = hidden_refs[0].shape
    place = idx_ref[0] % PLANE
    summed = own_ref[...]
    for got in got_refs:
        summed = summed + got[...].astype(F32)
    cot_ref[...] = summed.astype(BF16)
    wv = jnp.zeros((HD, features), F32)
    for r in range(PLANE):
        at = pl.ds(pl.multiple_of((place ^ r) * tok, tok), tok)
        wv = wv + dot(cot_ref[:, at], hidden_refs[r][...])
    rows = features // n_ctx
    if wv_ref.shape[2] == 2 * HD:
        wv = jnp.transpose(wv.astype(BF16))
        for d in range(n_ctx):
            one = wv[d * rows:(d + 1) * rows]
            wv_ref[d] = jnp.concatenate([one[:rows // 2], one[rows // 2:]], axis=1)
    else:
        wv = jnp.transpose(wv)
        for d in range(n_ctx):
            wv_ref[d] = wv[d * rows:(d + 1) * rows].astype(BF16)


def results_kernel(idx_ref, part_ref, *refs):
    in_refs, out_refs = refs[:-2], refs[-2:]
    place = idx_ref[0] % PLANE
    lanes = in_refs[0].shape[1]
    tok = part_ref.shape[1] - 2 * lanes
    for i, out_ref in enumerate(out_refs):
        rest = list(in_refs[i * (PLANE - 1):(i + 1) * (PLANE - 1)])
        for r in range(PLANE):
            at = pl.ds(pl.multiple_of((place ^ r) * lanes, lanes), lanes)
            if r == 1:
                out_ref[:, at] = part_ref[:, tok + i * lanes:tok + (i + 1) * lanes]
            else:
                out_ref[:, at] = rest.pop(0)[...]


def finish_kernel(idx_ref, weight_ref, *rest):
    part_refs = rest[:PLANE]
    kg_ref, xg_ref, parts = rest[PLANE:]
    place = idx_ref[0] % PLANE
    for r in range(PLANE):
        tok = part_refs[0].shape[1]
        parts[place ^ r] = jnp.transpose(part_refs[r][:, 0:tok].astype(F32)).astype(BF16)
    kg_ref[...] = jnp.concatenate([parts[g, :, 0:HD] for g in range(PLANE)], axis=1)
    value_cot = jnp.concatenate([parts[g, :, HD:2 * HD] for g in range(PLANE)], axis=1)
    xg_ref[...] = lax.dot_general(
        value_cot, weight_ref[...], (((1,), (1,)), ((), ())), preferred_element_type=F32
    ).astype(BF16)


def wv_sum_kernel(wv_ref, out_ref):
    n_ctx, depth, lanes = wv_ref.shape
    sums = []
    for g in range(PLANE):
        total = wv_ref[g].astype(F32)
        for d in range(g + PLANE, n_ctx, PLANE):
            total = total + wv_ref[d].astype(F32)
        sums.append(total)
    for side in range(lanes // HD):
        out_ref[side * depth:(side + 1) * depth, :] = jnp.concatenate(
            [total[:, side * HD:(side + 1) * HD] for total in sums], axis=1
        )


def shifted(x, by):
    n = lax.axis_size("ctx")
    return lax.ppermute(x, "ctx", [(i, i + by) for i in range(n) if 0 <= i + by < n])


def crossed(x, by):
    n = lax.axis_size("ctx")
    return lax.ppermute(x, "ctx", [(i, i ^ by) for i in range(n)])


def in_plane(x):
    n = lax.axis_size("ctx")
    planes = [list(range(i, i + PLANE)) for i in range(0, n, PLANE)]
    return lax.all_to_all(x, "ctx", 0, 0, axis_index_groups=planes, tiled=True)


def shards(
    queries, keys, hidden, value_weight, out_grad, new_logp, old_logp, rewards, group_ids, seq_lengths
):
    n_ctx = lax.axis_size("ctx")
    tok, width = queries.shape
    kv_width = keys.shape[1]
    features = hidden.shape[1]
    back = n_ctx // 2 // PLANE
    ctx = lax.axis_index("ctx").astype(jnp.int32)
    idx = ctx.reshape(1)
    lanes = width // PLANE
    plane_rows = PLANE * tok

    outs = pl.pallas_call(
        prepare_kernel,
        out_shape=[jax.ShapeDtypeStruct((tok, 2 * HD), BF16)] * PLANE
        + [jax.ShapeDtypeStruct((tok, 2 * lanes), BF16)] * PLANE,
        in_specs=[whole(SMEM)] + [whole(pltpu.HBM)] * 10,
        out_specs=[whole(pltpu.HBM)] * (2 * PLANE),
        scratch_shapes=[
            VMEM((PLANE, tok, 2 * HD), BF16),
            VMEM(hidden.shape, BF16),
            VMEM(value_weight.shape, BF16),
            VMEM(keys.shape, BF16),
            VMEM((PLANE, tok, lanes), BF16),
            VMEM((PLANE, tok, lanes), BF16),
            VMEM((PLANE, tok, 2 * lanes), BF16),
            SMEM(seq_lengths.shape, jnp.int32),
            SMEM(group_ids.shape, jnp.int32),
            SMEM(rewards.shape, F32),
            VMEM((1, tok), F32),
            VMEM((1, tok), F32),
            pltpu.SemaphoreType.DMA((7, PLANE)),
            pltpu.SemaphoreType.DMA((5,)),
        ],
        **small("prepare", mib=60),
    )(
        idx, seq_lengths, group_ids, rewards, new_logp[None, :], old_logp[None, :],
        hidden, value_weight, keys, queries, out_grad,
    )
    kv, q_oc = list(outs[:PLANE]), list(outs[PLANE:])

    q_oc = [q_oc[0]] + [crossed(q_oc[r], r) for r in range(1, PLANE)]
    kv = [kv[0]] + [crossed(kv[r], r) for r in range(1, PLANE)]
    kv = pl.pallas_call(
        join_kernel,
        out_shape=jax.ShapeDtypeStruct((plane_rows, 2 * HD), BF16),
        in_specs=[whole(VMEM)] * PLANE,
        out_specs=whole(VMEM),
        **small("join", 10**10),
    )(*kv)
    kvs = [kv] + [shifted(kv, w * PLANE) for w in range(1, back + 1)]
    late_hidden, q_oc[1] = lax.optimization_barrier((hidden, q_oc[1]))
    hidden_c = crossed(late_hidden, 1)
    late_hidden, q_oc, hidden_c = lax.optimization_barrier((hidden, q_oc, hidden_c))
    hidden_y = crossed(late_hidden, 2)

    outs = list(forward(idx, seq_lengths, q_oc, kvs))
    attn, own_v, backs_v = outs[:PLANE], outs[PLANE], outs[PLANE + 1:PLANE + 1 + back]
    probs, om, inner = outs[PLANE + 1 + back:]
    got_v = [shifted(backs_v[w - 1], -w * PLANE) for w in range(1, back + 1)]
    attn = [attn[0], attn[1]] + [crossed(attn[r], r) for r in range(2, PLANE)]
    outs = list(backward(idx, seq_lengths, q_oc, kvs, probs, om, inner, attn[1]))
    outs, got_v, attn, hidden_y = lax.optimization_barrier((outs, got_v, attn, hidden_y))
    hidden_cy = crossed(hidden_y, 1)
    qg, own_k, backs_k = outs[:PLANE], outs[PLANE], outs[PLANE + 1:]
    got_k = [shifted(backs_k[w - 1], -w * PLANE) for w in range(1, back + 1)]
    rows = features // n_ctx
    packed = (rows // 2) % 16 == 0
    piece = (rows // 2, 2 * HD) if packed else (rows, HD)
    cot, wv = pl.pallas_call(
        functools.partial(wv_kernel, back=back, n_ctx=n_ctx),
        out_shape=[
            jax.ShapeDtypeStruct((HD, plane_rows), BF16),
            jax.ShapeDtypeStruct((n_ctx,) + piece, BF16),
        ],
        in_specs=[whole(SMEM)] + [whole(VMEM)] * (1 + back + PLANE),
        out_specs=[whole(VMEM)] * 2,
        **small("wv"),
    )(idx, own_v, *got_v, hidden, hidden_c, hidden_y, hidden_cy)
    qg = [qg[0], qg[1]] + [crossed(qg[r], r) for r in range(2, PLANE)]
    parts = pl.pallas_call(
        functools.partial(sum_kernel, back=back),
        out_shape=[
            jax.ShapeDtypeStruct((2 * HD, tok + 2 * lanes if r == 1 else tok), BF16) for r in range(PLANE)
        ],
        in_specs=[whole(SMEM)] + [whole(VMEM)] * (3 + back),
        out_specs=[whole(VMEM)] * PLANE,
        scratch_shapes=[VMEM((2 * HD, plane_rows), BF16)],
        **small("sum", 10**10),
    )(idx, own_k, *got_k, cot, qg[1])
    parts, qg[2:] = lax.optimization_barrier((list(parts), qg[2:]))
    parts = [parts[0]] + [crossed(parts[r], r) for r in range(1, PLANE)]
    attn, q_grad = pl.pallas_call(
        results_kernel,
        out_shape=[jax.ShapeDtypeStruct((tok, width), BF16)] * 2,
        in_specs=[whole(SMEM)] + [whole(VMEM)] * (2 * PLANE - 1),
        out_specs=[whole(VMEM)] * 2,
        **small("results", 10**9),
    )(idx, parts[1], attn[0], *attn[2:], qg[0], *qg[2:])
    wv = lax.all_to_all(wv, "ctx", 0, 0, tiled=True)
    k_grad, x_grad = pl.pallas_call(
        finish_kernel,
        out_shape=[
            jax.ShapeDtypeStruct((tok, kv_width), BF16),
            jax.ShapeDtypeStruct((tok, features), BF16),
        ],
        in_specs=[whole(SMEM)] + [whole(VMEM)] * (1 + PLANE),
        out_specs=[whole(VMEM)] * 2,
        scratch_shapes=[VMEM((PLANE, tok, 2 * HD), BF16)],
        **small("finish"),
    )(idx, value_weight, *parts)

    wv_grad = pl.pallas_call(
        wv_sum_kernel,
        out_shape=jax.ShapeDtypeStruct((rows, kv_width), F32),
        in_specs=[whole(VMEM)],
        out_specs=whole(VMEM),
        **small("wv_sum", 10**10),
    )(wv)
    return (attn, q_grad, k_grad, x_grad, wv_grad)


def solution(mesh):
    rows = P(("groups", "ctx"), None)
    flat = P(("groups", "ctx"))
    placed = (rows, rows, rows, P(), rows, flat, flat, P("groups"), P("groups"), P("groups"))
    return jax.shard_map(
        shards, mesh=mesh, in_specs=placed, out_specs=(rows,) * 5, check_vma=False
    )
```

```python
import functools
import math

import jax
import jax.numpy as jnp
from jax import lax
from jax.experimental import pallas as pl
from jax.experimental.pallas import tpu as pltpu
from jax.sharding import PartitionSpec as P

HD = 64
PLANE = 4
SCALE = 1.0 / math.sqrt(HD)
BIG_NEGATIVE = -1e30
VMEM = pltpu.VMEM
SMEM = pltpu.SMEM
BF16 = jnp.bfloat16
F32 = jnp.float32


def dot(a, b):
    return lax.dot_general(a, b, (((1,), (0,)), ((), ())), preferred_element_type=F32)


def whole(space):
    return pl.BlockSpec(memory_space=space)


def small(name, flops=10**6, mib=12):
    return dict(
        name=name,
        compiler_params=pltpu.CompilerParams(vmem_limit_bytes=mib * 2**20),
        cost_estimate=pl.CostEstimate(flops=flops, bytes_accessed=2**16, transcendentals=0),
    )


def token_weights(idx, tok, seq_ref, rew_ref, gid_ref, new_ref, old_ref):
    nseq = seq_ref.shape[0]
    pos = idx * tok + lax.broadcasted_iota(jnp.int32, (1, tok), 1)
    reward = jnp.zeros(pos.shape, F32)
    total = jnp.zeros(pos.shape, F32)
    count = jnp.ones(pos.shape, F32)
    begin = jnp.int32(0)
    for i in range(nseq):
        gsum = F32(0)
        gcount = F32(0)
        for j in range(nseq):
            same = gid_ref[j] == gid_ref[i]
            gsum = gsum + jnp.where(same, rew_ref[j], 0.0)
            gcount = gcount + jnp.where(same, 1.0, 0.0)
        here = pos >= begin
        reward = jnp.where(here, rew_ref[i], reward)
        total = jnp.where(here, gsum, total)
        count = jnp.where(here, gcount, count)
        begin = begin + seq_ref[i]
    return (total / count - reward) * jnp.exp(new_ref[...] - old_ref[...])


def prepare_kernel(
    idx_ref, seq_hbm, gid_hbm, rew_hbm, new_hbm, old_hbm, hidden_hbm, weight_hbm, keys_hbm, q_hbm, og_hbm, *rest
):
    kv_refs, q_refs = rest[:PLANE], rest[PLANE:2 * PLANE]
    (parts, hidden, weight, keys, q_in, og_in, q_out, seq_ref, gid_ref, rew_ref, new_ref, old_ref, sems,
     scalar_sems) = rest[2 * PLANE:]
    _, tok, lanes = q_in.shape
    place = idx_ref[0] % PLANE
    depth = hidden.shape[1] // PLANE
    value_copies = []
    query_copies = []
    for c in range(PLANE):
        at = pl.ds(c * depth, depth)
        value_copies.append((
            pltpu.make_async_copy(weight_hbm.at[at, :], weight.at[at, :], sems.at[0, c]),
            pltpu.make_async_copy(hidden_hbm.at[:, at], hidden.at[:, at], sems.at[1, c]),
        ))
        at = pl.ds(pl.multiple_of((place ^ c) * lanes, lanes), lanes)
        query_copies.append((
            pltpu.make_async_copy(q_hbm.at[:, at], q_in.at[c], sems.at[2, c]),
            pltpu.make_async_copy(og_hbm.at[:, at], og_in.at[c], sems.at[3, c]),
        ))
    key_copy = pltpu.make_async_copy(keys_hbm, keys, sems.at[4, 0])
    for pair in value_copies:
        for copy in pair:
            copy.start()
    key_copy.start()
    for pair in query_copies:
        for copy in pair:
            copy.start()
    scalars = [
        pltpu.make_async_copy(source, target, scalar_sems.at[i])
        for i, (source, target) in enumerate((
            (seq_hbm, seq_ref), (gid_hbm, gid_ref), (rew_hbm, rew_ref), (new_hbm, new_ref), (old_hbm, old_ref)
        ))
    ]
    for copy in scalars:
        copy.start()
    values = jnp.zeros((hidden.shape[0], weight.shape[1]), F32)
    for c, pair in enumerate(value_copies):
        for copy in pair:
            copy.wait()
        at = slice(c * depth, (c + 1) * depth)
        values = values + dot(hidden[:, at], weight[at, :])
    values = values.astype(BF16)
    key_copy.wait()
    for g in range(PLANE):
        at = slice(g * HD, (g + 1) * HD)
        parts[g] = jnp.concatenate([keys[:, at], values[:, at]], axis=1)
    results = [pltpu.make_async_copy(parts.at[place ^ r], kv_refs[r], sems.at[5, r]) for r in range(PLANE)]
    for copy in results:
        copy.start()
    for copy in scalars:
        copy.wait()
    token = token_weights(idx_ref[0], tok, seq_ref, rew_ref, gid_ref, new_ref, old_ref)
    token = jnp.transpose(jnp.broadcast_to(token, (tok, tok)))[:, 0:1]
    for r, pair in enumerate(query_copies):
        for copy in pair:
            copy.wait()
        q_out[r, :, 0:lanes] = (q_in[r].astype(F32) * SCALE).astype(BF16)
        q_out[r, :, lanes:2 * lanes] = (og_in[r].astype(F32) * token).astype(BF16)
        results.append(pltpu.make_async_copy(q_out.at[r], q_refs[r], sems.at[6, r]))
        results[-1].start()
    for copy in results:
        copy.wait()


def join_kernel(*refs):
    tok = refs[0].shape[0]
    for r in range(PLANE):
        refs[PLANE][r * tok:(r + 1) * tok, :] = refs[r][...]


def twice(x):
    return jnp.concatenate([x, x], axis=1)


def first_of(position, seq_ref):
    start = position * 0
    begin = jnp.int32(0)
    for i in range(seq_ref.shape[0]):
        start = jnp.where(position >= begin, begin, start)
        begin = begin + seq_ref[i]
    return start


def in_twos(steps, begin, two, one):
    def body(i, carry):
        two(2 * i)
        return carry

    lax.fori_loop(begin, steps // 2, body, 0)
    pl.when(steps % 2 == 1)(lambda: one(steps - 1))


def head_pairs(per_pass, blk):
    return [
        (slice(2 * a * blk, (2 * a + 1) * blk), slice((2 * a + 1) * blk, (2 * a + 2) * blk))
        for a in range(per_pass // 2)
    ]


def row_groups(per_pass, blk):
    rows = min(per_pass, 4) * blk
    return [slice(i, i + rows) for i in range(0, per_pass * blk, rows)]


def lanes_of(h0, a, offset=0):
    return slice(offset + (h0 + 2 * a) * HD, offset + (h0 + 2 * a + 2) * HD)


def gather_queries(in_refs, place, q_in):
    tok = in_refs[0].shape[0]
    for r in range(PLANE):
        q_in[pl.ds(pl.multiple_of((place ^ r) * tok, tok), tok), :] = in_refs[r][...]


def key_blocks(kv_refs, place, tok, back):
    for w in range(back + 1):
        for r in range(PLANE):
            at = pl.ds(pl.multiple_of(((back - w) * PLANE + (place ^ r)) * tok, tok), tok)
            yield at, kv_refs[w][r * tok:(r + 1) * tok, :].astype(F32)


def send_back(acc, own_ref, back_refs, rows_all):
    back = len(back_refs)
    own_ref[...] = acc[:, back * rows_all:]
    for w in range(1, back + 1):
        back_refs[w - 1][...] = acc[:, (back - w) * rows_all:(back - w + 1) * rows_all].astype(BF16)


def forward_kernel(idx_ref, seq_ref, *rest, back, heads, per_pass):
    in_refs = rest[:PLANE]
    kv_refs = rest[PLANE:PLANE + back + 1]
    rest = rest[PLANE + back + 1:]
    out_refs = rest[:PLANE]
    own_ref = rest[PLANE]
    back_refs = rest[PLANE + 1:PLANE + 1 + back]
    probs, om, inner, q_in, res, k2t, v2, qm, ot, start, bias, score, o_acc, top, acc_v = rest[PLANE + 1 + back:]
    tok = in_refs[0].shape[0]
    rows_all = PLANE * tok
    blk = rows_all // 2
    width = heads * HD
    passes = heads // per_pass
    pairs = 2 * back + 1
    plane = idx_ref[0] // PLANE
    place = idx_ref[0] % PLANE
    base = (plane - back) * 2

    gather_queries(in_refs, place, q_in)
    lower = lax.broadcasted_iota(jnp.int32, (tok, 2 * HD), 1) < HD
    for at, part in key_blocks(kv_refs, place, tok, back):
        v2[at, 0:2 * HD] = jnp.where(lower, pltpu.roll(part, HD, 1), part).astype(BF16)
        key_t = jnp.transpose(part).astype(BF16)[:HD]
        k2t[:, at] = jnp.concatenate([key_t, key_t], axis=0)
    v2[:, 2 * HD:] = jnp.ones((v2.shape[0], 2 * HD), BF16)
    acc_v[...] = jnp.zeros_like(acc_v)
    left = lax.broadcasted_iota(jnp.int32, (blk, 2 * HD), 1) < HD
    pairs_at = head_pairs(per_pass, blk)

    def block(b, carry):
        pair_hi = plane * 2 + b
        first = pair_hi * blk
        start[...] = first_of(first + lax.broadcasted_iota(jnp.int32, (blk, 2 * HD), 0), seq_ref)
        start_hi = first_of(first + blk - 1, seq_ref)
        steps = jnp.clip(pair_hi - first_of(first, seq_ref) // blk + 1, 2, pairs)
        q_rows = pl.ds(pl.multiple_of(b * blk, blk), blk)

        for h0 in range(0, heads, per_pass):
            kept = b * passes + h0 // per_pass
            for a, (even, odd) in enumerate(pairs_at):
                q2 = q_in[q_rows, lanes_of(h0, a)]
                qm[even, :] = jnp.where(left, q2, jnp.zeros_like(q2))
                qm[odd, :] = jnp.where(left, jnp.zeros_like(q2), q2)

            def scores(step, count, first_time=False, edges=True):
                k_t = [
                    k2t[:, pl.ds(pl.multiple_of((pair_hi - step - c - base) * blk, blk), blk)] for c in range(count)
                ]
                if edges:
                    for c in range(count):
                        key_pos = (pair_hi - step - c) * blk + lax.broadcasted_iota(jnp.int32, (blk, blk), 1)
                        tok_pos = first + lax.broadcasted_iota(jnp.int32, (blk, blk), 0)
                        seen = (key_pos >= twice(start[...])) & (key_pos <= tok_pos)
                        bias[c] = jnp.where(seen, 0.0, BIG_NEGATIVE)
                for at in row_groups(per_pass, blk):
                    most = None if first_time else top[at, :]
                    for c in range(count):
                        s = dot(qm[at, :], k_t[c])
                        if edges:
                            s = s + jnp.concatenate([bias[c]] * min(per_pass, 4), axis=0)
                        score[step + c, at, :] = s
                        one = jnp.maximum(s[:, :2 * HD], s[:, 2 * HD:])
                        most = one if most is None else jnp.maximum(most, one)
                    top[at, :] = most

            def outputs(step, count, first_time=False):
                vv = v2[pl.ds(pl.multiple_of((pair_hi - step - count + 1 - base) * blk, blk), count * blk), :]
                for at in row_groups(per_pass, blk):
                    most = twice(top[at, :])
                    ebs = []
                    for c in reversed(range(count)):
                        eb = jnp.exp(score[step + c, at, :] - most).astype(BF16)
                        probs[kept * pairs + step + c, at, :] = eb
                        ebs.append(eb)
                    out = dot(jnp.concatenate(ebs, axis=1), vv)
                    o_acc[at, :] = out if first_time else o_acc[at, :] + out

            def value_grad(step, count):
                for c in range(count):
                    rows = pl.ds(pl.multiple_of((pair_hi - step - c - base) * blk, blk), blk)
                    acc_v[:, rows] = acc_v[:, rows] + dot(ot[...], probs[kept * pairs + step + c])

            def more_scores(step):
                inside = (pair_hi - step - 1) * blk >= start_hi
                pl.when(inside)(functools.partial(scores, step, 2, edges=False))
                pl.when(jnp.logical_not(inside))(functools.partial(scores, step, 2))

            scores(0, 2, first_time=True)
            in_twos(steps, 1, more_scores, functools.partial(scores, count=1))
            top[...] = jnp.broadcast_to(jnp.max(top[...], axis=1, keepdims=True), top.shape)
            outputs(0, 2, first_time=True)
            in_twos(steps, 1, functools.partial(outputs, count=2), functools.partial(outputs, count=1))
            for a, pair_at in enumerate(pairs_at):
                o2 = q_in[q_rows, lanes_of(h0, a, width)].astype(F32)
                out = []
                scaled = []
                for side, at in enumerate(pair_at):
                    inv = 1.0 / o_acc[at, 2 * HD:]
                    out.append(o_acc[at, 0:2 * HD] * inv)
                    mine = jnp.where(left if side == 0 else jnp.logical_not(left), o2, 0.0) * inv
                    inner[kept, at, :] = jnp.broadcast_to(
                        jnp.sum(mine * out[side], axis=1, keepdims=True), (blk, 2 * HD)
                    )
                    scaled.append(mine)
                    om[kept, at, :] = mine.astype(BF16)
                res[q_rows, lanes_of(h0, a)] = jnp.where(left, out[0], out[1]).astype(BF16)
                o2t = jnp.transpose(scaled[0] + scaled[1]).astype(BF16)
                ot[:, pair_at[0]] = o2t[:HD]
                ot[:, pair_at[1]] = o2t[HD:]

            in_twos(steps, 0, functools.partial(value_grad, count=2), functools.partial(value_grad, count=1))
        return carry

    lax.fori_loop(0, 2, block, 0)
    send_back(acc_v, own_ref, back_refs, rows_all)
    for r in range(PLANE):
        out_refs[r][...] = res[pl.ds(pl.multiple_of((place ^ r) * tok, tok), tok), :]


def backward_kernel(idx_ref, seq_ref, *rest, back, heads, per_pass):
    in_refs = rest[:PLANE]
    kv_refs = rest[PLANE:PLANE + back + 1]
    probs, om, inner, attn_ref = rest[PLANE + back + 1:PLANE + back + 5]
    rest = rest[PLANE + back + 5:]
    out_refs = rest[:PLANE]
    own_ref = rest[PLANE]
    back_refs = rest[PLANE + 1:PLANE + 1 + back]
    q_in, res, k2, v2t, qt, dscore, q_acc, acc_k = rest[PLANE + 1 + back:]
    tok = in_refs[0].shape[0]
    rows_all = PLANE * tok
    blk = rows_all // 2
    passes = heads // per_pass
    pairs = 2 * back + 1
    plane = idx_ref[0] // PLANE
    place = idx_ref[0] % PLANE
    base = (plane - back) * 2

    gather_queries(in_refs, place, q_in)
    lower = lax.broadcasted_iota(jnp.int32, (tok, 2 * HD), 1) < HD
    for at, part in key_blocks(kv_refs, place, tok, back):
        k2[at, :] = jnp.where(lower, part, pltpu.roll(part, HD, 1)).astype(BF16)
        value_t = jnp.transpose(part).astype(BF16)[HD:]
        v2t[:, at] = jnp.concatenate([value_t, value_t], axis=0)
    acc_k[...] = jnp.zeros_like(acc_k)
    left = lax.broadcasted_iota(jnp.int32, (blk, 2 * HD), 1) < HD
    pairs_at = head_pairs(per_pass, blk)

    def block(b, carry):
        pair_hi = plane * 2 + b
        steps = jnp.clip(pair_hi - first_of(pair_hi * blk, seq_ref) // blk + 1, 2, pairs)
        q_rows = pl.ds(pl.multiple_of(b * blk, blk), blk)

        for h0 in range(0, heads, per_pass):
            kept = b * passes + h0 // per_pass
            for a, (even, odd) in enumerate(pairs_at):
                q2t = jnp.transpose(q_in[q_rows, lanes_of(h0, a)].astype(F32)).astype(BF16)
                qt[:, even] = q2t[:HD]
                qt[:, odd] = q2t[HD:]
            def gradients(step, count, first_time=False):
                lowest = pair_hi - step - count + 1 - base
                kk = k2[pl.ds(pl.multiple_of(lowest * blk, blk), count * blk), :]
                rows = [pl.ds(pl.multiple_of((pair_hi - step - c - base) * blk, blk), blk) for c in range(count)]
                v_t = [v2t[:, at] for at in rows]
                for at in row_groups(per_pass, blk):
                    shift = twice(inner[kept, at, :])
                    each = []
                    for c in reversed(range(count)):
                        e = probs[kept * pairs + step + c, at, :].astype(F32)
                        ds = (e * (dot(om[kept, at, :], v_t[c]) - shift)).astype(BF16)
                        dscore[c, at, :] = ds
                        each.append(ds)
                    dq = dot(jnp.concatenate(each, axis=1), kk)
                    q_acc[at, :] = dq if first_time else q_acc[at, :] + dq
                for c in range(count):
                    acc_k[:, rows[c]] = acc_k[:, rows[c]] + dot(qt[...], dscore[c])

            gradients(0, 2, first_time=True)
            in_twos(steps, 1, functools.partial(gradients, count=2), functools.partial(gradients, count=1))
            for a, (even, odd) in enumerate(pairs_at):
                qg = jnp.where(left, q_acc[even, :], q_acc[odd, :]) * SCALE
                res[q_rows, lanes_of(h0, a)] = qg.astype(BF16)
        return carry

    lax.fori_loop(0, 2, block, 0)
    send_back(acc_k, own_ref, back_refs, rows_all)
    for r in range(PLANE):
        mine = res[pl.ds(pl.multiple_of((place ^ r) * tok, tok), tok), :]
        if r == 1:
            mine = jnp.concatenate([attn_ref[...], mine], axis=1)
        out_refs[r][...] = mine


def attention_sizes(q_oc, kvs):
    tok, width2 = q_oc[0].shape
    rows = PLANE * tok
    back = len(kvs) - 1
    heads = width2 // 2 // HD
    blk = rows // 2
    pairs = 2 * back + 1
    per_pass = heads
    while per_pass > 2 and pairs * blk * per_pass * blk * 4 > 12 * 2**20:
        per_pass //= 2
    return tok, width2, rows, back, heads, blk, pairs, per_pass


def kernel_params(name, held, flops):
    return dict(
        name=name,
        compiler_params=pltpu.CompilerParams(vmem_limit_bytes=min(60 * 2**20, held)),
        cost_estimate=pl.CostEstimate(flops=flops, bytes_accessed=2**20, transcendentals=0),
    )


def forward(idx, seq, q_oc, kvs):
    tok, width2, rows, back, heads, blk, pairs, per_pass = attention_sizes(q_oc, kvs)
    cols = per_pass * blk
    keys = rows * (back + 1)
    kept = 2 * heads // per_pass
    held = pairs * blk * cols * 4 + kept * pairs * blk * cols * 2 + 16 * 2**20
    return pl.pallas_call(
        functools.partial(forward_kernel, back=back, heads=heads, per_pass=per_pass),
        out_shape=(
            [jax.ShapeDtypeStruct((tok, width2 // 2), BF16)] * PLANE
            + [jax.ShapeDtypeStruct((HD, rows), F32)]
            + [jax.ShapeDtypeStruct((HD, rows), BF16)] * back
            + [
                jax.ShapeDtypeStruct((kept * pairs, cols, blk), BF16),
                jax.ShapeDtypeStruct((kept, cols, 2 * HD), BF16),
                jax.ShapeDtypeStruct((kept, cols, 2 * HD), F32),
            ]
        ),
        in_specs=[whole(SMEM)] * 2 + [whole(VMEM)] * (PLANE + len(kvs)),
        out_specs=[whole(VMEM)] * (PLANE + 1 + back + 3),
        scratch_shapes=[
            VMEM((rows, width2), BF16),
            VMEM((rows, width2 // 2), BF16),
            VMEM((2 * HD, keys), BF16),
            VMEM((keys, 4 * HD), BF16),
            VMEM((cols, 2 * HD), BF16),
            VMEM((HD, cols), BF16),
            VMEM((blk, 2 * HD), jnp.int32),
            VMEM((2, blk, blk), F32),
            VMEM((pairs, cols, blk), F32),
            VMEM((cols, 4 * HD), F32),
            VMEM((cols, 2 * HD), F32),
            VMEM((HD, keys), F32),
        ],
        **kernel_params("forward", held, 20 * keys * rows * width2 // 2),
    )(idx, seq, *q_oc, *kvs)


def backward(idx, seq, q_oc, kvs, probs, om, inner, attn):
    tok, width2, rows, back, heads, blk, pairs, per_pass = attention_sizes(q_oc, kvs)
    cols = per_pass * blk
    keys = rows * (back + 1)
    held = probs.size * 2 + 16 * 2**20
    return pl.pallas_call(
        functools.partial(backward_kernel, back=back, heads=heads, per_pass=per_pass),
        out_shape=(
            [jax.ShapeDtypeStruct((tok, width2 if r == 1 else width2 // 2), BF16) for r in range(PLANE)]
            + [jax.ShapeDtypeStruct((HD, rows), F32)]
            + [jax.ShapeDtypeStruct((HD, rows), BF16)] * back
        ),
        in_specs=[whole(SMEM)] * 2 + [whole(VMEM)] * (PLANE + len(kvs) + 4),
        out_specs=[whole(VMEM)] * (PLANE + 1 + back),
        scratch_shapes=[
            VMEM((rows, width2), BF16),
            VMEM((rows, width2 // 2), BF16),
            VMEM((keys, 2 * HD), BF16),
            VMEM((2 * HD, keys), BF16),
            VMEM((HD, cols), BF16),
            VMEM((2, cols, blk), BF16),
            VMEM((cols, 2 * HD), F32),
            VMEM((HD, keys), F32),
        ],
        **kernel_params("backward", held, keys * rows),
    )(idx, seq, *q_oc, *kvs, probs, om, inner, attn)


def sum_kernel(idx_ref, own_ref, *rest, back):
    got_refs = rest[:back]
    cot_ref, res_ref = rest[back:back + 2]
    part_refs = rest[back + 2:back + 2 + PLANE]
    total = rest[back + 2 + PLANE]
    tok = part_refs[0].shape[1]
    place = idx_ref[0] % PLANE
    summed = own_ref[...]
    for got in got_refs:
        summed = summed + got[...].astype(F32)
    total[0:HD, :] = summed.astype(BF16)
    total[HD:2 * HD, :] = cot_ref[...]
    for r in range(PLANE):
        part_refs[r][:, 0:tok] = total[:, pl.ds(pl.multiple_of((place ^ r) * tok, tok), tok)]
    part_refs[1][:, tok:] = res_ref[...]


def wv_kernel(idx_ref, own_ref, *refs, back, n_ctx):
    got_refs, hidden_refs = refs[:back], refs[back:back + PLANE]
    cot_ref, wv_ref = refs[back + PLANE:]
    tok, features = hidden_refs[0].shape
    place = idx_ref[0] % PLANE
    summed = own_ref[...]
    for got in got_refs:
        summed = summed + got[...].astype(F32)
    cot_ref[...] = summed.astype(BF16)
    wv = jnp.zeros((HD, features), F32)
    for r in range(0, PLANE, 2):
        cots = [cot_ref[:, pl.ds(pl.multiple_of((place ^ i) * tok, tok), tok)] for i in (r, r + 1)]
        blocks = [hidden_refs[r][...], hidden_refs[r + 1][...]]
        wv = wv + dot(jnp.concatenate(cots, axis=1), jnp.concatenate(blocks, axis=0))
    rows = features // n_ctx
    if wv_ref.shape[2] == 2 * HD:
        wv = jnp.transpose(wv.astype(BF16))
        for d in range(n_ctx):
            one = wv[d * rows:(d + 1) * rows]
            wv_ref[d] = jnp.concatenate([one[:rows // 2], one[rows // 2:]], axis=1)
    else:
        wv = jnp.transpose(wv)
        for d in range(n_ctx):
            wv_ref[d] = wv[d * rows:(d + 1) * rows].astype(BF16)


def results_kernel(idx_ref, part_ref, *refs):
    in_refs, out_refs = refs[:-2], refs[-2:]
    place = idx_ref[0] % PLANE
    lanes = in_refs[0].shape[1]
    tok = part_ref.shape[1] - 2 * lanes
    for i, out_ref in enumerate(out_refs):
        rest = list(in_refs[i * (PLANE - 1):(i + 1) * (PLANE - 1)])
        for r in range(PLANE):
            at = pl.ds(pl.multiple_of((place ^ r) * lanes, lanes), lanes)
            if r == 1:
                out_ref[:, at] = part_ref[:, tok + i * lanes:tok + (i + 1) * lanes]
            else:
                out_ref[:, at] = rest.pop(0)[...]


def finish_kernel(idx_ref, weight_ref, *rest):
    part_refs = rest[:PLANE]
    kg_ref, xg_ref, parts = rest[PLANE:]
    place = idx_ref[0] % PLANE
    for r in range(PLANE):
        tok = part_refs[0].shape[1]
        parts[place ^ r] = jnp.transpose(part_refs[r][:, 0:tok].astype(F32)).astype(BF16)
    kg_ref[...] = jnp.concatenate([parts[g, :, 0:HD] for g in range(PLANE)], axis=1)
    value_cot = jnp.concatenate([parts[g, :, HD:2 * HD] for g in range(PLANE)], axis=1)
    xg_ref[...] = lax.dot_general(
        value_cot, weight_ref[...], (((1,), (1,)), ((), ())), preferred_element_type=F32
    ).astype(BF16)


def wv_sum_kernel(wv_ref, out_ref):
    n_ctx, depth, lanes = wv_ref.shape
    sums = []
    for g in range(PLANE):
        total = wv_ref[g].astype(F32)
        for d in range(g + PLANE, n_ctx, PLANE):
            total = total + wv_ref[d].astype(F32)
        sums.append(total)
    for side in range(lanes // HD):
        out_ref[side * depth:(side + 1) * depth, :] = jnp.concatenate(
            [total[:, side * HD:(side + 1) * HD] for total in sums], axis=1
        )


def shifted(x, by):
    n = lax.axis_size("ctx")
    return lax.ppermute(x, "ctx", [(i, i + by) for i in range(n) if 0 <= i + by < n])


def crossed(x, by):
    n = lax.axis_size("ctx")
    return lax.ppermute(x, "ctx", [(i, i ^ by) for i in range(n)])


def in_plane(x):
    n = lax.axis_size("ctx")
    planes = [list(range(i, i + PLANE)) for i in range(0, n, PLANE)]
    return lax.all_to_all(x, "ctx", 0, 0, axis_index_groups=planes, tiled=True)


def shards(
    queries, keys, hidden, value_weight, out_grad, new_logp, old_logp, rewards, group_ids, seq_lengths
):
    n_ctx = lax.axis_size("ctx")
    tok, width = queries.shape
    kv_width = keys.shape[1]
    features = hidden.shape[1]
    back = n_ctx // 2 // PLANE
    ctx = lax.axis_index("ctx").astype(jnp.int32)
    idx = ctx.reshape(1)
    lanes = width // PLANE
    plane_rows = PLANE * tok

    outs = pl.pallas_call(
        prepare_kernel,
        out_shape=[jax.ShapeDtypeStruct((tok, 2 * HD), BF16)] * PLANE
        + [jax.ShapeDtypeStruct((tok, 2 * lanes), BF16)] * PLANE,
        in_specs=[whole(SMEM)] + [whole(pltpu.HBM)] * 10,
        out_specs=[whole(pltpu.HBM)] * (2 * PLANE),
        scratch_shapes=[
            VMEM((PLANE, tok, 2 * HD), BF16),
            VMEM(hidden.shape, BF16),
            VMEM(value_weight.shape, BF16),
            VMEM(keys.shape, BF16),
            VMEM((PLANE, tok, lanes), BF16),
            VMEM((PLANE, tok, lanes), BF16),
            VMEM((PLANE, tok, 2 * lanes), BF16),
            SMEM(seq_lengths.shape, jnp.int32),
            SMEM(group_ids.shape, jnp.int32),
            SMEM(rewards.shape, F32),
            VMEM((1, tok), F32),
            VMEM((1, tok), F32),
            pltpu.SemaphoreType.DMA((7, PLANE)),
            pltpu.SemaphoreType.DMA((5,)),
        ],
        **small("prepare", mib=60),
    )(
        idx, seq_lengths, group_ids, rewards, new_logp[None, :], old_logp[None, :],
        hidden, value_weight, keys, queries, out_grad,
    )
    kv, q_oc = list(outs[:PLANE]), list(outs[PLANE:])

    q_oc = [q_oc[0]] + [crossed(q_oc[r], r) for r in range(1, PLANE)]
    kv = [kv[0]] + [crossed(kv[r], r) for r in range(1, PLANE)]
    kv = pl.pallas_call(
        join_kernel,
        out_shape=jax.ShapeDtypeStruct((plane_rows, 2 * HD), BF16),
        in_specs=[whole(VMEM)] * PLANE,
        out_specs=whole(VMEM),
        **small("join", 10**10),
    )(*kv)
    kvs = [kv] + [shifted(kv, w * PLANE) for w in range(1, back + 1)]
    late_hidden, q_oc[1] = lax.optimization_barrier((hidden, q_oc[1]))
    hidden_c = crossed(late_hidden, 1)
    late_hidden, q_oc, hidden_c = lax.optimization_barrier((hidden, q_oc, hidden_c))
    hidden_y = crossed(late_hidden, 2)

    outs = list(forward(idx, seq_lengths, q_oc, kvs))
    attn, own_v, backs_v = outs[:PLANE], outs[PLANE], outs[PLANE + 1:PLANE + 1 + back]
    probs, om, inner = outs[PLANE + 1 + back:]
    got_v = [shifted(backs_v[w - 1], -w * PLANE) for w in range(1, back + 1)]
    attn = [attn[0], attn[1]] + [crossed(attn[r], r) for r in range(2, PLANE)]
    outs = list(backward(idx, seq_lengths, q_oc, kvs, probs, om, inner, attn[1]))
    outs, got_v, attn, hidden_y = lax.optimization_barrier((outs, got_v, attn, hidden_y))
    hidden_cy = crossed(hidden_y, 1)
    qg, own_k, backs_k = outs[:PLANE], outs[PLANE], outs[PLANE + 1:]
    got_k = [shifted(backs_k[w - 1], -w * PLANE) for w in range(1, back + 1)]
    rows = features // n_ctx
    packed = (rows // 2) % 16 == 0
    piece = (rows // 2, 2 * HD) if packed else (rows, HD)
    cot, wv = pl.pallas_call(
        functools.partial(wv_kernel, back=back, n_ctx=n_ctx),
        out_shape=[
            jax.ShapeDtypeStruct((HD, plane_rows), BF16),
            jax.ShapeDtypeStruct((n_ctx,) + piece, BF16),
        ],
        in_specs=[whole(SMEM)] + [whole(VMEM)] * (1 + back + PLANE),
        out_specs=[whole(VMEM)] * 2,
        **small("wv"),
    )(idx, own_v, *got_v, hidden, hidden_c, hidden_y, hidden_cy)
    qg = [qg[0], qg[1]] + [crossed(qg[r], r) for r in range(2, PLANE)]
    parts = pl.pallas_call(
        functools.partial(sum_kernel, back=back),
        out_shape=[
            jax.ShapeDtypeStruct((2 * HD, tok + 2 * lanes if r == 1 else tok), BF16) for r in range(PLANE)
        ],
        in_specs=[whole(SMEM)] + [whole(VMEM)] * (3 + back),
        out_specs=[whole(VMEM)] * PLANE,
        scratch_shapes=[VMEM((2 * HD, plane_rows), BF16)],
        **small("sum", 10**10),
    )(idx, own_k, *got_k, cot, qg[1])
    parts, qg[2:] = lax.optimization_barrier((list(parts), qg[2:]))
    parts = [parts[0]] + [crossed(parts[r], r) for r in range(1, PLANE)]
    attn, q_grad = pl.pallas_call(
        results_kernel,
        out_shape=[jax.ShapeDtypeStruct((tok, width), BF16)] * 2,
        in_specs=[whole(SMEM)] + [whole(VMEM)] * (2 * PLANE - 1),
        out_specs=[whole(VMEM)] * 2,
        **small("results", 10**9),
    )(idx, parts[1], attn[0], *attn[2:], qg[0], *qg[2:])
    wv = lax.all_to_all(wv, "ctx", 0, 0, tiled=True)
    k_grad, x_grad = pl.pallas_call(
        finish_kernel,
        out_shape=[
            jax.ShapeDtypeStruct((tok, kv_width), BF16),
            jax.ShapeDtypeStruct((tok, features), BF16),
        ],
        in_specs=[whole(SMEM)] + [whole(VMEM)] * (1 + PLANE),
        out_specs=[whole(VMEM)] * 2,
        scratch_shapes=[VMEM((PLANE, tok, 2 * HD), BF16)],
        **small("finish"),
    )(idx, value_weight, *parts)

    wv_grad = pl.pallas_call(
        wv_sum_kernel,
        out_shape=jax.ShapeDtypeStruct((rows, kv_width), F32),
        in_specs=[whole(VMEM)],
        out_specs=whole(VMEM),
        **small("wv_sum", 10**10),
    )(wv)
    return (attn, q_grad, k_grad, x_grad, wv_grad)


def solution(mesh):
    rows = P(("groups", "ctx"), None)
    flat = P(("groups", "ctx"))
    placed = (rows, rows, rows, P(), rows, flat, flat, P("groups"), P("groups"), P("groups"))
    return jax.shard_map(
        shards, mesh=mesh, in_specs=placed, out_specs=(rows,) * 5, check_vma=False
    )
```
